256 devices in a mesh: tm: 64 (over z, x, core), space: 4 (over y).
Axes of the slice: x: 4, y: 4, z: 8, core: 2. Of those that a mesh axis runs over, the one named last changes fastest.
Arguments:
- forcing: float32 [2, 64, 125, 8, 128], P(None, 'tm', None, 'space'), may hold values from -6 to 6
- init_state: float32 [125, 8, 128], P(None, 'space'), may hold values from -6 to 6
- elem_scale: float32 [8, 128], P('space'), may hold values from 0.5 to 2
- vol_op: float32 [125, 125], replicated, may hold values from -0.5 to 8, as said below
- face_ops: float32 [4, 125, 125], replicated, may hold values from -0.25 to 0.25
Outputs:
- solution: float32 [2, 64, 125, 8, 128], P(None, 'tm', None, 'space')
The draws below stay inside these ranges and needn't reach their ends.
Inputs may be any that keep to these rules, and one draw needn't show every extreme that they name: `vol_op`: its diagonal entries lie between 4 and 8.
All inputs are finite; a program needn't handle non-finite values.
Results may differ from the reference program's by a relative error of at most 0.0003.
Values sent between devices are 32-bit elements; how exact they have to be, the bound alone decides.
No kernel may reach another device: no remote copies, remote signals or barrier semaphores. Data moves between devices by JAX's collectives and lax.ppermute only.
A program may use at most 64 MiB of HBM per device.

```python
import math
import jax
import jax.numpy as jnp
from jax import lax

NB = 125
EX = 128
SWEEPS = 8
SECTIONS = 2
STEPS = 64
EY = 8


def draw_vol_op(key, part):
    key = jax.random.fold_in(key, 11)
    first, second = jax.random.split(key)
    spread = jax.random.normal(first, (NB, NB), jnp.float32) / NB ** 0.5
    spread = jnp.clip(spread, -0.5, 0.5)
    diagonal = jax.random.uniform(second, (NB,), jnp.float32, 4.0, 8.0)
    identity = jnp.eye(NB, dtype=jnp.float32)
    return (spread * (1.0 - identity) + identity * diagonal[None, :]).astype(jnp.float32)


def shard_levels(stream_key, extent, cuts, low, largest):
    loudness = 1.0
    for axis_at, parts in cuts:
        draws = jax.random.uniform(jax.random.fold_in(jax.random.fold_in(stream_key, 6), axis_at), (parts,), jnp.float32, low / len(cuts), largest / len(cuts))
        loudness = loudness * jnp.repeat(jnp.exp(draws), extent[axis_at] // parts).reshape((-1,) + (1,) * (len(extent) - 1 - axis_at))
    return loudness


def bell_draw(stream_key, extent, deviation, reach, shards=(), held_as=jnp.bfloat16):
    loudness = shard_levels(stream_key, extent, shards, -0.22, 0.18) if shards else 1.0
    values = jax.random.normal(stream_key, extent, jnp.float32) * deviation * loudness
    return jnp.minimum(jnp.maximum(values, -reach), reach).astype(held_as)


def setup_inputs(seed: int = 0) -> dict:
    key_of = jax.random.split(jax.random.key(seed), 6)
    forcing = bell_draw(key_of[0], (SECTIONS, STEPS, NB, EY, EX), 1.0, 6.0, ((1, 64), (3, 4)), jnp.float32)
    init_state = bell_draw(key_of[1], (NB, EY, EX), 1.0, 6.0, ((1, 4),), jnp.float32)
    elem_scale = jnp.clip(jnp.exp(math.log(2.0) - 1.3862944 * jax.random.uniform(key_of[2], (EY, EX), jnp.float32) ** shard_levels(key_of[2], (EY, EX), ((0, 4),), -0.2, 0.2)), 0.5, 2.0)
    vol_op = draw_vol_op(jax.random.fold_in(key_of[5], 71), 0)
    face_ops = bell_draw(key_of[4], (4, NB, NB), (4 * NB) ** -0.5, 0.25, (), jnp.float32)
    return {"forcing": forcing, "init_state": init_state, "elem_scale": elem_scale, "vol_op": vol_op, "face_ops": face_ops}


circ_alpha = 0.01
damping = 0.7


def apply_block(matrix, field):
    return jnp.einsum("ij,lcjyx->lciyx", matrix, field, precision=lax.Precision.HIGHEST)


def couple(field, elem_scale, vol_op, face_ops):
    zero_col = jnp.zeros(field.shape[:-1] + (1,), field.dtype)
    west = jnp.concatenate([zero_col, field[..., :-1]], axis=-1)
    east = jnp.concatenate([field[..., 1:], zero_col], axis=-1)
    south = jnp.roll(field, 1, axis=-2)
    north = jnp.roll(field, -1, axis=-2)
    total = elem_scale * apply_block(vol_op, field)
    total = total + apply_block(face_ops[0], west) + apply_block(face_ops[1], east)
    return total + apply_block(face_ops[2], south) + apply_block(face_ops[3], north)


def over_time(table, field):
    return jnp.einsum("kn,nabc->kabc", table, field, precision=lax.Precision.HIGHEST)


def reference(forcing, init_state, elem_scale, vol_op, face_ops):
    steps = forcing.shape[1]
    log_alpha = math.log(circ_alpha)
    place = jnp.arange(steps).astype(jnp.float32)
    grow = jnp.exp(place * (log_alpha / steps))[:, None, None, None]
    shrink = jnp.exp(place * (-log_alpha / steps))[:, None, None, None]
    table_index = (jnp.arange(steps)[:, None] * jnp.arange(steps)[None, :]) % steps
    angle = (2.0 * math.pi / steps) * table_index.astype(jnp.float32)
    cos_table = jnp.cos(angle)
    sin_table = jnp.sin(angle)
    root = math.exp(log_alpha / steps)
    theta = (2.0 * math.pi / steps) * place
    shift_re = (1.0 - root * jnp.cos(theta))[:, None, None, None]
    shift_im = (root * jnp.sin(theta))[:, None, None, None]
    diagonal = elem_scale * jnp.diagonal(vol_op)[:, None, None]
    divisor_re = shift_re + diagonal
    modulus = divisor_re * divisor_re + shift_im * shift_im
    state = init_state
    sections = []
    for section in range(SECTIONS):
        rhs = forcing[section] + 0.5 * state[None]
        rhs = rhs.at[0].add(state)
        scaled = grow * rhs
        spectrum_re = over_time(cos_table, scaled)
        spectrum_im = -over_time(sin_table, scaled)
        iterate_re = jnp.zeros_like(spectrum_re)
        iterate_im = jnp.zeros_like(spectrum_im)
        for sweep in range(SWEEPS):
            coupled = couple(jnp.stack((iterate_re, iterate_im), 1), elem_scale, vol_op, face_ops)
            residual_re = spectrum_re - (shift_re * iterate_re - shift_im * iterate_im + coupled[:, 0])
            residual_im = spectrum_im - (shift_re * iterate_im + shift_im * iterate_re + coupled[:, 1])
            iterate_re, iterate_im = (
                iterate_re + damping * (residual_re * divisor_re + residual_im * shift_im) / modulus,
                iterate_im + damping * (residual_im * divisor_re - residual_re * shift_im) / modulus,
            )
        real = over_time(cos_table, iterate_re) - over_time(sin_table, iterate_im)
        result = real * shrink / steps
        sections.append(result)
        state = result[-1]
    return jnp.stack(sections, 0)
```

```python
import math

import jax
import jax.numpy as jnp
import numpy as np
from jax import lax
from jax.experimental import pallas as pl
from jax.experimental.pallas import tpu as pltpu
from jax.sharding import Mesh
from jax.sharding import PartitionSpec as P

NB = 125
SWEEPS = 8
STEPS = 64
LANES = 128
FREQS = STEPS // 2
CHUNK = 16
WINDOW = 32
HALO = 8
ES_LANE = NB

circ_alpha = 0.01
damping = 0.7

TIME = ("z", "x", "core")
PLANE = ("x", "core", "y")


def tables():
    n = np.arange(STEPS)
    log_alpha = math.log(circ_alpha)
    grow = np.exp(n * (log_alpha / STEPS))
    forward = np.zeros((STEPS, STEPS))
    backward = np.zeros((STEPS, STEPS))
    shifts = np.zeros((FREQS, 4))
    root = math.exp(log_alpha / STEPS)
    forward[0] = 1.0
    forward[1] = (-1.0) ** n
    backward[:, 0] = 1.0
    backward[:, 1] = (-1.0) ** n
    shifts[0] = (1.0 - root, 1.0 + root, 0.0, 0.0)
    for k in range(1, FREQS):
        angle = 2.0 * math.pi * ((k * n) % STEPS) / STEPS
        forward[2 * k] = np.cos(angle)
        forward[2 * k + 1] = -np.sin(angle)
        backward[:, 2 * k] = 2.0 * np.cos(angle)
        backward[:, 2 * k + 1] = -2.0 * np.sin(angle)
        theta = 2.0 * math.pi * k / STEPS
        shifts[k, :3] = (1.0 - root * math.cos(theta), 1.0 - root * math.cos(theta), root * math.sin(theta))
    forward = forward * grow[None, :]
    backward = backward / grow[:, None] / STEPS
    carry = 0.5 * forward.sum(1) + forward[:, 0]
    last = backward[STEPS - 1]
    return tuple(a.astype(np.float32) for a in (forward, backward, shifts, carry, last))


FORWARD, BACKWARD, SHIFTS, CARRY, LAST = tables()
LAST_ROWS = np.repeat(LAST.reshape(FREQS, 2, 1), 4, axis=1).reshape(FREQS, 8, 1)

VMEM = pl.BlockSpec(memory_space=pltpu.VMEM)
SMEM = pl.BlockSpec(memory_space=pltpu.SMEM)
PARAMS = pltpu.CompilerParams(vmem_limit_bytes=32 * 1024 * 1024)


def exact(left, right):
    return jnp.dot(left, right, precision=lax.Precision.HIGHEST, preferred_element_type=jnp.float32)


def pack_kernel(forcing, init, scale, out, rows, flip):
    step = lax.axis_index("z") * 8 + lax.axis_index("x") * 2 + lax.axis_index("core")
    weight = jnp.where(step == 0, 1.5, 0.5).astype(jnp.float32)
    rows[NB:, :] = jnp.zeros((LANES - NB, LANES), jnp.float32)
    for s in range(2):
        for r in range(2):
            value = forcing[s, 0, :, r, :]
            if s == 0:
                value = value + weight * init[:, r, :]
            rows[:NB, :] = value
            rows[ES_LANE : ES_LANE + 1, :] = scale[r : r + 1, :]
            flip[...] = rows[...].T
            for c in range(2):
                out[pl.ds(s * 8 + c * 2 + r, STEPS, stride=16), :] = flip[pl.ds(c, STEPS, stride=2), :]
    blank = jnp.zeros((4, LANES), jnp.float32)
    for m in range(STEPS):
        source = m - 4 if m % 8 < 4 else m + 4
        for s in range(2):
            at = m * 16 + s * 8 + 4
            if 0 <= source < STEPS:
                out[at : at + 4, :] = out[source * 16 + s * 8 : source * 16 + s * 8 + 4, :]
            else:
                out[at : at + 4, :] = blank


def forward_kernel(table, got, out0, out1):
    lane = lax.broadcasted_iota(jnp.int32, (STEPS, LANES), 1)
    for s, out in enumerate((out0, out1)):
        parts = [got[pl.ds(s * 8 + p, STEPS, stride=16), :] for p in range(8)]
        waves = exact(table[...], jnp.concatenate(parts, axis=1))
        for p in range(8):
            wave = waves[:, p * LANES : (p + 1) * LANES]
            wave = jnp.where(lane == ES_LANE, jnp.broadcast_to(parts[p][:1, :], wave.shape), wave)
            out[pl.ds(p, STEPS, stride=8), :] = wave


def operator_kernel(vol, faces, out, diag, square):
    square[...] = jnp.zeros((LANES, LANES), jnp.float32)
    row = lax.broadcasted_iota(jnp.int32, (LANES, LANES), 0)
    col = lax.broadcasted_iota(jnp.int32, (LANES, LANES), 1)
    for op in range(5):
        square[:NB, :NB] = vol[...] if op == 0 else faces[op - 1]
        value = square[...]
        if op == 0:
            on = jnp.where(row == col, value, 0.0)
            diag[...] = jnp.broadcast_to(jnp.sum(on, axis=0, keepdims=True), (8, LANES))
            value = value - on
        value = value.T
        high = value.astype(jnp.bfloat16)
        low = (value - high.astype(jnp.float32)).astype(jnp.bfloat16)
        at = op * LANES
        out[:LANES, at : at + LANES] = high
        out[LANES : 2 * LANES, at : at + LANES] = high
        out[2 * LANES :, at : at + LANES] = low


def solve_kernel(shifts, ops, diag, got, out, iterate, source, inverse):
    kappa = lax.axis_index("x") * 8 + lax.axis_index("core") * 4 + lax.axis_index("y")
    for xc in range(8):
        for yd in range(4):
            for c in range(2):
                for col in range(4):
                    w = HALO + 2 * xc + col
                    if col >= 2:
                        w = (2 * xc if xc < 4 else 16 + 2 * xc) + col - 2
                    at = c * 8 + col * 2
                    iterate[c, w, 2 * yd : 2 * yd + 2, :] = got[xc * 4 + yd, at : at + 2, :]
    shape = (WINDOW, 8, LANES)
    scale = jnp.broadcast_to(iterate[0, :, :, ES_LANE : ES_LANE + 1], shape)
    lane = lax.broadcasted_iota(jnp.int32, shape, 2)
    place = lax.axis_index("z") * CHUNK - HALO + lax.broadcasted_iota(jnp.int32, shape, 0)
    inside = jnp.logical_and(place >= 0, place < 8 * CHUNK)
    scaled = scale * diag[...][None]
    im = shifts[kappa, 2]
    re0 = shifts[kappa, 0] + scaled
    re1 = shifts[kappa, 1] + scaled
    mod0 = jnp.where(inside, damping / (re0 * re0 + im * im), 0.0)
    mod1 = jnp.where(inside, damping / (re1 * re1 + im * im), 0.0)
    inverse[0] = re0 * mod0
    inverse[1] = re1 * mod1
    inverse[2] = im * mod0
    inverse[3] = scale
    g0 = jnp.where(lane < NB, iterate[0], 0.0)
    g1 = jnp.where(lane < NB, iterate[1], 0.0)
    source[0] = inverse[0] * g0 + inverse[2] * g1
    source[1] = inverse[1] * g1 - inverse[2] * g0
    iterate[0] = source[0]
    iterate[1] = source[1]
    for sweep in range(1, SWEEPS):
        lo, hi = sweep, WINDOW - sweep
        wide = hi - lo + 2
        coupled = []
        for c in range(2):
            field = iterate[c, lo - 1 : hi + 1].reshape(wide * 8, LANES)
            high = field.astype(jnp.bfloat16)
            low = (field - high.astype(jnp.float32)).astype(jnp.bfloat16)
            sums = jnp.dot(
                jnp.concatenate((high, low, high), axis=1), ops[...], preferred_element_type=jnp.float32
            )
            part = [sums[:, i * LANES : (i + 1) * LANES].reshape(wide, 8, LANES) for i in range(5)]
            coupled.append(
                inverse[3, lo:hi] * part[0][1:-1]
                + part[1][:-2]
                + part[2][2:]
                + pltpu.roll(part[3][1:-1], 1, 1)
                + pltpu.roll(part[4][1:-1], 7, 1)
            )
        cross = inverse[2, lo:hi]
        new0 = (1.0 - damping) * iterate[0, lo:hi] + source[0, lo:hi] - inverse[0, lo:hi] * coupled[0] - cross * coupled[1]
        new1 = (1.0 - damping) * iterate[1, lo:hi] + source[1, lo:hi] - inverse[1, lo:hi] * coupled[1] + cross * coupled[0]
        iterate[0, lo:hi] = new0
        iterate[1, lo:hi] = new1
    for xc in range(8):
        for yd in range(4):
            for c in range(2):
                for col in range(2):
                    at = c * 4 + col * 2
                    out[xc * 4 + yd, at : at + 2, :] = iterate[c, HALO + 2 * xc + col, 2 * yd : 2 * yd + 2, :]


def state_kernel(last, got, out):
    total = jnp.sum(got[...] * last[...], axis=0)
    out[...] = total + pltpu.roll(total, 4, 0)


def carry_kernel(carry, waves, own, near, out):
    row = lax.broadcasted_iota(jnp.int32, (8, LANES), 0)
    state = jnp.where(row < 4, own[...], near[...])
    for k in range(STEPS):
        out[k * 8 : k * 8 + 8, :] = waves[k * 8 : k * 8 + 8, :] + carry[k] * state


def backward_kernel(table, got0, got1, out):
    for s, got in enumerate((got0, got1)):
        parts = [got[pl.ds(p, STEPS, stride=4), :] for p in range(4)]
        slices = exact(table[...], jnp.concatenate(parts, axis=1))
        for p in range(4):
            out[pl.ds(s * 4 + p, STEPS, stride=8), :] = slices[:, p * LANES : (p + 1) * LANES]


def unpack_kernel(got, out, flip):
    for s in range(2):
        for r in range(2):
            for c in range(2):
                flip[pl.ds(c, STEPS, stride=2), :] = got[pl.ds(s * 4 + c * 2 + r, STEPS, stride=8), :]
            out[s, 0, :, r, :] = flip[...].T[:NB, :]


def call(kernel, outs, ins, scratch=(), specs=None, name=None):
    return pl.pallas_call(
        kernel,
        out_shape=outs,
        in_specs=specs or [VMEM] * len(ins),
        out_specs=jax.tree.map(lambda _: VMEM, outs),
        scratch_shapes=scratch,
        compiler_params=PARAMS,
        name=name,
    )(*ins)


def f32(*shape):
    return jax.ShapeDtypeStruct(shape, jnp.float32)


def exchange(rows, axes, count):
    blocks = rows.reshape(count, -1, LANES)
    return lax.all_to_all(blocks, axes, 0, 0, tiled=True)


def per_device(forcing, init_state, elem_scale, vol_op, face_ops):
    square = pltpu.VMEM((LANES, LANES), jnp.float32)
    ops, diag = call(
        operator_kernel,
        (jax.ShapeDtypeStruct((3 * LANES, 5 * LANES), jnp.bfloat16), f32(8, LANES)),
        (vol_op, face_ops),
        (square,),
        name="operators",
    )
    packed = call(pack_kernel, f32(STEPS * 16, LANES), (forcing, init_state, elem_scale), (square, square), name="pack")
    by_point = exchange(packed, TIME, STEPS).reshape(STEPS * 16, LANES)
    waves0, waves1 = call(
        forward_kernel, (f32(STEPS * 8, LANES), f32(STEPS * 8, LANES)), (FORWARD, by_point), name="forward"
    )

    def solve(waves):
        got = exchange(waves, PLANE, FREQS)
        cube = (WINDOW, 8, LANES)
        done = call(
            solve_kernel,
            f32(FREQS, 8, LANES),
            (SHIFTS, ops, diag, got),
            (
                pltpu.VMEM((2,) + cube, jnp.float32),
                pltpu.VMEM((2,) + cube, jnp.float32),
                pltpu.VMEM((4,) + cube, jnp.float32),
            ),
            [SMEM, VMEM, VMEM, VMEM],
            name="solve",
        )
        return exchange(done, PLANE, FREQS)

    solved0 = solve(waves0)
    own = call(state_kernel, f32(8, LANES), (LAST_ROWS, solved0), name="state")
    moves = []
    for m in range(STEPS):
        target = m + 4 if m % 8 >= 4 else m - 4
        moves.append((m, target % STEPS))
    near = lax.ppermute(own, TIME, moves)
    waves1 = call(
        carry_kernel, f32(STEPS * 8, LANES), (CARRY, waves1, own, near), (), [SMEM, VMEM, VMEM, VMEM], name="carry"
    )
    solved1 = solve(waves1)
    slices = call(
        backward_kernel,
        f32(STEPS * 8, LANES),
        (BACKWARD, solved0.reshape(-1, LANES), solved1.reshape(-1, LANES)),
        name="backward",
    )
    by_column = exchange(slices, TIME, STEPS).reshape(STEPS * 8, LANES)
    return call(unpack_kernel, f32(2, 1, NB, 2, LANES), (by_column,), (square,), name="unpack")


def solution(mesh):
    grid = Mesh(mesh.devices.reshape(8, 4, 2, 4), ("z", "x", "core", "y"))
    return jax.shard_map(
        per_device,
        mesh=grid,
        in_specs=(
            P(None, TIME, None, "y", None),
            P(None, "y", None),
            P("y", None),
            P(),
            P(),
        ),
        out_specs=P(None, TIME, None, "y", None),
        check_vma=False,
    )
```

```python
import math

import jax
import jax.numpy as jnp
import numpy as np
from jax import lax
from jax.experimental import pallas as pl
from jax.experimental.pallas import tpu as pltpu
from jax.sharding import Mesh
from jax.sharding import PartitionSpec as P

NB = 125
SWEEPS = 8
STEPS = 64
LANES = 128
FREQS = STEPS // 2
CHUNK = 16
WINDOW = 32
HALO = 8
ES_LANE = NB

circ_alpha = 0.01
damping = 0.7

TIME = ("z", "x", "core")
PLANE = ("x", "core", "y")


def tables():
    n = np.arange(STEPS)
    log_alpha = math.log(circ_alpha)
    grow = np.exp(n * (log_alpha / STEPS))
    forward = np.zeros((STEPS, STEPS))
    backward = np.zeros((STEPS, STEPS))
    shifts = np.zeros((FREQS, 4))
    root = math.exp(log_alpha / STEPS)
    forward[0] = 1.0
    forward[1] = (-1.0) ** n
    backward[:, 0] = 1.0
    backward[:, 1] = (-1.0) ** n
    shifts[0] = (1.0 - root, 1.0 + root, 0.0, 0.0)
    for k in range(1, FREQS):
        angle = 2.0 * math.pi * ((k * n) % STEPS) / STEPS
        forward[2 * k] = np.cos(angle)
        forward[2 * k + 1] = -np.sin(angle)
        backward[:, 2 * k] = 2.0 * np.cos(angle)
        backward[:, 2 * k + 1] = -2.0 * np.sin(angle)
        theta = 2.0 * math.pi * k / STEPS
        shifts[k, :3] = (1.0 - root * math.cos(theta), 1.0 - root * math.cos(theta), root * math.sin(theta))
    forward = forward * grow[None, :]
    backward = backward / grow[:, None] / STEPS
    carry = 0.5 * forward.sum(1) + forward[:, 0]
    last = backward[STEPS - 1]
    return tuple(a.astype(np.float32) for a in (forward, backward, shifts, carry, last))


FORWARD, BACKWARD, SHIFTS, CARRY, LAST = tables()
BY_PART = np.concatenate((np.arange(0, STEPS, 2), np.arange(1, STEPS, 2)))
FORWARD = FORWARD[BY_PART]
BACKWARD = BACKWARD[:, BY_PART]
SLOTS = np.concatenate((SHIFTS[:, :3], LAST.reshape(FREQS, 2), CARRY.reshape(FREQS, 2), SHIFTS[:, :1]), axis=1)

VMEM = pl.BlockSpec(memory_space=pltpu.VMEM)
SMEM = pl.BlockSpec(memory_space=pltpu.SMEM)
HBM = pl.BlockSpec(memory_space=pltpu.HBM)
PARAMS = pltpu.CompilerParams(vmem_limit_bytes=32 * 1024 * 1024)


def exact(left, right):
    return jnp.dot(left, right, precision=lax.Precision.HIGHEST, preferred_element_type=jnp.float32)


def pack_kernel(forcing, init, scale, out, value, state, elems, rows, flip, sems):
    copies = [
        pltpu.make_async_copy(ref, into, sems.at[i])
        for i, (ref, into) in enumerate(((forcing, value), (init, state), (scale, elems)))
    ]
    for copy in copies:
        copy.start()
    step = lax.axis_index("z") * 8 + lax.axis_index("x") * 2 + lax.axis_index("core")
    weight = jnp.where(step == 0, 1.5, 0.5).astype(jnp.float32)
    rows[NB:, :] = jnp.zeros((LANES - NB, LANES), jnp.float32)
    for copy in copies:
        copy.wait()
    for s in (1, 0):
        for r in range(2):
            if s == 0:
                rows[:NB, :] = value[s, 0, :, r, :] + weight * state[:, r, :]
                rows[ES_LANE : ES_LANE + 1, :] = elems[r : r + 1, :]
            else:
                rows[:NB, :] = value[s, 0, :, r, :]
            flip[...] = rows[...].T
            for c in range(2):
                out[pl.ds(s * 8 + c * 2 + r, STEPS, stride=12), :] = flip[pl.ds(c, STEPS, stride=2), :]
    blank = jnp.zeros((4, LANES), jnp.float32)
    for m in range(STEPS):
        source = m - 4 if m % 8 < 4 else m + 4
        at = m * 12 + 4
        if 0 <= source < STEPS:
            out[at : at + 4, :] = out[source * 12 : source * 12 + 4, :]
        else:
            out[at : at + 4, :] = blank


def forward_kernel(table, got, out):
    lane = lax.broadcasted_iota(jnp.int32, (STEPS, LANES), 1)
    parts = [got[pl.ds(p, STEPS, stride=12), :] for p in range(12)]
    waves = exact(table[...], jnp.concatenate(parts, axis=1))
    for p in range(12):
        wave = waves[:, p * LANES : (p + 1) * LANES]
        if p < 8:
            wave = jnp.where(lane == ES_LANE, jnp.broadcast_to(parts[p][:1, :], wave.shape), wave)
        for c in range(2):
            at = c * 8 + p if p < 8 else 16 + c * 4 + p - 8
            out[pl.ds(at, FREQS, stride=24), :] = wave[c * FREQS : (c + 1) * FREQS]


def operator_kernel(vol, faces, out, diag, square):
    square[...] = jnp.zeros((LANES, LANES), jnp.float32)
    row = lax.broadcasted_iota(jnp.int32, (LANES, LANES), 0)
    col = lax.broadcasted_iota(jnp.int32, (LANES, LANES), 1)
    for op in range(5):
        square[:NB, :NB] = vol[...] if op == 0 else faces[op - 1]
        value = square[...]
        if op == 0:
            on = jnp.where(row == col, value, 0.0)
            diag[...] = jnp.broadcast_to(jnp.sum(on, axis=0, keepdims=True), (8, LANES))
            value = value - on
        value = value.T
        high = value.astype(jnp.bfloat16)
        low = (value - high.astype(jnp.float32)).astype(jnp.bfloat16)
        at = op * LANES
        out[:LANES, at : at + LANES] = high
        out[LANES : 2 * LANES, at : at + LANES] = high
        out[2 * LANES :, at : at + LANES] = low


def slot():
    return lax.axis_index("x") * 8 + lax.axis_index("core") * 4 + lax.axis_index("y")


def relax(slots, ops, diag, scale, iterate, source, inverse):
    kappa = slot()
    shape = (WINDOW, 8, LANES)
    lane = lax.broadcasted_iota(jnp.int32, shape, 2)
    place = lax.axis_index("z") * CHUNK - HALO + lax.broadcasted_iota(jnp.int32, shape, 0)
    inside = jnp.logical_and(place >= 0, place < 8 * CHUNK)
    scaled = scale[...] * diag[...][None]
    im = slots[kappa, 2]
    re0 = slots[kappa, 0] + scaled
    re1 = slots[kappa, 1] + scaled
    mod0 = jnp.where(inside, damping / (re0 * re0 + im * im), 0.0)
    mod1 = jnp.where(inside, damping / (re1 * re1 + im * im), 0.0)
    inverse[0] = re0 * mod0
    inverse[1] = re1 * mod1
    inverse[2] = im * mod0
    g0 = jnp.where(lane < NB, iterate[0], 0.0)
    g1 = jnp.where(lane < NB, iterate[1], 0.0)
    source[0] = inverse[0] * g0 + inverse[2] * g1
    source[1] = inverse[1] * g1 - inverse[2] * g0
    iterate[0] = source[0]
    iterate[1] = source[1]
    for sweep in range(1, SWEEPS):
        lo, hi = sweep, WINDOW - sweep
        wide = hi - lo + 2
        coupled = []
        for c in range(2):
            field = iterate[c, lo - 1 : hi + 1].reshape(wide * 8, LANES)
            high = field.astype(jnp.bfloat16)
            low = (field - high.astype(jnp.float32)).astype(jnp.bfloat16)
            sums = jnp.dot(
                jnp.concatenate((high, low, high), axis=1), ops[...], preferred_element_type=jnp.float32
            )
            part = [sums[:, i * LANES : (i + 1) * LANES].reshape(wide, 8, LANES) for i in range(5)]
            coupled.append(
                scale[lo:hi] * part[0][1:-1]
                + part[1][:-2]
                + part[2][2:]
                + pltpu.roll(part[3][1:-1], 1, 1)
                + pltpu.roll(part[4][1:-1], 7, 1)
            )
        cross = inverse[2, lo:hi]
        new0 = (1.0 - damping) * iterate[0, lo:hi] + source[0, lo:hi] - inverse[0, lo:hi] * coupled[0] - cross * coupled[1]
        new1 = (1.0 - damping) * iterate[1, lo:hi] + source[1, lo:hi] - inverse[1, lo:hi] * coupled[1] + cross * coupled[0]
        iterate[0, lo:hi] = new0
        iterate[1, lo:hi] = new1


def hand_out(iterate, out, first):
    for xc in range(8):
        for yd in range(4):
            for c in range(2):
                for col in range(2):
                    at = first + c * 4 + col * 2
                    out[xc * 4 + yd, at : at + 2, :] = iterate[c, HALO + 2 * xc + col, 2 * yd : 2 * yd + 2, :]


def first_kernel(slots, ops, diag, got, out, state, scale, iterate, source, inverse):
    for xc in range(8):
        for yd in range(4):
            for c in range(2):
                for col in range(4):
                    w = HALO + 2 * xc + col
                    if col >= 2:
                        w = (2 * xc if xc < 4 else 16 + 2 * xc) + col - 2
                    at = c * 8 + col * 2
                    iterate[c, w, 2 * yd : 2 * yd + 2, :] = got[xc * 4 + yd, at : at + 2, :]
    scale[...] = jnp.broadcast_to(iterate[0, :, :, ES_LANE : ES_LANE + 1], scale.shape)
    relax(slots, ops, diag, scale, iterate, source, inverse)
    kappa = slot()
    middle = slice(HALO, HALO + CHUNK)
    state[...] = slots[kappa, 3] * iterate[0, middle] + slots[kappa, 4] * iterate[1, middle]
    hand_out(iterate, out, 0)


def carry_kernel(slots, got, state0, state1, state2, state3, left, right):
    state = (state0[...] + state1[...]) + (state2[...] + state3[...])
    kappa = slot()
    for c in range(2):
        part = slots[kappa, 5 + c] * state
        left[c] = part[: CHUNK // 2]
        right[c] = part[CHUNK // 2 :]
        for xc in range(8):
            side = left if xc < 4 else right
            for yd in range(4):
                for col in range(2):
                    at = 16 + c * 4 + col * 2
                    here = (c, 2 * (xc % 4) + col, slice(2 * yd, 2 * yd + 2))
                    side[here] = side[here] + got[xc * 4 + yd, at : at + 2, :]


def second_kernel(slots, ops, diag, scale, west, left, right, east, before, out, iterate, source, inverse):
    for i, part in enumerate((west, left, right, east)):
        iterate[:, i * HALO : (i + 1) * HALO] = part[...]
    out[:, :8, :] = before[...]
    relax(slots, ops, diag, scale, iterate, source, inverse)
    hand_out(iterate, out, 8)


def backward_kernel(table, got, out):
    parts = []
    for p in range(8):
        at = (p // 4) * 8 + p % 4
        halves = [got[pl.ds(at + 4 * c, FREQS, stride=16), :] for c in range(2)]
        parts.append(jnp.concatenate(halves, axis=0))
    slices = exact(table[...], jnp.concatenate(parts, axis=1))
    for p in range(8):
        out[pl.ds(p, STEPS, stride=8), :] = slices[:, p * LANES : (p + 1) * LANES]


def unpack_kernel(got, out, flip):
    for s in range(2):
        for r in range(2):
            for c in range(2):
                flip[pl.ds(c, STEPS, stride=2), :] = got[pl.ds(s * 4 + c * 2 + r, STEPS, stride=8), :]
            out[s, 0, :, r, :] = flip[...].T[:NB, :]


def call(kernel, outs, ins, scratch=(), specs=None, name=None, params=PARAMS):
    return pl.pallas_call(
        kernel,
        out_shape=outs,
        in_specs=specs or [VMEM] * len(ins),
        out_specs=jax.tree.map(lambda _: VMEM, outs),
        scratch_shapes=scratch,
        compiler_params=params,
        name=name,
    )(*ins)


def f32(*shape):
    return jax.ShapeDtypeStruct(shape, jnp.float32)


def exchange(blocks, axes):
    return lax.all_to_all(blocks, axes, 0, 0, tiled=True)


def moved(block, axis, by):
    count = lax.axis_size(axis)
    return lax.ppermute(block, axis, [(i, (i + by) % count) for i in range(count)])


def per_device(forcing, init_state, elem_scale, vol_op, face_ops):
    square = pltpu.VMEM((LANES, LANES), jnp.float32)
    window = (WINDOW, 8, LANES)
    work = [pltpu.VMEM((count,) + window, jnp.float32) for count in (2, 2, 3)]
    ops, diag = call(
        operator_kernel,
        (jax.ShapeDtypeStruct((3 * LANES, 5 * LANES), jnp.bfloat16), f32(8, LANES)),
        (vol_op, face_ops),
        (square,),
        name="operators",
    )
    packed = call(
        pack_kernel,
        f32(STEPS * 12, LANES),
        (forcing, init_state, elem_scale),
        (
            pltpu.VMEM(forcing.shape, jnp.float32),
            pltpu.VMEM(init_state.shape, jnp.float32),
            pltpu.VMEM(elem_scale.shape, jnp.float32),
            square,
            square,
            pltpu.SemaphoreType.DMA((3,)),
        ),
        [HBM] * 3,
        name="pack",
        params=pltpu.CompilerParams(vmem_limit_bytes=60 * 1024 * 1024),
    )
    by_point = exchange(packed.reshape(STEPS, 3, 4, LANES), TIME).reshape(STEPS * 12, LANES)
    waves = call(forward_kernel, f32(FREQS * 24, LANES), (FORWARD, by_point), name="forward")
    got = exchange(waves.reshape(FREQS, 24, LANES), PLANE)
    done, state, scale = call(
        first_kernel,
        (f32(FREQS, 8, LANES), f32(CHUNK, 8, LANES), f32(*window)),
        (SLOTS, ops, diag, got),
        work,
        [SMEM, VMEM, VMEM, VMEM],
        name="first",
    )
    state = state + moved(state, "core", 1)
    state = state + moved(state, "y", 1) + moved(state, "y", 2) + moved(state, "y", 3)
    states = [state] + [moved(state, "x", by) for by in (1, 2, 3)]
    half = f32(2, CHUNK // 2, 8, LANES)
    left, right = call(carry_kernel, (half, half), (SLOTS, got, *states), (), [SMEM] + [VMEM] * 5, name="carry")
    west = moved(right, "z", 1)
    east = moved(left, "z", -1)
    done = call(
        second_kernel,
        f32(FREQS, 16, LANES),
        (SLOTS, ops, diag, scale, west, left, right, east, done),
        work,
        [SMEM] + [VMEM] * 8,
        name="second",
    )
    got = exchange(done, PLANE).reshape(FREQS * 16, LANES)
    slices = call(backward_kernel, f32(STEPS * 8, LANES), (BACKWARD, got), name="backward")
    by_column = exchange(slices.reshape(STEPS, 8, LANES), TIME).reshape(STEPS * 8, LANES)
    return call(unpack_kernel, f32(2, 1, NB, 2, LANES), (by_column,), (square,), name="unpack")


def solution(mesh):
    grid = Mesh(mesh.devices.reshape(8, 4, 2, 4), ("z", "x", "core", "y"))
    return jax.shard_map(
        per_device,
        mesh=grid,
        in_specs=(
            P(None, TIME, None, "y", None),
            P(None, "y", None),
            P("y", None),
            P(),
            P(),
        ),
        out_specs=P(None, TIME, None, "y", None),
        check_vma=False,
    )
```

```python
import math

import jax
import jax.numpy as jnp
import numpy as np
from jax import lax
from jax.experimental import pallas as pl
from jax.experimental.pallas import tpu as pltpu
from jax.sharding import Mesh
from jax.sharding import PartitionSpec as P

NB = 125
SWEEPS = 8
STEPS = 64
LANES = 128
FREQS = STEPS // 2
CHUNK = 16
WINDOW = 32
HALO = 8
ES_LANE = NB

circ_alpha = 0.01
damping = 0.7

TIME = ("z", "x", "core")
PLANE = ("x", "core", "y")


def tables():
    n = np.arange(STEPS)
    log_alpha = math.log(circ_alpha)
    grow = np.exp(n * (log_alpha / STEPS))
    forward = np.zeros((STEPS, STEPS))
    backward = np.zeros((STEPS, STEPS))
    shifts = np.zeros((FREQS, 4))
    root = math.exp(log_alpha / STEPS)
    forward[0] = 1.0
    forward[1] = (-1.0) ** n
    backward[:, 0] = 1.0
    backward[:, 1] = (-1.0) ** n
    shifts[0] = (1.0 - root, 1.0 + root, 0.0, 0.0)
    for k in range(1, FREQS):
        angle = 2.0 * math.pi * ((k * n) % STEPS) / STEPS
        forward[2 * k] = np.cos(angle)
        forward[2 * k + 1] = -np.sin(angle)
        backward[:, 2 * k] = 2.0 * np.cos(angle)
        backward[:, 2 * k + 1] = -2.0 * np.sin(angle)
        theta = 2.0 * math.pi * k / STEPS
        shifts[k, :3] = (1.0 - root * math.cos(theta), 1.0 - root * math.cos(theta), root * math.sin(theta))
    forward = forward * grow[None, :]
    backward = backward / grow[:, None] / STEPS
    carry = 0.5 * forward.sum(1) + forward[:, 0]
    last = backward[STEPS - 1]
    return tuple(a.astype(np.float32) for a in (forward, backward, shifts, carry, last))


FORWARD, BACKWARD, SHIFTS, CARRY, LAST = tables()
BY_PART = np.concatenate((np.arange(0, STEPS, 2), np.arange(1, STEPS, 2)))
FORWARD = FORWARD[BY_PART]
BACKWARD = BACKWARD[:, BY_PART]
SLOTS = np.concatenate((SHIFTS[:, :3], LAST.reshape(FREQS, 2), CARRY.reshape(FREQS, 2), SHIFTS[:, :1]), axis=1)
SLOTS = np.repeat(SLOTS[:, :, None], LANES, axis=2)

VMEM = pl.BlockSpec(memory_space=pltpu.VMEM)
HBM = pl.BlockSpec(memory_space=pltpu.HBM)
ANY = pl.BlockSpec(memory_space=pl.ANY)
PARAMS = pltpu.CompilerParams(vmem_limit_bytes=32 * 1024 * 1024)


def exact(left, right):
    return jnp.dot(left, right, precision=lax.Precision.HIGHEST, preferred_element_type=jnp.float32)


def pack_kernel(
    forcing, init, scale, vol, faces, out, ops, diag, value, state, elems, volume, sides, rows, flip, sems
):
    copies = [
        pltpu.make_async_copy(ref, into, sems.at[i])
        for i, (ref, into) in enumerate(
            ((vol, volume), (faces, sides), (forcing, value), (init, state), (scale, elems))
        )
    ]
    for copy in copies:
        copy.start()
    step = lax.axis_index("z") * 8 + lax.axis_index("x") * 2 + lax.axis_index("core")
    weight = jnp.where(step == 0, 1.5, 0.5).astype(jnp.float32)
    flip[...] = jnp.zeros((LANES, LANES), jnp.float32)
    rows[NB:, :] = jnp.zeros((LANES - NB, LANES), jnp.float32)
    for copy in copies[:2]:
        copy.wait()
    row = lax.broadcasted_iota(jnp.int32, (LANES, LANES), 0)
    col = lax.broadcasted_iota(jnp.int32, (LANES, LANES), 1)
    for op in range(5):
        flip[:NB, :NB] = volume[...] if op == 0 else sides[:, op - 1, :]
        square = flip[...]
        if op == 0:
            on = jnp.where(row == col, square, 0.0)
            diag[...] = jnp.broadcast_to(jnp.sum(on, axis=0, keepdims=True), (8, LANES))
            square = square - on
        square = square.T
        high = square.astype(jnp.bfloat16)
        low = (square - high.astype(jnp.float32)).astype(jnp.bfloat16)
        at = op * LANES
        ops[:LANES, at : at + LANES] = high
        ops[LANES : 2 * LANES, at : at + LANES] = high
        ops[2 * LANES :, at : at + LANES] = low
    for copy in copies[2:]:
        copy.wait()
    for s in (1, 0):
        for r in range(2):
            if s == 0:
                rows[:NB, :] = value[s, 0, :, r, :] + weight * state[:, r, :]
                rows[ES_LANE : ES_LANE + 1, :] = elems[r : r + 1, :]
            else:
                rows[:NB, :] = value[s, 0, :, r, :]
            flip[...] = rows[...].T
            for c in range(2):
                out[pl.ds(s * 8 + c * 2 + r, STEPS, stride=12), :] = flip[pl.ds(c, STEPS, stride=2), :]
    blank = jnp.zeros((4, LANES), jnp.float32)
    for m in range(STEPS):
        source = m - 4 if m % 8 < 4 else m + 4
        at = m * 12 + 4
        if 0 <= source < STEPS:
            out[at : at + 4, :] = out[source * 12 : source * 12 + 4, :]
        else:
            out[at : at + 4, :] = blank


def forward_kernel(table, got, out):
    lane = lax.broadcasted_iota(jnp.int32, (STEPS, LANES), 1)
    parts = [got[pl.ds(p, STEPS, stride=12), :] for p in range(12)]
    waves = exact(table[...], jnp.concatenate(parts, axis=1))
    for p in range(12):
        wave = waves[:, p * LANES : (p + 1) * LANES]
        if p < 8:
            wave = jnp.where(lane == ES_LANE, jnp.broadcast_to(parts[p][:1, :], wave.shape), wave)
        for c in range(2):
            at = c * 8 + p if p < 8 else 16 + c * 4 + p - 8
            out[pl.ds(at, FREQS, stride=24), :] = wave[c * FREQS : (c + 1) * FREQS]


def slot():
    return lax.axis_index("x") * 8 + lax.axis_index("core") * 4 + lax.axis_index("y")


def invert(slots, diag, scale, inverse):
    mine = slots[slot()]
    shape = (WINDOW, 8, LANES)
    place = lax.axis_index("z") * CHUNK - HALO + lax.broadcasted_iota(jnp.int32, shape, 0)
    inside = jnp.logical_and(place >= 0, place < 8 * CHUNK)
    scaled = scale[...] * diag[...][None]
    im = mine[2:3][None]
    re0 = mine[0:1][None] + scaled
    re1 = mine[1:2][None] + scaled
    mod0 = jnp.where(inside, damping / (re0 * re0 + im * im), 0.0)
    mod1 = jnp.where(inside, damping / (re1 * re1 + im * im), 0.0)
    inverse[0] = re0 * mod0
    inverse[1] = re1 * mod1
    inverse[2] = im * mod0


def relax(ops, scale, inverse, iterate, source):
    lane = lax.broadcasted_iota(jnp.int32, (WINDOW, 8, LANES), 2)
    g0 = jnp.where(lane < NB, iterate[0], 0.0)
    g1 = jnp.where(lane < NB, iterate[1], 0.0)
    source[0] = inverse[0] * g0 + inverse[2] * g1
    source[1] = inverse[1] * g1 - inverse[2] * g0
    iterate[0] = source[0]
    iterate[1] = source[1]
    for sweep in range(1, SWEEPS):
        lo, hi = sweep + 1, WINDOW - sweep - 1
        wide = hi - lo + 2
        coupled = []
        for c in range(2):
            field = iterate[c, lo - 1 : hi + 1].reshape(wide * 8, LANES)
            high = field.astype(jnp.bfloat16)
            low = (field - high.astype(jnp.float32)).astype(jnp.bfloat16)
            sums = jnp.dot(
                jnp.concatenate((high, low, high), axis=1), ops[...], preferred_element_type=jnp.float32
            )
            part = [sums[:, i * LANES : (i + 1) * LANES].reshape(wide, 8, LANES) for i in range(5)]
            coupled.append(
                scale[lo:hi] * part[0][1:-1]
                + part[1][:-2]
                + part[2][2:]
                + pltpu.roll(part[3][1:-1], 1, 1)
                + pltpu.roll(part[4][1:-1], 7, 1)
            )
        cross = inverse[2, lo:hi]
        new0 = (1.0 - damping) * iterate[0, lo:hi] + source[0, lo:hi] - inverse[0, lo:hi] * coupled[0] - cross * coupled[1]
        new1 = (1.0 - damping) * iterate[1, lo:hi] + source[1, lo:hi] - inverse[1, lo:hi] * coupled[1] + cross * coupled[0]
        iterate[0, lo:hi] = new0
        iterate[1, lo:hi] = new1


def first_kernel(slots, ops, diag, got, solved, state, scale, inverse, iterate, source):
    for xc in range(8):
        for yd in range(4):
            for c in range(2):
                for col in range(4):
                    w = HALO + 2 * xc + col
                    if col >= 2:
                        w = (2 * xc if xc < 4 else 16 + 2 * xc) + col - 2
                    at = c * 8 + col * 2
                    iterate[c, w, 2 * yd : 2 * yd + 2, :] = got[xc * 4 + yd, at : at + 2, :]
    scale[...] = jnp.broadcast_to(iterate[0, :, :, ES_LANE : ES_LANE + 1], scale.shape)
    invert(slots, diag, scale, inverse)
    relax(ops, scale, inverse, iterate, source)
    mine = slots[slot()]
    middle = iterate[:, HALO : HALO + CHUNK]
    solved[...] = middle
    state[...] = mine[3:4][None] * middle[0] + mine[4:5][None] * middle[1]


def between_kernel(got, solved, after, done, left, right):
    del after
    for c in range(2):
        for xc in range(8):
            side = left if xc < 4 else right
            for yd in range(4):
                for col in range(2):
                    rows = slice(2 * yd, 2 * yd + 2)
                    at = c * 4 + col * 2
                    done[xc * 4 + yd, at : at + 2, :] = solved[c, 2 * xc + col, rows, :]
                    side[c, 2 * (xc % 4) + col, rows, :] = got[xc * 4 + yd, 16 + at : 18 + at, :]


def carry_kernel(slots, left, right, state0, state1, state2, state3, out_left, out_right):
    state = (state0[...] + state1[...]) + (state2[...] + state3[...])
    mine = slots[slot()]
    for c in range(2):
        part = mine[5 + c : 6 + c][None] * state
        out_left[c] = left[c] + part[: CHUNK // 2]
        out_right[c] = right[c] + part[CHUNK // 2 :]


def second_kernel(ops, scale, inverse, west, left, right, east, before, out, iterate, source):
    for i, part in enumerate((west, left, right, east)):
        iterate[:, i * HALO : (i + 1) * HALO] = part[...]
    out[:, :8, :] = before[...]
    relax(ops, scale, inverse, iterate, source)
    for xc in range(8):
        for yd in range(4):
            for c in range(2):
                for col in range(2):
                    at = 8 + c * 4 + col * 2
                    out[xc * 4 + yd, at : at + 2, :] = iterate[c, HALO + 2 * xc + col, 2 * yd : 2 * yd + 2, :]


def backward_kernel(table, got, out):
    parts = []
    for p in range(8):
        at = (p // 4) * 8 + p % 4
        halves = [got[pl.ds(at + 4 * c, FREQS, stride=16), :] for c in range(2)]
        parts.append(jnp.concatenate(halves, axis=0))
    slices = exact(table[...], jnp.concatenate(parts, axis=1))
    for p in range(8):
        out[pl.ds(p, STEPS, stride=8), :] = slices[:, p * LANES : (p + 1) * LANES]


def unpack_kernel(got, out, flip):
    for s in range(2):
        for r in range(2):
            for c in range(2):
                flip[pl.ds(c, STEPS, stride=2), :] = got[pl.ds(s * 4 + c * 2 + r, STEPS, stride=8), :]
            out[s, 0, :, r, :] = flip[...].T[:NB, :]


def call(kernel, outs, ins, scratch=(), specs=None, name=None, params=PARAMS):
    return pl.pallas_call(
        kernel,
        out_shape=outs,
        in_specs=specs or [VMEM] * len(ins),
        out_specs=jax.tree.map(lambda _: VMEM, outs),
        scratch_shapes=scratch,
        compiler_params=params,
        name=name,
    )(*ins)


def f32(*shape):
    return jax.ShapeDtypeStruct(shape, jnp.float32)


def exchange(blocks, axes):
    return lax.all_to_all(blocks, axes, 0, 0, tiled=True)


def moved(block, axis, by):
    count = lax.axis_size(axis)
    return lax.ppermute(block, axis, [(i, (i + by) % count) for i in range(count)])


def per_device(forcing, init_state, elem_scale, vol_op, face_ops):
    square = pltpu.VMEM((LANES, LANES), jnp.float32)
    window = (WINDOW, 8, LANES)
    inputs = (forcing, init_state, elem_scale, vol_op, jnp.transpose(face_ops, (1, 0, 2)))
    packed, ops, diag = call(
        pack_kernel,
        (f32(STEPS * 12, LANES), jax.ShapeDtypeStruct((3 * LANES, 5 * LANES), jnp.bfloat16), f32(8, LANES)),
        inputs,
        [pltpu.VMEM(value.shape, jnp.float32) for value in inputs]
        + [square, square, pltpu.SemaphoreType.DMA((len(inputs),))],
        [HBM] * len(inputs),
        name="pack",
        params=pltpu.CompilerParams(vmem_limit_bytes=60 * 1024 * 1024),
    )
    by_point = exchange(packed.reshape(STEPS, 3, 4, LANES), TIME).reshape(STEPS * 12, LANES)
    waves = call(forward_kernel, f32(FREQS * 24, LANES), (FORWARD, by_point), name="forward")
    got = exchange(waves.reshape(FREQS, 24, LANES), PLANE)
    both = pltpu.VMEM((2,) + window, jnp.float32)
    solved, state, scale, inverse = call(
        first_kernel,
        (f32(2, CHUNK, 8, LANES), f32(CHUNK, 8, LANES), f32(*window), f32(3, *window)),
        (SLOTS, ops, diag, got),
        (both, both),
        name="first",
    )
    half = f32(2, CHUNK // 2, 8, LANES)
    state = state + moved(state, "core", 1)
    done, left, right = call(
        between_kernel, (f32(FREQS, 8, LANES), half, half), (got, solved, state), (), [VMEM, VMEM, ANY], name="between"
    )
    state = state + moved(state, "y", 1) + moved(state, "y", 2) + moved(state, "y", 3)
    states = [state] + [moved(state, "x", by) for by in (1, 2, 3)]
    left, right = call(carry_kernel, (half, half), (SLOTS, left, right, *states), name="carry")
    west = moved(right, "z", 1)
    east = moved(left, "z", -1)
    done = call(
        second_kernel,
        f32(FREQS, 16, LANES),
        (ops, scale, inverse, west, left, right, east, done),
        (both, both),
        name="second",
    )
    got = exchange(done, PLANE).reshape(FREQS * 16, LANES)
    slices = call(backward_kernel, f32(STEPS * 8, LANES), (BACKWARD, got), name="backward")
    by_column = exchange(slices.reshape(STEPS, 8, LANES), TIME).reshape(STEPS * 8, LANES)
    return call(unpack_kernel, f32(2, 1, NB, 2, LANES), (by_column,), (square,), name="unpack")


def solution(mesh):
    grid = Mesh(mesh.devices.reshape(8, 4, 2, 4), ("z", "x", "core", "y"))
    return jax.shard_map(
        per_device,
        mesh=grid,
        in_specs=(
            P(None, TIME, None, "y", None),
            P(None, "y", None),
            P("y", None),
            P(),
            P(),
        ),
        out_specs=P(None, TIME, None, "y", None),
        check_vma=False,
    )
```

```python
import math

import jax
import jax.numpy as jnp
import ml_dtypes
import numpy as np
from jax import lax
from jax.experimental import pallas as pl
from jax.experimental.pallas import tpu as pltpu
from jax.sharding import Mesh
from jax.sharding import PartitionSpec as P

NB = 125
SWEEPS = 8
STEPS = 64
LANES = 128
FREQS = STEPS // 2
CHUNK = 16
WINDOW = 32
HALO = 8
ES_LANE = NB

circ_alpha = 0.01
damping = 0.7

TIME = ("z", "x", "core")
PLANE = ("x", "core", "y")


def tables():
    n = np.arange(STEPS)
    log_alpha = math.log(circ_alpha)
    grow = np.exp(n * (log_alpha / STEPS))
    forward = np.zeros((STEPS, STEPS))
    backward = np.zeros((STEPS, STEPS))
    shifts = np.zeros((FREQS, 4))
    root = math.exp(log_alpha / STEPS)
    forward[0] = 1.0
    forward[1] = (-1.0) ** n
    backward[:, 0] = 1.0
    backward[:, 1] = (-1.0) ** n
    shifts[0] = (1.0 - root, 1.0 + root, 0.0, 0.0)
    for k in range(1, FREQS):
        angle = 2.0 * math.pi * ((k * n) % STEPS) / STEPS
        forward[2 * k] = np.cos(angle)
        forward[2 * k + 1] = -np.sin(angle)
        backward[:, 2 * k] = 2.0 * np.cos(angle)
        backward[:, 2 * k + 1] = -2.0 * np.sin(angle)
        theta = 2.0 * math.pi * k / STEPS
        shifts[k, :3] = (1.0 - root * math.cos(theta), 1.0 - root * math.cos(theta), root * math.sin(theta))
    forward = forward * grow[None, :]
    backward = backward / grow[:, None] / STEPS
    carry = 0.5 * forward.sum(1) + forward[:, 0]
    last = backward[STEPS - 1]
    return tuple(a.astype(np.float32) for a in (forward, backward, shifts, carry, last))


def in_parts(table):
    high = table.astype(ml_dtypes.bfloat16)
    low = (table - high.astype(np.float32)).astype(ml_dtypes.bfloat16)
    return np.concatenate((high, high, low), axis=1)


FORWARD, BACKWARD, SHIFTS, CARRY, LAST = tables()
BY_PART = np.concatenate((np.arange(0, STEPS, 2), np.arange(1, STEPS, 2)))
FORWARD = in_parts(FORWARD[BY_PART])
BACKWARD = in_parts(BACKWARD[:, BY_PART])
SLOTS = np.concatenate((SHIFTS[:, :3], LAST.reshape(FREQS, 2), CARRY.reshape(FREQS, 2), SHIFTS[:, :1]), axis=1)
SLOTS = np.repeat(SLOTS[:, :, None], LANES, axis=2)

VMEM = pl.BlockSpec(memory_space=pltpu.VMEM)
HBM = pl.BlockSpec(memory_space=pltpu.HBM)
ANY = pl.BlockSpec(memory_space=pl.ANY)
PARAMS = pltpu.CompilerParams(vmem_limit_bytes=32 * 1024 * 1024)


def split(value):
    high = value.astype(jnp.bfloat16)
    return high, (value - high.astype(jnp.float32)).astype(jnp.bfloat16)


def transform(table, parts):
    high, low = split(jnp.concatenate(parts, axis=1))
    return jnp.dot(table[...], jnp.concatenate((high, low, high), axis=0), preferred_element_type=jnp.float32)


def pack_kernel(
    forcing, init, scale, vol, faces, out, ops, lows, diag, value, state, elems, volume, sides, rows, flip, sems
):
    copies = [
        pltpu.make_async_copy(ref, into, sems.at[i])
        for i, (ref, into) in enumerate(
            ((vol, volume), (faces, sides), (forcing, value), (init, state), (scale, elems))
        )
    ]
    for copy in copies:
        copy.start()
    step = lax.axis_index("z") * 8 + lax.axis_index("x") * 2 + lax.axis_index("core")
    weight = jnp.where(step == 0, 1.5, 0.5).astype(jnp.float32)
    flip[...] = jnp.zeros((LANES, LANES), jnp.float32)
    rows[NB:, :] = jnp.zeros((LANES - NB, LANES), jnp.float32)
    for copy in copies[:2]:
        copy.wait()
    row = lax.broadcasted_iota(jnp.int32, (LANES, LANES), 0)
    col = lax.broadcasted_iota(jnp.int32, (LANES, LANES), 1)
    for op in range(5):
        flip[:NB, :NB] = volume[0] if op == 0 else sides[:, op - 1, :]
        square = flip[...]
        if op == 0:
            on = jnp.where(row == col, square, 0.0)
            diag[...] = jnp.broadcast_to(jnp.sum(on, axis=0, keepdims=True), (8, LANES))
            square = square - on
        square = square.T
        high, low = split(square)
        if op == 0:
            here, rest = 4 * LANES, ops.at[:LANES, 5 * LANES :]
        else:
            here = (op - 1) * LANES
            rest = lows.at[:, here : here + LANES]
        ops[:LANES, here : here + LANES] = high
        ops[LANES:, here : here + LANES] = high
        rest[...] = low
    ops[LANES:, 5 * LANES :] = jnp.zeros((LANES, LANES), jnp.bfloat16)
    for copy in copies[2:]:
        copy.wait()
    for s in (1, 0):
        for r in range(2):
            if s == 0:
                rows[:NB, :] = value[s * NB : (s + 1) * NB, r, :] + weight * state[0, :, r, :]
                rows[ES_LANE : ES_LANE + 1, :] = elems[0, r : r + 1, :]
            else:
                rows[:NB, :] = value[s * NB : (s + 1) * NB, r, :]
            flip[...] = rows[...].T
            for c in range(2):
                out[pl.ds(s * 8 + c * 2 + r, STEPS, stride=12), :] = flip[pl.ds(c, STEPS, stride=2), :]
    blank = jnp.zeros((4, LANES), jnp.float32)
    for m in range(STEPS):
        source = m - 4 if m % 8 < 4 else m + 4
        at = m * 12 + 4
        if 0 <= source < STEPS:
            out[at : at + 4, :] = out[source * 12 : source * 12 + 4, :]
        else:
            out[at : at + 4, :] = blank


def forward_kernel(table, got, out):
    lane = lax.broadcasted_iota(jnp.int32, (STEPS, LANES), 1)
    parts = [got[pl.ds(p, STEPS, stride=12), :] for p in range(12)]
    waves = transform(table, parts)
    for p in range(12):
        wave = waves[:, p * LANES : (p + 1) * LANES]
        if p < 8:
            wave = jnp.where(lane == ES_LANE, jnp.broadcast_to(parts[p][:1, :], wave.shape), wave)
        for c in range(2):
            at = c * 8 + p if p < 8 else 16 + c * 4 + p - 8
            out[pl.ds(at, FREQS, stride=24), :] = wave[c * FREQS : (c + 1) * FREQS]


def slot():
    return lax.axis_index("x") * 8 + lax.axis_index("core") * 4 + lax.axis_index("y")


def invert(slots, diag, scale, inverse):
    mine = slots[slot()]
    shape = (WINDOW, 8, LANES)
    place = lax.axis_index("z") * CHUNK - HALO + lax.broadcasted_iota(jnp.int32, shape, 0)
    inside = jnp.logical_and(place >= 0, place < 8 * CHUNK)
    scaled = scale[...] * diag[...][None]
    im = mine[2:3][None]
    re0 = mine[0:1][None] + scaled
    re1 = mine[1:2][None] + scaled
    mod0 = jnp.where(inside, damping / (re0 * re0 + im * im), 0.0)
    mod1 = jnp.where(inside, damping / (re1 * re1 + im * im), 0.0)
    inverse[0] = re0 * mod0
    inverse[1] = re1 * mod1
    inverse[2] = im * mod0


def relax(ops, lows, scale, inverse, iterate, source):
    lane = lax.broadcasted_iota(jnp.int32, (WINDOW, 8, LANES), 2)
    g0 = jnp.where(lane < NB, iterate[0], 0.0)
    g1 = jnp.where(lane < NB, iterate[1], 0.0)
    source[0] = inverse[0] * g0 + inverse[2] * g1
    source[1] = inverse[1] * g1 - inverse[2] * g0
    iterate[0] = source[0]
    iterate[1] = source[1]
    for sweep in range(1, SWEEPS):
        lo, hi = sweep + 1, WINDOW - sweep - 1
        wide = hi - lo + 2
        coupled = []
        for c in range(2):
            field = iterate[c, lo - 1 : hi + 1].reshape(wide * 8, LANES)
            high, low = split(field)
            sums = jnp.dot(
                jnp.concatenate((high, low), axis=1), ops[...], preferred_element_type=jnp.float32
            )
            rest = jnp.dot(high, lows[...], preferred_element_type=jnp.float32)
            part = [sums[:, i * LANES : (i + 1) * LANES].reshape(wide, 8, LANES) for i in range(6)]
            face = [
                part[i] + rest[:, i * LANES : (i + 1) * LANES].reshape(wide, 8, LANES) for i in range(4)
            ]
            coupled.append(
                scale[lo:hi] * (part[4] + part[5])[1:-1]
                + face[0][:-2]
                + face[1][2:]
                + pltpu.roll(face[2][1:-1], 1, 1)
                + pltpu.roll(face[3][1:-1], 7, 1)
            )
        cross = inverse[2, lo:hi]
        new0 = (1.0 - damping) * iterate[0, lo:hi] + source[0, lo:hi] - inverse[0, lo:hi] * coupled[0] - cross * coupled[1]
        new1 = (1.0 - damping) * iterate[1, lo:hi] + source[1, lo:hi] - inverse[1, lo:hi] * coupled[1] + cross * coupled[0]
        iterate[0, lo:hi] = new0
        iterate[1, lo:hi] = new1


def first_kernel(slots, ops, lows, diag, got, solved, state, scale, inverse, iterate, source):
    for xc in range(8):
        for yd in range(4):
            for c in range(2):
                for col in range(4):
                    w = HALO + 2 * xc + col
                    if col >= 2:
                        w = (2 * xc if xc < 4 else 16 + 2 * xc) + col - 2
                    at = c * 8 + col * 2
                    iterate[c, w, 2 * yd : 2 * yd + 2, :] = got[xc * 4 + yd, at : at + 2, :]
    scale[...] = jnp.broadcast_to(iterate[0, :, :, ES_LANE : ES_LANE + 1], scale.shape)
    invert(slots, diag, scale, inverse)
    relax(ops, lows, scale, inverse, iterate, source)
    mine = slots[slot()]
    middle = iterate[:, HALO : HALO + CHUNK]
    solved[...] = middle
    state[...] = mine[3:4][None] * middle[0] + mine[4:5][None] * middle[1]


def between_kernel(got, solved, after, done, left, right):
    del after
    for c in range(2):
        for xc in range(8):
            side = left if xc < 4 else right
            for yd in range(4):
                for col in range(2):
                    rows = slice(2 * yd, 2 * yd + 2)
                    at = c * 4 + col * 2
                    done[xc * 4 + yd, at : at + 2, :] = solved[c, 2 * xc + col, rows, :]
                    side[c, 2 * (xc % 4) + col, rows, :] = got[xc * 4 + yd, 16 + at : 18 + at, :]


def carry_kernel(slots, left, right, state0, state1, state2, state3, out_left, out_right):
    state = (state0[...] + state1[...]) + (state2[...] + state3[...])
    mine = slots[slot()]
    for c in range(2):
        part = mine[5 + c : 6 + c][None] * state
        out_left[c] = left[c] + part[: CHUNK // 2]
        out_right[c] = right[c] + part[CHUNK // 2 :]


def second_kernel(ops, lows, scale, inverse, west, left, right, east, before, out, iterate, source):
    for i, part in enumerate((west, left, right, east)):
        iterate[:, i * HALO : (i + 1) * HALO] = part[...]
    out[:, :8, :] = before[...]
    relax(ops, lows, scale, inverse, iterate, source)
    for xc in range(8):
        for yd in range(4):
            for c in range(2):
                for col in range(2):
                    at = 8 + c * 4 + col * 2
                    out[xc * 4 + yd, at : at + 2, :] = iterate[c, HALO + 2 * xc + col, 2 * yd : 2 * yd + 2, :]


def backward_kernel(table, got, out):
    parts = []
    for p in range(8):
        at = (p // 4) * 8 + p % 4
        halves = [got[pl.ds(at + 4 * c, FREQS, stride=16), :] for c in range(2)]
        parts.append(jnp.concatenate(halves, axis=0))
    slices = transform(table, parts)
    for p in range(8):
        out[pl.ds(p, STEPS, stride=8), :] = slices[:, p * LANES : (p + 1) * LANES]


def unpack_kernel(got, out, flip, held, sems):
    copies = []
    for s in range(2):
        for r in range(2):
            for c in range(2):
                flip[pl.ds(c, STEPS, stride=2), :] = got[pl.ds(s * 4 + c * 2 + r, STEPS, stride=8), :]
            held[s, 0, :, r, :] = flip[...].T[:NB, :]
        copies.append(pltpu.make_async_copy(held.at[s], out.at[s], sems.at[s]))
        copies[s].start()
    for copy in copies:
        copy.wait()


def call(kernel, outs, ins, scratch=(), specs=None, name=None, params=PARAMS, out=VMEM):
    return pl.pallas_call(
        kernel,
        out_shape=outs,
        in_specs=specs or [VMEM] * len(ins),
        out_specs=jax.tree.map(lambda _: out, outs),
        scratch_shapes=scratch,
        compiler_params=params,
        name=name,
    )(*ins)


def f32(*shape):
    return jax.ShapeDtypeStruct(shape, jnp.float32)


def exchange(blocks, axes):
    return lax.all_to_all(blocks, axes, 0, 0, tiled=True)


def moved(block, axis, by):
    count = lax.axis_size(axis)
    return lax.ppermute(block, axis, [(i, (i + by) % count) for i in range(count)])


def per_device(forcing, init_state, elem_scale, vol_op, face_ops):
    square = pltpu.VMEM((LANES, LANES), jnp.float32)
    window = (WINDOW, 8, LANES)
    inputs = (
        forcing.reshape(2 * NB, 2, LANES),
        init_state.reshape(1, NB, 2, LANES),
        elem_scale.reshape(1, 2, LANES),
        vol_op.reshape(1, NB, NB),
        jnp.transpose(face_ops, (1, 0, 2)),
    )
    packed, ops, lows, diag = call(
        pack_kernel,
        (
            pltpu.VMEM((STEPS * 12, LANES), jnp.float32),
            pltpu.VMEM((2 * LANES, 6 * LANES), jnp.bfloat16),
            pltpu.VMEM((LANES, 4 * LANES), jnp.bfloat16),
            pltpu.VMEM((8, LANES), jnp.float32),
        ),
        inputs,
        [pltpu.VMEM(value.shape, jnp.float32) for value in inputs]
        + [square, square, pltpu.SemaphoreType.DMA((len(inputs),))],
        [HBM] * len(inputs),
        name="pack",
        params=pltpu.CompilerParams(vmem_limit_bytes=60 * 1024 * 1024),
    )
    by_point = exchange(packed.reshape(STEPS, 3, 4, LANES), TIME).reshape(STEPS * 12, LANES)
    waves = call(forward_kernel, f32(FREQS * 24, LANES), (FORWARD, by_point), name="forward")
    got = exchange(waves.reshape(FREQS, 24, LANES), PLANE)
    both = pltpu.VMEM((2,) + window, jnp.float32)
    solved, state, scale, inverse = call(
        first_kernel,
        (f32(2, CHUNK, 8, LANES), f32(CHUNK, 8, LANES), f32(*window), f32(3, *window)),
        (SLOTS, ops, lows, diag, got),
        (both, both),
        name="first",
    )
    half = f32(2, CHUNK // 2, 8, LANES)
    state = state + moved(state, "core", 1)
    done, left, right = call(
        between_kernel, (f32(FREQS, 8, LANES), half, half), (got, solved, state), (), [VMEM, VMEM, ANY], name="between"
    )
    state = state + moved(state, "y", 1) + moved(state, "y", 2) + moved(state, "y", 3)
    states = [state] + [moved(state, "x", by) for by in (1, 2, 3)]
    left, right = call(carry_kernel, (half, half), (SLOTS, left, right, *states), name="carry")
    west = moved(right, "z", 1)
    east = moved(left, "z", -1)
    done = call(
        second_kernel,
        f32(FREQS, 16, LANES),
        (ops, lows, scale, inverse, west, left, right, east, done),
        (both, both),
        name="second",
    )
    got = exchange(done, PLANE).reshape(FREQS * 16, LANES)
    slices = call(backward_kernel, f32(STEPS * 8, LANES), (BACKWARD, got), name="backward")
    by_column = exchange(slices.reshape(STEPS, 8, LANES), TIME).reshape(STEPS * 8, LANES)
    result = f32(2, 1, NB, 2, LANES)
    return call(
        unpack_kernel,
        result,
        (by_column,),
        (square, pltpu.VMEM(result.shape, jnp.float32), pltpu.SemaphoreType.DMA((2,))),
        name="unpack",
        out=ANY,
    )


def solution(mesh):
    grid = Mesh(mesh.devices.reshape(8, 4, 2, 4), ("z", "x", "core", "y"))
    return jax.shard_map(
        per_device,
        mesh=grid,
        in_specs=(
            P(None, TIME, None, "y", None),
            P(None, "y", None),
            P("y", None),
            P(),
            P(),
        ),
        out_specs=P(None, TIME, None, "y", None),
        check_vma=False,
    )
```

```python
import math

import jax
import jax.numpy as jnp
import ml_dtypes
import numpy as np
from jax import lax
from jax.experimental import pallas as pl
from jax.experimental.pallas import tpu as pltpu
from jax.sharding import Mesh
from jax.sharding import PartitionSpec as P

NB = 125
SWEEPS = 8
STEPS = 64
LANES = 128
FREQS = STEPS // 2
CHUNK = 16
WINDOW = 32
HALO = 8
ES_LANE = NB

circ_alpha = 0.01
damping = 0.7

TIME = ("z", "x", "core")
PLANE = ("x", "core", "y")


def tables():
    n = np.arange(STEPS)
    log_alpha = math.log(circ_alpha)
    grow = np.exp(n * (log_alpha / STEPS))
    forward = np.zeros((STEPS, STEPS))
    backward = np.zeros((STEPS, STEPS))
    shifts = np.zeros((FREQS, 4))
    root = math.exp(log_alpha / STEPS)
    forward[0] = 1.0
    forward[1] = (-1.0) ** n
    backward[:, 0] = 1.0
    backward[:, 1] = (-1.0) ** n
    shifts[0] = (1.0 - root, 1.0 + root, 0.0, 0.0)
    for k in range(1, FREQS):
        angle = 2.0 * math.pi * ((k * n) % STEPS) / STEPS
        forward[2 * k] = np.cos(angle)
        forward[2 * k + 1] = -np.sin(angle)
        backward[:, 2 * k] = 2.0 * np.cos(angle)
        backward[:, 2 * k + 1] = -2.0 * np.sin(angle)
        theta = 2.0 * math.pi * k / STEPS
        shifts[k, :3] = (1.0 - root * math.cos(theta), 1.0 - root * math.cos(theta), root * math.sin(theta))
    forward = forward * grow[None, :]
    backward = backward / grow[:, None] / STEPS
    carry = 0.5 * forward.sum(1) + forward[:, 0]
    last = backward[STEPS - 1]
    return tuple(a.astype(np.float32) for a in (forward, backward, shifts, carry, last))


def in_parts(table):
    high = table.astype(ml_dtypes.bfloat16)
    rest = table - high.astype(np.float32)
    middle = rest.astype(ml_dtypes.bfloat16)
    low = (rest - middle.astype(np.float32)).astype(ml_dtypes.bfloat16)
    return np.concatenate((high, high, middle, high, middle, low), axis=1)


FORWARD, BACKWARD, SHIFTS, CARRY, LAST = tables()
BY_PART = np.concatenate((np.arange(0, STEPS, 2), np.arange(1, STEPS, 2)))
FORWARD = in_parts(FORWARD[BY_PART])
BACKWARD = in_parts(BACKWARD[:, BY_PART])
SLOTS = np.concatenate((SHIFTS[:, :3], LAST.reshape(FREQS, 2), CARRY.reshape(FREQS, 2), SHIFTS[:, :1]), axis=1)
SLOTS = np.repeat(SLOTS[:, :, None], LANES, axis=2)

VMEM = pl.BlockSpec(memory_space=pltpu.VMEM)
HBM = pl.BlockSpec(memory_space=pltpu.HBM)
ANY = pl.BlockSpec(memory_space=pl.ANY)
PARAMS = pltpu.CompilerParams(vmem_limit_bytes=32 * 1024 * 1024)


def split(value):
    high = value.astype(jnp.bfloat16)
    return high, (value - high.astype(jnp.float32)).astype(jnp.bfloat16)


def transform(table, parts):
    whole = jnp.concatenate(parts, axis=1)
    high = whole.astype(jnp.bfloat16)
    middle, low = split(whole - high.astype(jnp.float32))
    stack = jnp.concatenate((high, middle, high, low, middle, high), axis=0)
    return jnp.dot(table[...], stack, preferred_element_type=jnp.float32)


def pack_kernel(
    forcing, init, scale, vol, faces, out, ops, lows, diag, value, state, elems, volume, sides, rows, flip, sems
):
    copies = [
        pltpu.make_async_copy(ref, into, sems.at[i])
        for i, (ref, into) in enumerate(
            ((vol, volume), (faces, sides), (forcing, value), (init, state), (scale, elems))
        )
    ]
    for copy in copies:
        copy.start()
    step = lax.axis_index("z") * 8 + lax.axis_index("x") * 2 + lax.axis_index("core")
    weight = jnp.where(step == 0, 1.5, 0.5).astype(jnp.float32)
    flip[...] = jnp.zeros((LANES, LANES), jnp.float32)
    rows[NB:, :] = jnp.zeros((LANES - NB, LANES), jnp.float32)
    for copy in copies[:2]:
        copy.wait()
    row = lax.broadcasted_iota(jnp.int32, (LANES, LANES), 0)
    col = lax.broadcasted_iota(jnp.int32, (LANES, LANES), 1)
    for op in range(5):
        flip[:NB, :NB] = volume[0] if op == 0 else sides[:, op - 1, :]
        square = flip[...]
        if op == 0:
            on = jnp.where(row == col, square, 0.0)
            diag[...] = jnp.broadcast_to(jnp.sum(on, axis=0, keepdims=True), (8, LANES))
            square = square - on
        square = square.T
        high, low = split(square)
        if op == 0:
            here, rest = 4 * LANES, ops.at[:LANES, 5 * LANES :]
        else:
            here = (op - 1) * LANES
            rest = lows.at[:, here : here + LANES]
        ops[:LANES, here : here + LANES] = high
        ops[LANES:, here : here + LANES] = high
        rest[...] = low
    ops[LANES:, 5 * LANES :] = jnp.zeros((LANES, LANES), jnp.bfloat16)
    for copy in copies[2:]:
        copy.wait()
    for s in (1, 0):
        for r in range(2):
            if s == 0:
                rows[:NB, :] = value[s * NB : (s + 1) * NB, r, :] + weight * state[0, :, r, :]
                rows[ES_LANE : ES_LANE + 1, :] = elems[0, r : r + 1, :]
            else:
                rows[:NB, :] = value[s * NB : (s + 1) * NB, r, :]
            flip[...] = rows[...].T
            for c in range(2):
                out[pl.ds(s * 8 + c * 2 + r, STEPS, stride=12), :] = flip[pl.ds(c, STEPS, stride=2), :]
    blank = jnp.zeros((4, LANES), jnp.float32)
    for m in range(STEPS):
        source = m - 4 if m % 8 < 4 else m + 4
        at = m * 12 + 4
        if 0 <= source < STEPS:
            out[at : at + 4, :] = out[source * 12 : source * 12 + 4, :]
        else:
            out[at : at + 4, :] = blank


def forward_kernel(table, got, out):
    lane = lax.broadcasted_iota(jnp.int32, (STEPS, LANES), 1)
    parts = [got[pl.ds(p, STEPS, stride=12), :] for p in range(12)]
    waves = transform(table, parts)
    for p in range(12):
        wave = waves[:, p * LANES : (p + 1) * LANES]
        if p < 8:
            wave = jnp.where(lane == ES_LANE, jnp.broadcast_to(parts[p][:1, :], wave.shape), wave)
        for c in range(2):
            at = c * 8 + p if p < 8 else 16 + c * 4 + p - 8
            out[pl.ds(at, FREQS, stride=24), :] = wave[c * FREQS : (c + 1) * FREQS]


def slot():
    return lax.axis_index("x") * 8 + lax.axis_index("core") * 4 + lax.axis_index("y")


def invert(slots, diag, scale, inverse):
    mine = slots[slot()]
    shape = (WINDOW, 8, LANES)
    place = lax.axis_index("z") * CHUNK - HALO + lax.broadcasted_iota(jnp.int32, shape, 0)
    inside = jnp.logical_and(place >= 0, place < 8 * CHUNK)
    scaled = scale[...] * diag[...][None]
    im = mine[2:3][None]
    re0 = mine[0:1][None] + scaled
    re1 = mine[1:2][None] + scaled
    mod0 = jnp.where(inside, damping / (re0 * re0 + im * im), 0.0)
    mod1 = jnp.where(inside, damping / (re1 * re1 + im * im), 0.0)
    inverse[0] = re0 * mod0
    inverse[1] = re1 * mod1
    inverse[2] = im * mod0


def start(inverse, field, source, at):
    lane = lax.broadcasted_iota(jnp.int32, field.shape[1:], 2)
    g0 = jnp.where(lane < NB, field[0], 0.0)
    g1 = jnp.where(lane < NB, field[1], 0.0)
    source[0, at] = inverse[0, at] * g0 + inverse[2, at] * g1
    source[1, at] = inverse[1, at] * g1 - inverse[2, at] * g0


def couple(ops, lows, scale, field):
    wide = field.shape[0]
    inner = (wide - 2, 8, LANES)
    high, low = split(field.reshape(wide * 8, LANES))
    both = jnp.concatenate((high, low), axis=1)

    def product(left, right):
        return jnp.dot(left, right, preferred_element_type=jnp.float32)

    def columns(sums, i):
        return sums[:, i * LANES : (i + 1) * LANES].reshape(-1, 8, LANES)

    own = product(both[8:-8], ops[:, 4 * LANES :])
    along = product(both, ops[:, : 2 * LANES]) + product(high, lows[:, : 2 * LANES])
    across = product(both[8:-8], ops[:, 2 * LANES : 4 * LANES]) + product(high[8:-8], lows[:, 2 * LANES :])
    return (
        scale * (columns(own, 0) + columns(own, 1))
        + columns(along, 0)[:-2]
        + columns(along, 1)[2:]
        + pltpu.roll(columns(across, 0), 1, 1)
        + pltpu.roll(columns(across, 1), 7, 1)
    )


def damped(field, source, inverse, coupled):
    keep = 1.0 - damping
    return (
        keep * field[0] + source[0] - inverse[0] * coupled[0] - inverse[2] * coupled[1],
        keep * field[1] + source[1] - inverse[1] * coupled[1] + inverse[2] * coupled[0],
    )


def relax(ops, lows, scale, inverse, iterate, source):
    start(inverse, iterate[...], source, slice(0, WINDOW))
    iterate[...] = source[...]
    for sweep in range(1, SWEEPS):
        here = slice(sweep + 1, WINDOW - sweep - 1)
        coupled = [couple(ops, lows, scale[here], iterate[c, sweep : WINDOW - sweep]) for c in range(2)]
        fresh = damped(iterate[:, here], source[:, here], inverse[:, here], coupled)
        iterate[0, here] = fresh[0]
        iterate[1, here] = fresh[1]


def first_kernel(slots, ops, lows, diag, got, solved, state, scale, inverse, iterate, source):
    for xc in range(8):
        for yd in range(4):
            for c in range(2):
                for col in range(4):
                    w = HALO + 2 * xc + col
                    if col >= 2:
                        w = (2 * xc if xc < 4 else 16 + 2 * xc) + col - 2
                    at = c * 8 + col * 2
                    iterate[c, w, 2 * yd : 2 * yd + 2, :] = got[xc * 4 + yd, at : at + 2, :]
    scale[...] = jnp.broadcast_to(iterate[0, :, :, ES_LANE : ES_LANE + 1], scale.shape)
    invert(slots, diag, scale, inverse)
    relax(ops, lows, scale, inverse, iterate, source)
    mine = slots[slot()]
    middle = iterate[:, HALO : HALO + CHUNK]
    solved[...] = middle
    state[...] = mine[3:4][None] * middle[0] + mine[4:5][None] * middle[1]


def between_kernel(got, solved, after, done, left, right):
    del after
    for c in range(2):
        for xc in range(8):
            side = left if xc < 4 else right
            for yd in range(4):
                for col in range(2):
                    rows = slice(2 * yd, 2 * yd + 2)
                    at = c * 4 + col * 2
                    done[xc * 4 + yd, at : at + 2, :] = solved[c, 2 * xc + col, rows, :]
                    side[c, 2 * (xc % 4) + col, rows, :] = got[xc * 4 + yd, 16 + at : 18 + at, :]


def carry_kernel(slots, left, right, state0, state1, state2, state3, out_left, out_right):
    state = (state0[...] + state1[...]) + (state2[...] + state3[...])
    mine = slots[slot()]
    for c in range(2):
        part = mine[5 + c : 6 + c][None] * state
        out_left[c] = left[c] + part[: CHUNK // 2]
        out_right[c] = right[c] + part[CHUNK // 2 :]


def inner_kernel(ops, lows, scale, inverse, left, right, edges, iterate, source):
    middle = slice(HALO, HALO + CHUNK)
    for i, part in enumerate((left, right)):
        start(inverse, part[...], source, slice((i + 1) * HALO, (i + 2) * HALO))
    iterate[...] = source[:, middle]
    for sweep in range(SWEEPS):
        lo, hi = sweep, CHUNK - sweep
        if sweep:
            here = slice(HALO + lo, HALO + hi)
            coupled = [couple(ops, lows, scale[here], iterate[c, lo - 1 : hi + 1]) for c in range(2)]
            fresh = damped(iterate[:, lo:hi], source[:, here], inverse[:, here], coupled)
            iterate[0, lo:hi] = fresh[0]
            iterate[1, lo:hi] = fresh[1]
        edges[sweep, :, :2] = iterate[:, lo : lo + 2]
        edges[sweep, :, 2:] = iterate[:, hi - 2 : hi]


def outer_kernel(ops, lows, scale, inverse, west, left, right, east, edges, before, out, iterate, source):
    for i, part in enumerate((west, left, right, east)):
        start(inverse, part[...], source, slice(i * HALO, (i + 1) * HALO))
    out[:, :8, :] = before[...]
    reach = SWEEPS - 1
    iterate[:, :reach] = source[:, 1:HALO]
    iterate[:, reach + 4 :] = source[:, HALO + CHUNK : WINDOW - 1]
    for sweep in range(1, SWEEPS):
        iterate[:, reach : reach + 4] = edges[sweep - 1]
        one = slice(sweep + 1, HALO + sweep)
        two = slice(WINDOW - HALO - sweep, WINDOW - 1 - sweep)
        sides = [
            jnp.concatenate((ref[one], ref[HALO : HALO + 2], ref[two]), axis=0)
            for ref in [scale] + [inverse.at[i] for i in range(3)] + [source.at[i] for i in range(2)]
        ]
        coupled = [couple(ops, lows, sides[0], iterate[c]) for c in range(2)]
        fresh = damped(iterate[:, 1:-1], sides[4:], sides[1:4], coupled)
        for c in range(2):
            iterate[c, :reach] = fresh[c][:reach]
            iterate[c, reach + 4 :] = fresh[c][reach + 2 :]
    last = edges.at[SWEEPS - 1]
    for xc in range(8):
        for col in range(2):
            x = 2 * xc + col
            for c in range(2):
                if x < reach:
                    tile = iterate.at[c, x]
                elif x < reach + 2:
                    tile = last.at[c, x - reach]
                else:
                    tile = iterate.at[c, x + 2]
                at = 8 + c * 4 + col * 2
                for yd in range(4):
                    out[xc * 4 + yd, at : at + 2, :] = tile[2 * yd : 2 * yd + 2, :]


def backward_kernel(table, got, out):
    parts = []
    for p in range(8):
        at = (p // 4) * 8 + p % 4
        halves = [got[pl.ds(at + 4 * c, FREQS, stride=16), :] for c in range(2)]
        parts.append(jnp.concatenate(halves, axis=0))
    slices = transform(table, parts)
    for p in range(8):
        out[pl.ds(p, STEPS, stride=8), :] = slices[:, p * LANES : (p + 1) * LANES]


def unpack_kernel(got, out, flip, held, sems):
    copies = []
    for s in range(2):
        for r in range(2):
            for c in range(2):
                flip[pl.ds(c, STEPS, stride=2), :] = got[pl.ds(s * 4 + c * 2 + r, STEPS, stride=8), :]
            held[s, 0, :, r, :] = flip[...].T[:NB, :]
        copies.append(pltpu.make_async_copy(held.at[s], out.at[s], sems.at[s]))
        copies[s].start()
    for copy in copies:
        copy.wait()


def call(kernel, outs, ins, scratch=(), specs=None, name=None, params=PARAMS, out=VMEM, cost=None):
    return pl.pallas_call(
        kernel,
        out_shape=outs,
        in_specs=specs or [VMEM] * len(ins),
        out_specs=jax.tree.map(lambda _: out, outs),
        scratch_shapes=scratch,
        compiler_params=params,
        cost_estimate=cost,
        name=name,
    )(*ins)


def f32(*shape):
    return jax.ShapeDtypeStruct(shape, jnp.float32)


def exchange(blocks, axes):
    return lax.all_to_all(blocks, axes, 0, 0, tiled=True)


def moved(block, axis, by):
    count = lax.axis_size(axis)
    return lax.ppermute(block, axis, [(i, (i + by) % count) for i in range(count)])


def per_device(forcing, init_state, elem_scale, vol_op, face_ops):
    square = pltpu.VMEM((LANES, LANES), jnp.float32)
    window = (WINDOW, 8, LANES)
    inputs = (
        forcing.reshape(2 * NB, 2, LANES),
        init_state.reshape(1, NB, 2, LANES),
        elem_scale.reshape(1, 2, LANES),
        vol_op.reshape(1, NB, NB),
        jnp.transpose(face_ops, (1, 0, 2)),
    )
    packed, ops, lows, diag = call(
        pack_kernel,
        (
            pltpu.VMEM((STEPS * 12, LANES), jnp.float32),
            pltpu.VMEM((2 * LANES, 6 * LANES), jnp.bfloat16),
            pltpu.VMEM((LANES, 4 * LANES), jnp.bfloat16),
            pltpu.VMEM((8, LANES), jnp.float32),
        ),
        inputs,
        [pltpu.VMEM(value.shape, jnp.float32) for value in inputs]
        + [square, square, pltpu.SemaphoreType.DMA((len(inputs),))],
        [HBM] * len(inputs),
        name="pack",
        params=pltpu.CompilerParams(vmem_limit_bytes=60 * 1024 * 1024),
    )
    by_point = exchange(packed.reshape(STEPS, 3, 4, LANES), TIME).reshape(STEPS * 12, LANES)
    waves = call(forward_kernel, f32(FREQS * 24, LANES), (FORWARD, by_point), name="forward")
    got = exchange(waves.reshape(FREQS, 24, LANES), PLANE)
    both = pltpu.VMEM((2,) + window, jnp.float32)
    solved, state, scale, inverse = call(
        first_kernel,
        (f32(2, CHUNK, 8, LANES), f32(CHUNK, 8, LANES), f32(*window), f32(3, *window)),
        (SLOTS, ops, lows, diag, got),
        (both, both),
        name="first",
    )
    half = f32(2, CHUNK // 2, 8, LANES)
    state = state + moved(state, "core", 1)
    done, left, right = call(
        between_kernel, (f32(FREQS, 8, LANES), half, half), (got, solved, state), (), [VMEM, VMEM, ANY], name="between"
    )
    state = state + moved(state, "y", 1) + moved(state, "y", 2) + moved(state, "y", 3)
    states = [state] + [moved(state, "x", by) for by in (1, 2, 3)]
    left, right = call(carry_kernel, (half, half), (SLOTS, left, right, *states), name="carry")
    west = moved(right, "z", 1)
    east = moved(left, "z", -1)
    edges = call(
        inner_kernel,
        f32(SWEEPS, 2, 4, 8, LANES),
        (ops, lows, scale, inverse, left, right),
        (pltpu.VMEM((2, CHUNK, 8, LANES), jnp.float32), both),
        name="inner",
        cost=pl.CostEstimate(flops=2_000_000_000, bytes_accessed=1_000_000, transcendentals=0),
    )
    done = call(
        outer_kernel,
        f32(FREQS, 16, LANES),
        (ops, lows, scale, inverse, west, left, right, east, edges, done),
        (pltpu.VMEM((2, 2 * SWEEPS + 2, 8, LANES), jnp.float32), both),
        name="outer",
    )
    got = exchange(done, PLANE).reshape(FREQS * 16, LANES)
    slices = call(backward_kernel, f32(STEPS * 8, LANES), (BACKWARD, got), name="backward")
    by_column = exchange(slices.reshape(STEPS, 8, LANES), TIME).reshape(STEPS * 8, LANES)
    result = f32(2, 1, NB, 2, LANES)
    return call(
        unpack_kernel,
        result,
        (by_column,),
        (square, pltpu.VMEM(result.shape, jnp.float32), pltpu.SemaphoreType.DMA((2,))),
        name="unpack",
        out=ANY,
    )


def solution(mesh):
    grid = Mesh(mesh.devices.reshape(8, 4, 2, 4), ("z", "x", "core", "y"))
    return jax.shard_map(
        per_device,
        mesh=grid,
        in_specs=(
            P(None, TIME, None, "y", None),
            P(None, "y", None),
            P("y", None),
            P(),
            P(),
        ),
        out_specs=P(None, TIME, None, "y", None),
        check_vma=False,
    )
```

```python
import math

import jax
import jax.numpy as jnp
import ml_dtypes
import numpy as np
from jax import lax
from jax.experimental import pallas as pl
from jax.experimental.pallas import tpu as pltpu
from jax.sharding import Mesh
from jax.sharding import PartitionSpec as P

NB = 125
SWEEPS = 8
STEPS = 64
LANES = 128
FREQS = STEPS // 2
CHUNK = 16
WINDOW = 32
HALO = 8
ES_LANE = NB

circ_alpha = 0.01
damping = 0.7

TIME = ("z", "x", "core")
PLANE = ("core", "y", "x")


def tables():
    n = np.arange(STEPS)
    log_alpha = math.log(circ_alpha)
    grow = np.exp(n * (log_alpha / STEPS))
    forward = np.zeros((STEPS, STEPS))
    backward = np.zeros((STEPS, STEPS))
    shifts = np.zeros((FREQS, 4))
    root = math.exp(log_alpha / STEPS)
    forward[0] = 1.0
    forward[1] = (-1.0) ** n
    backward[:, 0] = 1.0
    backward[:, 1] = (-1.0) ** n
    shifts[0] = (1.0 - root, 1.0 + root, 0.0, 0.0)
    for k in range(1, FREQS):
        angle = 2.0 * math.pi * ((k * n) % STEPS) / STEPS
        forward[2 * k] = np.cos(angle)
        forward[2 * k + 1] = -np.sin(angle)
        backward[:, 2 * k] = 2.0 * np.cos(angle)
        backward[:, 2 * k + 1] = -2.0 * np.sin(angle)
        theta = 2.0 * math.pi * k / STEPS
        shifts[k, :3] = (1.0 - root * math.cos(theta), 1.0 - root * math.cos(theta), root * math.sin(theta))
    forward = forward * grow[None, :]
    backward = backward / grow[:, None] / STEPS
    carry = 0.5 * forward.sum(1) + forward[:, 0]
    last = backward[STEPS - 1]
    return tuple(a.astype(np.float32) for a in (forward, backward, shifts, carry, last))


def in_parts(table):
    high = table.astype(ml_dtypes.bfloat16)
    rest = table - high.astype(np.float32)
    middle = rest.astype(ml_dtypes.bfloat16)
    low = (rest - middle.astype(np.float32)).astype(ml_dtypes.bfloat16)
    return np.concatenate((high, high, middle, high, middle, low), axis=1)


FORWARD, BACKWARD, SHIFTS, CARRY, LAST = tables()
BY_PART = np.concatenate((np.arange(0, STEPS, 2), np.arange(1, STEPS, 2)))
FORWARD = in_parts(FORWARD[BY_PART])
BACKWARD = in_parts(BACKWARD[:, BY_PART])
SLOTS = np.concatenate((SHIFTS[:, :3], LAST.reshape(FREQS, 2), CARRY.reshape(FREQS, 2), SHIFTS[:, :1]), axis=1)
SLOTS = np.repeat(SLOTS[:, :, None], LANES, axis=2)

VMEM = pl.BlockSpec(memory_space=pltpu.VMEM)
HBM = pl.BlockSpec(memory_space=pltpu.HBM)
ANY = pl.BlockSpec(memory_space=pl.ANY)
PARAMS = pltpu.CompilerParams(vmem_limit_bytes=32 * 1024 * 1024)


def split(value):
    high = value.astype(jnp.bfloat16)
    return high, (value - high.astype(jnp.float32)).astype(jnp.bfloat16)


def transform(table, parts):
    whole = jnp.concatenate(parts, axis=1)
    high = whole.astype(jnp.bfloat16)
    middle, low = split(whole - high.astype(jnp.float32))
    stack = jnp.concatenate((high, middle, high, low, middle, high), axis=0)
    return jnp.dot(table[...], stack, preferred_element_type=jnp.float32)


def pack_kernel(
    forcing, init, scale, vol, faces, out, ops, lows, diag, value, state, elems, volume, sides, rows, flip, sems
):
    copies = [
        pltpu.make_async_copy(ref, into, sems.at[i])
        for i, (ref, into) in enumerate(
            ((vol, volume), (faces, sides), (forcing, value), (init, state), (scale, elems))
        )
    ]
    for copy in copies:
        copy.start()
    step = lax.axis_index("z") * 8 + lax.axis_index("x") * 2 + lax.axis_index("core")
    weight = jnp.where(step == 0, 1.5, 0.5).astype(jnp.float32)
    flip[...] = jnp.zeros((LANES, LANES), jnp.float32)
    rows[NB:, :] = jnp.zeros((LANES - NB, LANES), jnp.float32)
    for copy in copies[:2]:
        copy.wait()
    row = lax.broadcasted_iota(jnp.int32, (LANES, LANES), 0)
    col = lax.broadcasted_iota(jnp.int32, (LANES, LANES), 1)
    for op in range(5):
        flip[:NB, :NB] = volume[0] if op == 0 else sides[:, op - 1, :]
        square = flip[...]
        if op == 0:
            on = jnp.where(row == col, square, 0.0)
            diag[...] = jnp.broadcast_to(jnp.sum(on, axis=0, keepdims=True), (8, LANES))
            square = square - on
        square = square.T
        high, low = split(square)
        if op == 0:
            here, rest = 4 * LANES, ops.at[:LANES, 5 * LANES :]
        else:
            here = (op - 1) * LANES
            rest = lows.at[:, here : here + LANES]
        ops[:LANES, here : here + LANES] = high
        ops[LANES:, here : here + LANES] = high
        rest[...] = low
    ops[LANES:, 5 * LANES :] = jnp.zeros((LANES, LANES), jnp.bfloat16)
    for copy in copies[2:]:
        copy.wait()
    for s in (1, 0):
        for r in range(2):
            if s == 0:
                rows[:NB, :] = value[s * NB : (s + 1) * NB, r, :] + weight * state[0, :, r, :]
                rows[ES_LANE : ES_LANE + 1, :] = elems[0, r : r + 1, :]
            else:
                rows[:NB, :] = value[s * NB : (s + 1) * NB, r, :]
            flip[...] = rows[...].T
            for c in range(2):
                out[pl.ds(s * 8 + c * 2 + r, STEPS, stride=12), :] = flip[pl.ds(c, STEPS, stride=2), :]
    blank = jnp.zeros((4, LANES), jnp.float32)
    for m in range(STEPS):
        source = m - 4 if m % 8 < 4 else m + 4
        at = m * 12 + 4
        if 0 <= source < STEPS:
            out[at : at + 4, :] = out[source * 12 : source * 12 + 4, :]
        else:
            out[at : at + 4, :] = blank


def forward_kernel(table, got, out):
    lane = lax.broadcasted_iota(jnp.int32, (STEPS, LANES), 1)
    parts = [got[pl.ds(p, STEPS, stride=12), :] for p in range(12)]
    waves = transform(table, parts)
    for p in range(12):
        wave = waves[:, p * LANES : (p + 1) * LANES]
        if p < 8:
            wave = jnp.where(lane == ES_LANE, jnp.broadcast_to(parts[p][:1, :], wave.shape), wave)
        for c in range(2):
            at = c * 8 + p if p < 8 else 16 + c * 4 + p - 8
            out[pl.ds(at, FREQS, stride=24), :] = wave[c * FREQS : (c + 1) * FREQS]


def slot():
    return lax.axis_index("core") * 16 + lax.axis_index("y") * 4 + lax.axis_index("x")


def seat(xc, yd):
    return xc % 2 * 16 + yd * 4 + xc // 2


def invert(slots, diag, scale, inverse):
    mine = slots[slot()]
    shape = (WINDOW, 8, LANES)
    place = lax.axis_index("z") * CHUNK - HALO + lax.broadcasted_iota(jnp.int32, shape, 0)
    inside = jnp.logical_and(place >= 0, place < 8 * CHUNK)
    scaled = scale[...] * diag[...][None]
    im = mine[2:3][None]
    re0 = mine[0:1][None] + scaled
    re1 = mine[1:2][None] + scaled
    mod0 = jnp.where(inside, damping / (re0 * re0 + im * im), 0.0)
    mod1 = jnp.where(inside, damping / (re1 * re1 + im * im), 0.0)
    inverse[0] = re0 * mod0
    inverse[1] = re1 * mod1
    inverse[2] = im * mod0


def start(inverse, field, source, at):
    lane = lax.broadcasted_iota(jnp.int32, field.shape[1:], 2)
    g0 = jnp.where(lane < NB, field[0], 0.0)
    g1 = jnp.where(lane < NB, field[1], 0.0)
    source[0, at] = inverse[0, at] * g0 + inverse[2, at] * g1
    source[1, at] = inverse[1, at] * g1 - inverse[2, at] * g0


def couple(ops, lows, scale, field):
    wide = field.shape[0]
    inner = (wide - 2, 8, LANES)
    high, low = split(field.reshape(wide * 8, LANES))
    both = jnp.concatenate((high, low), axis=1)

    def product(left, right):
        return jnp.dot(left, right, preferred_element_type=jnp.float32)

    def columns(sums, i):
        return sums[:, i * LANES : (i + 1) * LANES].reshape(-1, 8, LANES)

    own = product(both[8:-8], ops[:, 4 * LANES :])
    along = product(both, ops[:, : 2 * LANES]) + product(high, lows[:, : 2 * LANES])
    across = product(both[8:-8], ops[:, 2 * LANES : 4 * LANES]) + product(high[8:-8], lows[:, 2 * LANES :])
    return (
        scale * (columns(own, 0) + columns(own, 1))
        + columns(along, 0)[:-2]
        + columns(along, 1)[2:]
        + pltpu.roll(columns(across, 0), 1, 1)
        + pltpu.roll(columns(across, 1), 7, 1)
    )


def damped(field, source, inverse, coupled):
    keep = 1.0 - damping
    return (
        keep * field[0] + source[0] - inverse[0] * coupled[0] - inverse[2] * coupled[1],
        keep * field[1] + source[1] - inverse[1] * coupled[1] + inverse[2] * coupled[0],
    )


def relax(ops, lows, scale, inverse, iterate, source):
    start(inverse, iterate[...], source, slice(0, WINDOW))
    iterate[...] = source[...]
    for sweep in range(1, SWEEPS):
        here = slice(sweep + 1, WINDOW - sweep - 1)
        coupled = [couple(ops, lows, scale[here], iterate[c, sweep : WINDOW - sweep]) for c in range(2)]
        fresh = damped(iterate[:, here], source[:, here], inverse[:, here], coupled)
        iterate[0, here] = fresh[0]
        iterate[1, here] = fresh[1]


def first_kernel(slots, ops, lows, diag, got, solved, state, scale, inverse, iterate, source):
    for xc in range(8):
        for yd in range(4):
            for c in range(2):
                for col in range(4):
                    w = HALO + 2 * xc + col
                    if col >= 2:
                        w = (2 * xc if xc < 4 else 16 + 2 * xc) + col - 2
                    at = c * 8 + col * 2
                    iterate[c, w, 2 * yd : 2 * yd + 2, :] = got[seat(xc, yd), at : at + 2, :]
    scale[...] = jnp.broadcast_to(iterate[0, :, :, ES_LANE : ES_LANE + 1], scale.shape)
    invert(slots, diag, scale, inverse)
    relax(ops, lows, scale, inverse, iterate, source)
    mine = slots[slot()]
    middle = iterate[:, HALO : HALO + CHUNK]
    solved[...] = middle
    state[...] = mine[3:4][None] * middle[0] + mine[4:5][None] * middle[1]


def between_kernel(got, solved, after, done, left, right):
    del after
    for c in range(2):
        for xc in range(8):
            side = left if xc < 4 else right
            for yd in range(4):
                for col in range(2):
                    rows = slice(2 * yd, 2 * yd + 2)
                    at = c * 4 + col * 2
                    done[seat(xc, yd), at : at + 2, :] = solved[c, 2 * xc + col, rows, :]
                    side[c, 2 * (xc % 4) + col, rows, :] = got[seat(xc, yd), 16 + at : 18 + at, :]


def carry_kernel(slots, left, right, state0, state1, state2, state3, out_left, out_right):
    state = (state0[...] + state1[...]) + (state2[...] + state3[...])
    mine = slots[slot()]
    for c in range(2):
        part = mine[5 + c : 6 + c][None] * state
        out_left[c] = left[c] + part[: CHUNK // 2]
        out_right[c] = right[c] + part[CHUNK // 2 :]


def inner_kernel(ops, lows, scale, inverse, left, right, edges, iterate, source):
    middle = slice(HALO, HALO + CHUNK)
    for i, part in enumerate((left, right)):
        start(inverse, part[...], source, slice((i + 1) * HALO, (i + 2) * HALO))
    iterate[...] = source[:, middle]
    for sweep in range(SWEEPS):
        lo, hi = sweep, CHUNK - sweep
        if sweep:
            here = slice(HALO + lo, HALO + hi)
            coupled = [couple(ops, lows, scale[here], iterate[c, lo - 1 : hi + 1]) for c in range(2)]
            fresh = damped(iterate[:, lo:hi], source[:, here], inverse[:, here], coupled)
            iterate[0, lo:hi] = fresh[0]
            iterate[1, lo:hi] = fresh[1]
        edges[sweep, :, :2] = iterate[:, lo : lo + 2]
        edges[sweep, :, 2:] = iterate[:, hi - 2 : hi]


def outer_kernel(ops, lows, scale, inverse, west, left, right, east, edges, before, out, iterate, source):
    for i, part in enumerate((west, left, right, east)):
        start(inverse, part[...], source, slice(i * HALO, (i + 1) * HALO))
    out[:, :8, :] = before[...]
    reach = SWEEPS - 1
    iterate[:, :reach] = source[:, 1:HALO]
    iterate[:, reach + 4 :] = source[:, HALO + CHUNK : WINDOW - 1]
    for sweep in range(1, SWEEPS):
        iterate[:, reach : reach + 4] = edges[sweep - 1]
        one = slice(sweep + 1, HALO + sweep)
        two = slice(WINDOW - HALO - sweep, WINDOW - 1 - sweep)
        sides = [
            jnp.concatenate((ref[one], ref[HALO : HALO + 2], ref[two]), axis=0)
            for ref in [scale] + [inverse.at[i] for i in range(3)] + [source.at[i] for i in range(2)]
        ]
        coupled = [couple(ops, lows, sides[0], iterate[c]) for c in range(2)]
        fresh = damped(iterate[:, 1:-1], sides[4:], sides[1:4], coupled)
        for c in range(2):
            iterate[c, :reach] = fresh[c][:reach]
            iterate[c, reach + 4 :] = fresh[c][reach + 2 :]
    last = edges.at[SWEEPS - 1]
    for xc in range(8):
        for col in range(2):
            x = 2 * xc + col
            for c in range(2):
                if x < reach:
                    tile = iterate.at[c, x]
                elif x < reach + 2:
                    tile = last.at[c, x - reach]
                else:
                    tile = iterate.at[c, x + 2]
                at = 8 + c * 4 + col * 2
                for yd in range(4):
                    out[seat(xc, yd), at : at + 2, :] = tile[2 * yd : 2 * yd + 2, :]


def backward_kernel(table, got, out):
    parts = []
    for p in range(8):
        at = (p // 4) * 8 + p % 4
        halves = [got[pl.ds(at + 4 * c, FREQS, stride=16), :] for c in range(2)]
        parts.append(jnp.concatenate(halves, axis=0))
    slices = transform(table, parts)
    for p in range(8):
        out[pl.ds(p, STEPS, stride=8), :] = slices[:, p * LANES : (p + 1) * LANES]


def unpack_kernel(got, out, flip, held, sems):
    copies = []
    for s in range(2):
        for r in range(2):
            for c in range(2):
                flip[pl.ds(c, STEPS, stride=2), :] = got[pl.ds(s * 4 + c * 2 + r, STEPS, stride=8), :]
            held[s, 0, :, r, :] = flip[...].T[:NB, :]
        copies.append(pltpu.make_async_copy(held.at[s], out.at[s], sems.at[s]))
        copies[s].start()
    for copy in copies:
        copy.wait()


def call(kernel, outs, ins, scratch=(), specs=None, name=None, params=PARAMS, out=VMEM, cost=None):
    return pl.pallas_call(
        kernel,
        out_shape=outs,
        in_specs=specs or [VMEM] * len(ins),
        out_specs=jax.tree.map(lambda _: out, outs),
        scratch_shapes=scratch,
        compiler_params=params,
        cost_estimate=cost,
        name=name,
    )(*ins)


def f32(*shape):
    return jax.ShapeDtypeStruct(shape, jnp.float32)


def exchange(blocks, axes):
    return lax.all_to_all(blocks, axes, 0, 0, tiled=True)


def moved(block, axis, by):
    count = lax.axis_size(axis)
    return lax.ppermute(block, axis, [(i, (i + by) % count) for i in range(count)])


def swapped(block, axis, bits):
    return lax.ppermute(block, axis, [(i, i ^ bits) for i in range(lax.axis_size(axis))])


def per_device(forcing, init_state, elem_scale, vol_op, face_ops):
    square = pltpu.VMEM((LANES, LANES), jnp.float32)
    window = (WINDOW, 8, LANES)
    inputs = (
        forcing.reshape(2 * NB, 2, LANES),
        init_state.reshape(1, NB, 2, LANES),
        elem_scale.reshape(1, 2, LANES),
        vol_op.reshape(1, NB, NB),
        jnp.transpose(face_ops, (1, 0, 2)),
    )
    packed, ops, lows, diag = call(
        pack_kernel,
        (
            pltpu.VMEM((STEPS * 12, LANES), jnp.float32),
            pltpu.VMEM((2 * LANES, 6 * LANES), jnp.bfloat16),
            pltpu.VMEM((LANES, 4 * LANES), jnp.bfloat16),
            pltpu.VMEM((8, LANES), jnp.float32),
        ),
        inputs,
        [pltpu.VMEM(value.shape, jnp.float32) for value in inputs]
        + [square, square, pltpu.SemaphoreType.DMA((len(inputs),))],
        [HBM] * len(inputs),
        name="pack",
        params=pltpu.CompilerParams(vmem_limit_bytes=60 * 1024 * 1024),
    )
    by_point = exchange(packed.reshape(STEPS, 3, 4, LANES), TIME).reshape(STEPS * 12, LANES)
    waves = call(forward_kernel, f32(FREQS * 24, LANES), (FORWARD, by_point), name="forward")
    got = exchange(waves.reshape(FREQS, 24, LANES), PLANE)
    both = pltpu.VMEM((2,) + window, jnp.float32)
    solved, state, scale, inverse = call(
        first_kernel,
        (f32(2, CHUNK, 8, LANES), f32(CHUNK, 8, LANES), f32(*window), f32(3, *window)),
        (SLOTS, ops, lows, diag, got),
        (both, both),
        name="first",
    )
    half = f32(2, CHUNK // 2, 8, LANES)
    state = state + swapped(state, "core", 1)
    done, left, right = call(
        between_kernel, (f32(FREQS, 8, LANES), half, half), (got, solved, state), (), [VMEM, VMEM, ANY], name="between"
    )
    near, far, across = (swapped(state, "y", bits) for bits in (1, 3, 2))
    state = ((state + near) + far) + across
    states = [state] + [swapped(state, "x", bits) for bits in (1, 3, 2)]
    left, right = call(carry_kernel, (half, half), (SLOTS, left, right, *states), name="carry")
    west = moved(right, "z", 1)
    east = moved(left, "z", -1)
    edges = call(
        inner_kernel,
        f32(SWEEPS, 2, 4, 8, LANES),
        (ops, lows, scale, inverse, left, right),
        (pltpu.VMEM((2, CHUNK, 8, LANES), jnp.float32), both),
        name="inner",
        cost=pl.CostEstimate(flops=2_000_000_000, bytes_accessed=1_000_000, transcendentals=0),
    )
    done = call(
        outer_kernel,
        f32(FREQS, 16, LANES),
        (ops, lows, scale, inverse, west, left, right, east, edges, done),
        (pltpu.VMEM((2, 2 * SWEEPS + 2, 8, LANES), jnp.float32), both),
        name="outer",
    )
    got = exchange(done, PLANE).reshape(FREQS * 16, LANES)
    slices = call(backward_kernel, f32(STEPS * 8, LANES), (BACKWARD, got), name="backward")
    by_column = exchange(slices.reshape(STEPS, 8, LANES), TIME).reshape(STEPS * 8, LANES)
    result = f32(2, 1, NB, 2, LANES)
    return call(
        unpack_kernel,
        result,
        (by_column,),
        (square, pltpu.VMEM(result.shape, jnp.float32), pltpu.SemaphoreType.DMA((2,))),
        name="unpack",
        out=ANY,
    )


def solution(mesh):
    grid = Mesh(mesh.devices.reshape(8, 4, 2, 4), ("z", "x", "core", "y"))
    return jax.shard_map(
        per_device,
        mesh=grid,
        in_specs=(
            P(None, TIME, None, "y", None),
            P(None, "y", None),
            P("y", None),
            P(),
            P(),
        ),
        out_specs=P(None, TIME, None, "y", None),
        check_vma=False,
    )
```

```python
import math

import jax
import jax.numpy as jnp
import ml_dtypes
import numpy as np
from jax import lax
from jax.experimental import pallas as pl
from jax.experimental.pallas import tpu as pltpu
from jax.sharding import Mesh
from jax.sharding import PartitionSpec as P

NB = 125
SWEEPS = 8
STEPS = 64
LANES = 128
FREQS = STEPS // 2
CHUNK = 16
WINDOW = 32
HALO = 8
ES_LANE = NB

circ_alpha = 0.01
damping = 0.7

TIME = ("z", "x", "core")
PLANE = ("core", "y", "x")


def tables():
    n = np.arange(STEPS)
    log_alpha = math.log(circ_alpha)
    grow = np.exp(n * (log_alpha / STEPS))
    forward = np.zeros((STEPS, STEPS))
    backward = np.zeros((STEPS, STEPS))
    shifts = np.zeros((FREQS, 4))
    root = math.exp(log_alpha / STEPS)
    forward[0] = 1.0
    forward[1] = (-1.0) ** n
    backward[:, 0] = 1.0
    backward[:, 1] = (-1.0) ** n
    shifts[0] = (1.0 - root, 1.0 + root, 0.0, 0.0)
    for k in range(1, FREQS):
        angle = 2.0 * math.pi * ((k * n) % STEPS) / STEPS
        forward[2 * k] = np.cos(angle)
        forward[2 * k + 1] = -np.sin(angle)
        backward[:, 2 * k] = 2.0 * np.cos(angle)
        backward[:, 2 * k + 1] = -2.0 * np.sin(angle)
        theta = 2.0 * math.pi * k / STEPS
        shifts[k, :3] = (1.0 - root * math.cos(theta), 1.0 - root * math.cos(theta), root * math.sin(theta))
    forward = forward * grow[None, :]
    backward = backward / grow[:, None] / STEPS
    carry = 0.5 * forward.sum(1) + forward[:, 0]
    last = backward[STEPS - 1]
    return tuple(a.astype(np.float32) for a in (forward, backward, shifts, carry, last))


def in_parts(table):
    high = table.astype(ml_dtypes.bfloat16)
    rest = table - high.astype(np.float32)
    middle = rest.astype(ml_dtypes.bfloat16)
    low = (rest - middle.astype(np.float32)).astype(ml_dtypes.bfloat16)
    return np.concatenate((high, high, middle, high, middle, low), axis=1)


FORWARD, BACKWARD, SHIFTS, CARRY, LAST = tables()
BY_PART = np.concatenate((np.arange(0, STEPS, 2), np.arange(1, STEPS, 2)))
FORWARD = in_parts(FORWARD[BY_PART])
BACKWARD = in_parts(BACKWARD[:, BY_PART])
SLOTS = np.concatenate((SHIFTS[:, :3], LAST.reshape(FREQS, 2), CARRY.reshape(FREQS, 2), SHIFTS[:, :1]), axis=1)
SLOTS = np.repeat(SLOTS[:, :, None], LANES, axis=2)

VMEM = pl.BlockSpec(memory_space=pltpu.VMEM)
HBM = pl.BlockSpec(memory_space=pltpu.HBM)
ANY = pl.BlockSpec(memory_space=pl.ANY)
PARAMS = pltpu.CompilerParams(vmem_limit_bytes=32 * 1024 * 1024)


def split(value):
    high = value.astype(jnp.bfloat16)
    return high, (value - high.astype(jnp.float32)).astype(jnp.bfloat16)


def transform(table, parts):
    whole = jnp.concatenate(parts, axis=1)
    high = whole.astype(jnp.bfloat16)
    middle, low = split(whole - high.astype(jnp.float32))
    stack = jnp.concatenate((high, middle, high, low, middle, high), axis=0)
    return jnp.dot(table[...], stack, preferred_element_type=jnp.float32)


def pack_kernel(
    forcing, init, scale, vol, faces, out, ops, lows, diag, value, state, elems, volume, sides, rows, flip, sems
):
    copies = [
        pltpu.make_async_copy(ref, into, sems.at[i])
        for i, (ref, into) in enumerate(
            ((vol, volume), (faces, sides), (forcing, value), (init, state), (scale, elems))
        )
    ]
    for copy in copies:
        copy.start()
    step = lax.axis_index("z") * 8 + lax.axis_index("x") * 2 + lax.axis_index("core")
    weight = jnp.where(step == 0, 1.5, 0.5).astype(jnp.float32)
    flip[...] = jnp.zeros((LANES, LANES), jnp.float32)
    rows[NB:, :] = jnp.zeros((LANES - NB, LANES), jnp.float32)
    for copy in copies[:2]:
        copy.wait()
    row = lax.broadcasted_iota(jnp.int32, (LANES, LANES), 0)
    col = lax.broadcasted_iota(jnp.int32, (LANES, LANES), 1)
    for op in range(5):
        flip[:NB, :NB] = volume[0] if op == 0 else sides[:, op - 1, :]
        square = flip[...]
        if op == 0:
            on = jnp.where(row == col, square, 0.0)
            diag[...] = jnp.broadcast_to(jnp.sum(on, axis=0, keepdims=True), (8, LANES))
            square = square - on
        square = square.T
        high, low = split(square)
        if op == 0:
            here, rest = 4 * LANES, ops.at[:LANES, 5 * LANES :]
        else:
            here = (op - 1) * LANES
            rest = lows.at[:, here : here + LANES]
        ops[:LANES, here : here + LANES] = high
        ops[LANES:, here : here + LANES] = high
        rest[...] = low
    ops[LANES:, 5 * LANES :] = jnp.zeros((LANES, LANES), jnp.bfloat16)
    for copy in copies[2:]:
        copy.wait()
    for s in (1, 0):
        for r in range(2):
            if s == 0:
                rows[:NB, :] = value[s * NB : (s + 1) * NB, r, :] + weight * state[0, :, r, :]
                rows[ES_LANE : ES_LANE + 1, :] = elems[0, r : r + 1, :]
            else:
                rows[:NB, :] = value[s * NB : (s + 1) * NB, r, :]
            flip[...] = rows[...].T
            for c in range(2):
                out[pl.ds(s * 8 + c * 2 + r, STEPS, stride=12), :] = flip[pl.ds(c, STEPS, stride=2), :]
    blank = jnp.zeros((4, LANES), jnp.float32)
    for m in range(STEPS):
        source = m - 4 if m % 8 < 4 else m + 4
        at = m * 12 + 4
        if 0 <= source < STEPS:
            out[at : at + 4, :] = out[source * 12 : source * 12 + 4, :]
        else:
            out[at : at + 4, :] = blank


def forward_kernel(table, got, out):
    lane = lax.broadcasted_iota(jnp.int32, (STEPS, LANES), 1)
    parts = [got[pl.ds(p, STEPS, stride=12), :] for p in range(12)]
    waves = transform(table, parts)
    for p in range(12):
        wave = waves[:, p * LANES : (p + 1) * LANES]
        if p < 8:
            wave = jnp.where(lane == ES_LANE, jnp.broadcast_to(parts[p][:1, :], wave.shape), wave)
        for c in range(2):
            at = c * 8 + p if p < 8 else 16 + c * 4 + p - 8
            out[pl.ds(at, FREQS, stride=24), :] = wave[c * FREQS : (c + 1) * FREQS]


def slot():
    return lax.axis_index("core") * 16 + lax.axis_index("y") * 4 + lax.axis_index("x")


def seat(xc, yd):
    return xc % 2 * 16 + yd * 4 + xc // 2


def invert(slots, diag, scale, inverse):
    mine = slots[slot()]
    shape = (WINDOW, 8, LANES)
    place = lax.axis_index("z") * CHUNK - HALO + lax.broadcasted_iota(jnp.int32, shape, 0)
    inside = jnp.logical_and(place >= 0, place < 8 * CHUNK)
    scaled = scale[...] * diag[...][None]
    im = mine[2:3][None]
    re0 = mine[0:1][None] + scaled
    re1 = mine[1:2][None] + scaled
    mod0 = jnp.where(inside, damping / (re0 * re0 + im * im), 0.0)
    mod1 = jnp.where(inside, damping / (re1 * re1 + im * im), 0.0)
    inverse[0] = re0 * mod0
    inverse[1] = re1 * mod1
    inverse[2] = im * mod0


def start(inverse, field, source, at):
    lane = lax.broadcasted_iota(jnp.int32, field.shape[1:], 2)
    g0 = jnp.where(lane < NB, field[0], 0.0)
    g1 = jnp.where(lane < NB, field[1], 0.0)
    source[0, at] = inverse[0, at] * g0 + inverse[2, at] * g1
    source[1, at] = inverse[1, at] * g1 - inverse[2, at] * g0


def couple(ops, lows, scale, field):
    wide = field.shape[0]
    inner = (wide - 2, 8, LANES)
    high, low = split(field.reshape(wide * 8, LANES))
    both = jnp.concatenate((high, low), axis=1)

    def product(left, right):
        return jnp.dot(left, right, preferred_element_type=jnp.float32)

    def columns(sums, i):
        return sums[:, i * LANES : (i + 1) * LANES].reshape(-1, 8, LANES)

    own = product(both[8:-8], ops[:, 4 * LANES :])
    along = product(both, ops[:, : 2 * LANES]) + product(high, lows[:, : 2 * LANES])
    across = product(both[8:-8], ops[:, 2 * LANES : 4 * LANES]) + product(high[8:-8], lows[:, 2 * LANES :])
    return (
        scale * (columns(own, 0) + columns(own, 1))
        + columns(along, 0)[:-2]
        + columns(along, 1)[2:]
        + pltpu.roll(columns(across, 0), 1, 1)
        + pltpu.roll(columns(across, 1), 7, 1)
    )


def damped(field, source, inverse, coupled):
    keep = 1.0 - damping
    return (
        keep * field[0] + source[0] - inverse[0] * coupled[0] - inverse[2] * coupled[1],
        keep * field[1] + source[1] - inverse[1] * coupled[1] + inverse[2] * coupled[0],
    )


def relax(ops, lows, scale, inverse, iterate, source):
    start(inverse, iterate[...], source, slice(0, WINDOW))
    iterate[...] = source[...]
    for sweep in range(1, SWEEPS):
        here = slice(sweep + 1, WINDOW - sweep - 1)
        coupled = [couple(ops, lows, scale[here], iterate[c, sweep : WINDOW - sweep]) for c in range(2)]
        fresh = damped(iterate[:, here], source[:, here], inverse[:, here], coupled)
        iterate[0, here] = fresh[0]
        iterate[1, here] = fresh[1]


def first_kernel(slots, ops, lows, diag, got, solved, state, scale, inverse, iterate, source):
    for xc in range(8):
        for yd in range(4):
            for c in range(2):
                for col in range(4):
                    w = HALO + 2 * xc + col
                    if col >= 2:
                        w = (2 * xc if xc < 4 else 16 + 2 * xc) + col - 2
                    at = c * 8 + col * 2
                    iterate[c, w, 2 * yd : 2 * yd + 2, :] = got[seat(xc, yd), at : at + 2, :]
    scale[...] = jnp.broadcast_to(iterate[0, :, :, ES_LANE : ES_LANE + 1], scale.shape)
    invert(slots, diag, scale, inverse)
    relax(ops, lows, scale, inverse, iterate, source)
    mine = slots[slot()]
    middle = iterate[:, HALO : HALO + CHUNK]
    solved[...] = middle
    state[...] = mine[3:4][None] * middle[0] + mine[4:5][None] * middle[1]


def between_kernel(got, solved, after, done, left, right):
    del after
    for c in range(2):
        for xc in range(8):
            side = left if xc < 4 else right
            for yd in range(4):
                for col in range(2):
                    rows = slice(2 * yd, 2 * yd + 2)
                    at = c * 4 + col * 2
                    done[seat(xc, yd), at : at + 2, :] = solved[c, 2 * xc + col, rows, :]
                    side[c, 2 * (xc % 4) + col, rows, :] = got[seat(xc, yd), 16 + at : 18 + at, :]


def by_side(one, two):
    even = lax.rem(lax.axis_index("z"), 2) == 0
    return jnp.where(even, two, one), jnp.where(even, one, two)


def carry_kernel(slots, left, right, state0, state1, state2, state3, near, far):
    state = (state0[...] + state1[...]) + (state2[...] + state3[...])
    mine = slots[slot()]
    for c in range(2):
        part = mine[5 + c : 6 + c][None] * state
        far[c], near[c] = by_side(right[c] + part[CHUNK // 2 :], left[c] + part[: CHUNK // 2])


def inner_kernel(ops, lows, scale, inverse, near, far, edges, iterate, source):
    middle = slice(HALO, HALO + CHUNK)
    for i, part in enumerate(by_side(near[...], far[...])):
        start(inverse, part, source, slice((i + 1) * HALO, (i + 2) * HALO))
    iterate[...] = source[:, middle]
    for sweep in range(SWEEPS):
        lo, hi = sweep, CHUNK - sweep
        if sweep:
            here = slice(HALO + lo, HALO + hi)
            coupled = [couple(ops, lows, scale[here], iterate[c, lo - 1 : hi + 1]) for c in range(2)]
            fresh = damped(iterate[:, lo:hi], source[:, here], inverse[:, here], coupled)
            iterate[0, lo:hi] = fresh[0]
            iterate[1, lo:hi] = fresh[1]
        edges[sweep, :, :2] = iterate[:, lo : lo + 2]
        edges[sweep, :, 2:] = iterate[:, hi - 2 : hi]


def outer_kernel(ops, lows, scale, inverse, near, far, beyond_near, beyond_far, edges, before, out, iterate, source):
    left, right = by_side(near[...], far[...])
    west, east = by_side(beyond_near[...], beyond_far[...])
    for i, part in enumerate((west, left, right, east)):
        start(inverse, part, source, slice(i * HALO, (i + 1) * HALO))
    out[:, :8, :] = before[...]
    reach = SWEEPS - 1
    iterate[:, :reach] = source[:, 1:HALO]
    iterate[:, reach + 4 :] = source[:, HALO + CHUNK : WINDOW - 1]
    for sweep in range(1, SWEEPS):
        iterate[:, reach : reach + 4] = edges[sweep - 1]
        one = slice(sweep + 1, HALO + sweep)
        two = slice(WINDOW - HALO - sweep, WINDOW - 1 - sweep)
        sides = [
            jnp.concatenate((ref[one], ref[HALO : HALO + 2], ref[two]), axis=0)
            for ref in [scale] + [inverse.at[i] for i in range(3)] + [source.at[i] for i in range(2)]
        ]
        coupled = [couple(ops, lows, sides[0], iterate[c]) for c in range(2)]
        fresh = damped(iterate[:, 1:-1], sides[4:], sides[1:4], coupled)
        for c in range(2):
            iterate[c, :reach] = fresh[c][:reach]
            iterate[c, reach + 4 :] = fresh[c][reach + 2 :]
    last = edges.at[SWEEPS - 1]
    for xc in range(8):
        for col in range(2):
            x = 2 * xc + col
            for c in range(2):
                if x < reach:
                    tile = iterate.at[c, x]
                elif x < reach + 2:
                    tile = last.at[c, x - reach]
                else:
                    tile = iterate.at[c, x + 2]
                at = 8 + c * 4 + col * 2
                for yd in range(4):
                    out[seat(xc, yd), at : at + 2, :] = tile[2 * yd : 2 * yd + 2, :]


def backward_kernel(table, got, out):
    parts = []
    for p in range(8):
        at = (p // 4) * 8 + p % 4
        halves = [got[pl.ds(at + 4 * c, FREQS, stride=16), :] for c in range(2)]
        parts.append(jnp.concatenate(halves, axis=0))
    slices = transform(table, parts)
    for p in range(8):
        out[pl.ds(p, STEPS, stride=8), :] = slices[:, p * LANES : (p + 1) * LANES]


def unpack_kernel(got, out, flip, held, sems):
    copies = []
    for s in range(2):
        for r in range(2):
            for c in range(2):
                flip[pl.ds(c, STEPS, stride=2), :] = got[pl.ds(s * 4 + c * 2 + r, STEPS, stride=8), :]
            held[s, 0, :, r, :] = flip[...].T[:NB, :]
        copies.append(pltpu.make_async_copy(held.at[s], out.at[s], sems.at[s]))
        copies[s].start()
    for copy in copies:
        copy.wait()


def call(kernel, outs, ins, scratch=(), specs=None, name=None, params=PARAMS, out=VMEM, cost=None):
    return pl.pallas_call(
        kernel,
        out_shape=outs,
        in_specs=specs or [VMEM] * len(ins),
        out_specs=jax.tree.map(lambda _: out, outs),
        scratch_shapes=scratch,
        compiler_params=params,
        cost_estimate=cost,
        name=name,
    )(*ins)


def f32(*shape):
    return jax.ShapeDtypeStruct(shape, jnp.float32)


def exchange(blocks, axes):
    return lax.all_to_all(blocks, axes, 0, 0, tiled=True)


def swapped(block, axis, bits):
    return lax.ppermute(block, axis, [(i, i ^ bits) for i in range(lax.axis_size(axis))])


def per_device(forcing, init_state, elem_scale, vol_op, face_ops):
    square = pltpu.VMEM((LANES, LANES), jnp.float32)
    window = (WINDOW, 8, LANES)
    inputs = (
        forcing.reshape(2 * NB, 2, LANES),
        init_state.reshape(1, NB, 2, LANES),
        elem_scale.reshape(1, 2, LANES),
        vol_op.reshape(1, NB, NB),
        jnp.transpose(face_ops, (1, 0, 2)),
    )
    packed, ops, lows, diag = call(
        pack_kernel,
        (
            pltpu.VMEM((STEPS * 12, LANES), jnp.float32),
            pltpu.VMEM((2 * LANES, 6 * LANES), jnp.bfloat16),
            pltpu.VMEM((LANES, 4 * LANES), jnp.bfloat16),
            pltpu.VMEM((8, LANES), jnp.float32),
        ),
        inputs,
        [pltpu.VMEM(value.shape, jnp.float32) for value in inputs]
        + [square, square, pltpu.SemaphoreType.DMA((len(inputs),))],
        [HBM] * len(inputs),
        name="pack",
        params=pltpu.CompilerParams(vmem_limit_bytes=60 * 1024 * 1024),
    )
    by_point = exchange(packed.reshape(STEPS, 3, 4, LANES), TIME).reshape(STEPS * 12, LANES)
    waves = call(forward_kernel, f32(FREQS * 24, LANES), (FORWARD, by_point), name="forward")
    got = exchange(waves.reshape(FREQS, 24, LANES), PLANE)
    both = pltpu.VMEM((2,) + window, jnp.float32)
    solved, state, scale, inverse = call(
        first_kernel,
        (f32(2, CHUNK, 8, LANES), f32(CHUNK, 8, LANES), f32(*window), f32(3, *window)),
        (SLOTS, ops, lows, diag, got),
        (both, both),
        name="first",
    )
    half = f32(2, CHUNK // 2, 8, LANES)
    state = state + swapped(state, "core", 1)
    done, left, right = call(
        between_kernel, (f32(FREQS, 8, LANES), half, half), (got, solved, state), (), [VMEM, VMEM, ANY], name="between"
    )
    near, far, across = (swapped(state, "y", bits) for bits in (1, 3, 2))
    state = ((state + near) + far) + across
    states = [state] + [swapped(state, "x", bits) for bits in (1, 3, 2)]
    near, far = call(carry_kernel, (half, half), (SLOTS, left, right, *states), name="carry")
    beyond_near = swapped(near, "z", 1)
    planes = lax.axis_size("z")
    other = [(z, (z + 1 if z % 2 else z - 1) % planes) for z in range(planes)]
    beyond_far = lax.ppermute(far, "z", other)
    edges = call(
        inner_kernel,
        f32(SWEEPS, 2, 4, 8, LANES),
        (ops, lows, scale, inverse, near, far),
        (pltpu.VMEM((2, CHUNK, 8, LANES), jnp.float32), both),
        name="inner",
        cost=pl.CostEstimate(flops=2_000_000_000, bytes_accessed=1_000_000, transcendentals=0),
    )
    done = call(
        outer_kernel,
        f32(FREQS, 16, LANES),
        (ops, lows, scale, inverse, near, far, beyond_near, beyond_far, edges, done),
        (pltpu.VMEM((2, 2 * SWEEPS + 2, 8, LANES), jnp.float32), both),
        name="outer",
    )
    got = exchange(done, PLANE).reshape(FREQS * 16, LANES)
    slices = call(backward_kernel, f32(STEPS * 8, LANES), (BACKWARD, got), name="backward")
    by_column = exchange(slices.reshape(STEPS, 8, LANES), TIME).reshape(STEPS * 8, LANES)
    result = f32(2, 1, NB, 2, LANES)
    return call(
        unpack_kernel,
        result,
        (by_column,),
        (square, pltpu.VMEM(result.shape, jnp.float32), pltpu.SemaphoreType.DMA((2,))),
        name="unpack",
        out=ANY,
    )


def solution(mesh):
    grid = Mesh(mesh.devices.reshape(8, 4, 2, 4), ("z", "x", "core", "y"))
    return jax.shard_map(
        per_device,
        mesh=grid,
        in_specs=(
            P(None, TIME, None, "y", None),
            P(None, "y", None),
            P("y", None),
            P(),
            P(),
        ),
        out_specs=P(None, TIME, None, "y", None),
        check_vma=False,
    )
```

```python
import math

import jax
import jax.numpy as jnp
import ml_dtypes
import numpy as np
from jax import lax
from jax.experimental import pallas as pl
from jax.experimental.pallas import tpu as pltpu
from jax.sharding import Mesh
from jax.sharding import PartitionSpec as P

NB = 125
SWEEPS = 8
STEPS = 64
LANES = 128
FREQS = STEPS // 2
CHUNK = 16
WINDOW = 32
HALO = 8
ES_LANE = NB

circ_alpha = 0.01
damping = 0.7

TIME = ("z", "x", "core")
PLANE = ("core", "y", "x")


def tables():
    n = np.arange(STEPS)
    log_alpha = math.log(circ_alpha)
    grow = np.exp(n * (log_alpha / STEPS))
    forward = np.zeros((STEPS, STEPS))
    backward = np.zeros((STEPS, STEPS))
    shifts = np.zeros((FREQS, 4))
    root = math.exp(log_alpha / STEPS)
    forward[0] = 1.0
    forward[1] = (-1.0) ** n
    backward[:, 0] = 1.0
    backward[:, 1] = (-1.0) ** n
    shifts[0] = (1.0 - root, 1.0 + root, 0.0, 0.0)
    for k in range(1, FREQS):
        angle = 2.0 * math.pi * ((k * n) % STEPS) / STEPS
        forward[2 * k] = np.cos(angle)
        forward[2 * k + 1] = -np.sin(angle)
        backward[:, 2 * k] = 2.0 * np.cos(angle)
        backward[:, 2 * k + 1] = -2.0 * np.sin(angle)
        theta = 2.0 * math.pi * k / STEPS
        shifts[k, :3] = (1.0 - root * math.cos(theta), 1.0 - root * math.cos(theta), root * math.sin(theta))
    forward = forward * grow[None, :]
    backward = backward / grow[:, None] / STEPS
    carry = 0.5 * forward.sum(1) + forward[:, 0]
    last = backward[STEPS - 1]
    return tuple(a.astype(np.float32) for a in (forward, backward, shifts, carry, last))


def in_parts(table):
    high = table.astype(ml_dtypes.bfloat16)
    rest = table - high.astype(np.float32)
    middle = rest.astype(ml_dtypes.bfloat16)
    low = (rest - middle.astype(np.float32)).astype(ml_dtypes.bfloat16)
    return np.concatenate((high, high, middle, high, middle, low), axis=1)


FORWARD, BACKWARD, SHIFTS, CARRY, LAST = tables()
BY_PART = np.concatenate((np.arange(0, STEPS, 2), np.arange(1, STEPS, 2)))
FORWARD = in_parts(FORWARD[BY_PART])
BACKWARD = in_parts(BACKWARD[:, BY_PART])
SLOTS = np.concatenate((SHIFTS[:, :3], LAST.reshape(FREQS, 2), CARRY.reshape(FREQS, 2), SHIFTS[:, :1]), axis=1)
SLOTS = np.repeat(SLOTS[:, :, None], LANES, axis=2)

VMEM = pl.BlockSpec(memory_space=pltpu.VMEM)
HBM = pl.BlockSpec(memory_space=pltpu.HBM)
ANY = pl.BlockSpec(memory_space=pl.ANY)
PARAMS = pltpu.CompilerParams(vmem_limit_bytes=32 * 1024 * 1024)


def split(value):
    high = value.astype(jnp.bfloat16)
    return high, (value - high.astype(jnp.float32)).astype(jnp.bfloat16)


def transform(table, parts):
    whole = jnp.concatenate(parts, axis=1)
    high = whole.astype(jnp.bfloat16)
    middle, low = split(whole - high.astype(jnp.float32))
    stack = jnp.concatenate((high, middle, high, low, middle, high), axis=0)
    return jnp.dot(table[...], stack, preferred_element_type=jnp.float32)


def pack_kernel(
    forcing, init, scale, vol, faces, out, ops, lows, diag, value, state, elems, volume, sides, rows, flip, sems
):
    copies = [
        pltpu.make_async_copy(ref, into, sems.at[i])
        for i, (ref, into) in enumerate(
            ((vol, volume), (faces, sides), (forcing, value), (init, state), (scale, elems))
        )
    ]
    for copy in copies:
        copy.start()
    step = lax.axis_index("z") * 8 + lax.axis_index("x") * 2 + lax.axis_index("core")
    weight = jnp.where(step == 0, 1.5, 0.5).astype(jnp.float32)
    flip[...] = jnp.zeros((LANES, LANES), jnp.float32)
    rows[NB:, :] = jnp.zeros((LANES - NB, LANES), jnp.float32)
    for copy in copies[:2]:
        copy.wait()
    row = lax.broadcasted_iota(jnp.int32, (LANES, LANES), 0)
    col = lax.broadcasted_iota(jnp.int32, (LANES, LANES), 1)
    for op in range(5):
        flip[:NB, :NB] = volume[0] if op == 0 else sides[:, op - 1, :]
        square = flip[...]
        if op == 0:
            on = jnp.where(row == col, square, 0.0)
            diag[...] = jnp.broadcast_to(jnp.sum(on, axis=0, keepdims=True), (8, LANES))
            square = square - on
        square = square.T
        high, low = split(square)
        if op == 0:
            here, rest = 4 * LANES, ops.at[:LANES, 5 * LANES :]
        else:
            here = (op - 1) * LANES
            rest = lows.at[:, here : here + LANES]
        ops[:LANES, here : here + LANES] = high
        ops[LANES:, here : here + LANES] = high
        rest[...] = low
    ops[LANES:, 5 * LANES :] = jnp.zeros((LANES, LANES), jnp.bfloat16)
    for copy in copies[2:]:
        copy.wait()
    for s in (1, 0):
        for r in range(2):
            if s == 0:
                rows[:NB, :] = value[s * NB : (s + 1) * NB, r, :] + weight * state[0, :, r, :]
                rows[ES_LANE : ES_LANE + 1, :] = elems[0, r : r + 1, :]
            else:
                rows[:NB, :] = value[s * NB : (s + 1) * NB, r, :]
            flip[...] = rows[...].T
            for c in range(2):
                out[pl.ds(s * 8 + c * 2 + r, STEPS, stride=12), :] = flip[pl.ds(c, STEPS, stride=2), :]
    blank = jnp.zeros((4, LANES), jnp.float32)
    for m in range(STEPS):
        source = m - 4 if m % 8 < 4 else m + 4
        at = m * 12 + 4
        if 0 <= source < STEPS:
            out[at : at + 4, :] = out[source * 12 : source * 12 + 4, :]
        else:
            out[at : at + 4, :] = blank


def forward_kernel(table, got, out):
    lane = lax.broadcasted_iota(jnp.int32, (STEPS, LANES), 1)
    parts = [got[pl.ds(p, STEPS, stride=12), :] for p in range(12)]
    waves = transform(table, parts)
    for p in range(12):
        wave = waves[:, p * LANES : (p + 1) * LANES]
        if p < 8:
            wave = jnp.where(lane == ES_LANE, jnp.broadcast_to(parts[p][:1, :], wave.shape), wave)
        for c in range(2):
            at = c * 8 + p if p < 8 else 16 + c * 4 + p - 8
            out[pl.ds(at, FREQS, stride=24), :] = wave[c * FREQS : (c + 1) * FREQS]


def slot():
    return lax.axis_index("core") * 16 + lax.axis_index("y") * 4 + lax.axis_index("x")


def seat(xc, yd):
    return xc % 2 * 16 + yd * 4 + xc // 2


def invert(slots, diag, scale, inverse):
    mine = slots[slot()]
    shape = (WINDOW, 8, LANES)
    place = lax.axis_index("z") * CHUNK - HALO + lax.broadcasted_iota(jnp.int32, shape, 0)
    inside = jnp.logical_and(place >= 0, place < 8 * CHUNK)
    scaled = scale[...] * diag[...][None]
    im = mine[2:3][None]
    re0 = mine[0:1][None] + scaled
    re1 = mine[1:2][None] + scaled
    mod0 = jnp.where(inside, damping / (re0 * re0 + im * im), 0.0)
    mod1 = jnp.where(inside, damping / (re1 * re1 + im * im), 0.0)
    inverse[0] = re0 * mod0
    inverse[1] = re1 * mod1
    inverse[2] = im * mod0


def start(inverse, field, source, at):
    lane = lax.broadcasted_iota(jnp.int32, field.shape[1:], 2)
    g0 = jnp.where(lane < NB, field[0], 0.0)
    g1 = jnp.where(lane < NB, field[1], 0.0)
    source[0, at] = inverse[0, at] * g0 + inverse[2, at] * g1
    source[1, at] = inverse[1, at] * g1 - inverse[2, at] * g0


def couple(ops, lows, scale, field):
    wide = field.shape[0]
    inner = (wide - 2, 8, LANES)
    high, low = split(field.reshape(wide * 8, LANES))
    both = jnp.concatenate((high, low), axis=1)

    def product(left, right):
        return jnp.dot(left, right, preferred_element_type=jnp.float32)

    def columns(sums, i):
        return sums[:, i * LANES : (i + 1) * LANES].reshape(-1, 8, LANES)

    own = product(both[8:-8], ops[:, 4 * LANES :])
    along = product(both, ops[:, : 2 * LANES]) + product(high, lows[:, : 2 * LANES])
    across = product(both[8:-8], ops[:, 2 * LANES : 4 * LANES]) + product(high[8:-8], lows[:, 2 * LANES :])
    return (
        scale * (columns(own, 0) + columns(own, 1))
        + columns(along, 0)[:-2]
        + columns(along, 1)[2:]
        + pltpu.roll(columns(across, 0), 1, 1)
        + pltpu.roll(columns(across, 1), 7, 1)
    )


def damped(field, source, inverse, coupled):
    keep = 1.0 - damping
    return (
        keep * field[0] + source[0] - inverse[0] * coupled[0] - inverse[2] * coupled[1],
        keep * field[1] + source[1] - inverse[1] * coupled[1] + inverse[2] * coupled[0],
    )


def relax(ops, lows, scale, inverse, iterate, source):
    start(inverse, iterate[...], source, slice(0, WINDOW))
    iterate[...] = source[...]
    for sweep in range(1, SWEEPS):
        here = slice(sweep + 1, WINDOW - sweep - 1)
        coupled = [couple(ops, lows, scale[here], iterate[c, sweep : WINDOW - sweep]) for c in range(2)]
        fresh = damped(iterate[:, here], source[:, here], inverse[:, here], coupled)
        iterate[0, here] = fresh[0]
        iterate[1, here] = fresh[1]


def first_kernel(slots, ops, lows, diag, got, solved, state, scale, inverse, iterate, source):
    for xc in range(8):
        for yd in range(4):
            for c in range(2):
                for col in range(4):
                    w = HALO + 2 * xc + col
                    if col >= 2:
                        w = (2 * xc if xc < 4 else 16 + 2 * xc) + col - 2
                    at = c * 8 + col * 2
                    iterate[c, w, 2 * yd : 2 * yd + 2, :] = got[seat(xc, yd), at : at + 2, :]
    scale[...] = jnp.broadcast_to(iterate[0, :, :, ES_LANE : ES_LANE + 1], scale.shape)
    invert(slots, diag, scale, inverse)
    relax(ops, lows, scale, inverse, iterate, source)
    mine = slots[slot()]
    middle = iterate[:, HALO : HALO + CHUNK]
    solved[...] = middle
    state[...] = mine[3:4][None] * middle[0] + mine[4:5][None] * middle[1]


def between_kernel(got, solved, after, done, left, right):
    del after
    for c in range(2):
        for xc in range(8):
            side = left if xc < 4 else right
            for yd in range(4):
                for col in range(2):
                    rows = slice(2 * yd, 2 * yd + 2)
                    at = c * 4 + col * 2
                    done[seat(xc, yd), at : at + 2, :] = solved[c, 2 * xc + col, rows, :]
                    side[c, 2 * (xc % 4) + col, rows, :] = got[seat(xc, yd), 16 + at : 18 + at, :]


def by_side(one, two):
    even = lax.rem(lax.axis_index("z"), 2) == 0
    return jnp.where(even, two, one), jnp.where(even, one, two)


def carry_kernel(slots, left, right, state0, state1, state2, state3, near, far):
    state = (state0[...] + state1[...]) + (state2[...] + state3[...])
    mine = slots[slot()]
    for c in range(2):
        part = mine[5 + c : 6 + c][None] * state
        far[c], near[c] = by_side(right[c] + part[CHUNK // 2 :], left[c] + part[: CHUNK // 2])


def second_kernel(ops, lows, scale, inverse, near, far, beyond_near, beyond_far, before, out, iterate, source):
    left, right = by_side(near[...], far[...])
    west, east = by_side(beyond_near[...], beyond_far[...])
    for i, part in enumerate((west, left, right, east)):
        iterate[:, i * HALO : (i + 1) * HALO] = part
    out[:, :8, :] = before[...]
    relax(ops, lows, scale, inverse, iterate, source)
    for xc in range(8):
        for yd in range(4):
            for c in range(2):
                for col in range(2):
                    at = 8 + c * 4 + col * 2
                    out[seat(xc, yd), at : at + 2, :] = iterate[c, HALO + 2 * xc + col, 2 * yd : 2 * yd + 2, :]


def backward_kernel(table, got, out):
    parts = []
    for p in range(8):
        at = (p // 4) * 8 + p % 4
        halves = [got[pl.ds(at + 4 * c, FREQS, stride=16), :] for c in range(2)]
        parts.append(jnp.concatenate(halves, axis=0))
    slices = transform(table, parts)
    for p in range(8):
        out[pl.ds(p, STEPS, stride=8), :] = slices[:, p * LANES : (p + 1) * LANES]


def unpack_kernel(got, out, flip, held, sems):
    copies = []
    for s in range(2):
        for r in range(2):
            for c in range(2):
                flip[pl.ds(c, STEPS, stride=2), :] = got[pl.ds(s * 4 + c * 2 + r, STEPS, stride=8), :]
            held[s, 0, :, r, :] = flip[...].T[:NB, :]
        copies.append(pltpu.make_async_copy(held.at[s], out.at[s], sems.at[s]))
        copies[s].start()
    for copy in copies:
        copy.wait()


def call(kernel, outs, ins, scratch=(), specs=None, name=None, params=PARAMS, out=VMEM):
    return pl.pallas_call(
        kernel,
        out_shape=outs,
        in_specs=specs or [VMEM] * len(ins),
        out_specs=jax.tree.map(lambda _: out, outs),
        scratch_shapes=scratch,
        compiler_params=params,
        name=name,
    )(*ins)


def f32(*shape):
    return jax.ShapeDtypeStruct(shape, jnp.float32)


def exchange(blocks, axes):
    return lax.all_to_all(blocks, axes, 0, 0, tiled=True)


def swapped(block, axis, bits):
    return lax.ppermute(block, axis, [(i, i ^ bits) for i in range(lax.axis_size(axis))])


def per_device(forcing, init_state, elem_scale, vol_op, face_ops):
    square = pltpu.VMEM((LANES, LANES), jnp.float32)
    window = (WINDOW, 8, LANES)
    inputs = (
        forcing.reshape(2 * NB, 2, LANES),
        init_state.reshape(1, NB, 2, LANES),
        elem_scale.reshape(1, 2, LANES),
        vol_op.reshape(1, NB, NB),
        jnp.transpose(face_ops, (1, 0, 2)),
    )
    packed, ops, lows, diag = call(
        pack_kernel,
        (
            pltpu.VMEM((STEPS * 12, LANES), jnp.float32),
            pltpu.VMEM((2 * LANES, 6 * LANES), jnp.bfloat16),
            pltpu.VMEM((LANES, 4 * LANES), jnp.bfloat16),
            pltpu.VMEM((8, LANES), jnp.float32),
        ),
        inputs,
        [pltpu.VMEM(value.shape, jnp.float32) for value in inputs]
        + [square, square, pltpu.SemaphoreType.DMA((len(inputs),))],
        [HBM] * len(inputs),
        name="pack",
        params=pltpu.CompilerParams(vmem_limit_bytes=60 * 1024 * 1024),
    )
    by_point = exchange(packed.reshape(STEPS, 3, 4, LANES), TIME).reshape(STEPS * 12, LANES)
    waves = call(forward_kernel, f32(FREQS * 24, LANES), (FORWARD, by_point), name="forward")
    got = exchange(waves.reshape(FREQS, 24, LANES), PLANE)
    both = pltpu.VMEM((2,) + window, jnp.float32)
    solved, state, scale, inverse = call(
        first_kernel,
        (f32(2, CHUNK, 8, LANES), f32(CHUNK, 8, LANES), f32(*window), f32(3, *window)),
        (SLOTS, ops, lows, diag, got),
        (both, both),
        name="first",
    )
    half = f32(2, CHUNK // 2, 8, LANES)
    state = state + swapped(state, "core", 1)
    done, left, right = call(
        between_kernel, (f32(FREQS, 8, LANES), half, half), (got, solved, state), (), [VMEM, VMEM, ANY], name="between"
    )
    near, far, across = (swapped(state, "y", bits) for bits in (1, 3, 2))
    state = ((state + near) + far) + across
    states = [state] + [swapped(state, "x", bits) for bits in (1, 3, 2)]
    near, far = call(carry_kernel, (half, half), (SLOTS, left, right, *states), name="carry")
    beyond_near = swapped(near, "z", 1)
    planes = lax.axis_size("z")
    other = [(z, (z + 1 if z % 2 else z - 1) % planes) for z in range(planes)]
    beyond_far = lax.ppermute(far, "z", other)
    done = call(
        second_kernel,
        f32(FREQS, 16, LANES),
        (ops, lows, scale, inverse, near, far, beyond_near, beyond_far, done),
        (both, both),
        name="second",
    )
    got = exchange(done, PLANE).reshape(FREQS * 16, LANES)
    slices = call(backward_kernel, f32(STEPS * 8, LANES), (BACKWARD, got), name="backward")
    by_column = exchange(slices.reshape(STEPS, 8, LANES), TIME).reshape(STEPS * 8, LANES)
    result = f32(2, 1, NB, 2, LANES)
    return call(
        unpack_kernel,
        result,
        (by_column,),
        (square, pltpu.VMEM(result.shape, jnp.float32), pltpu.SemaphoreType.DMA((2,))),
        name="unpack",
        out=ANY,
    )


def solution(mesh):
    grid = Mesh(mesh.devices.reshape(8, 4, 2, 4), ("z", "x", "core", "y"))
    return jax.shard_map(
        per_device,
        mesh=grid,
        in_specs=(
            P(None, TIME, None, "y", None),
            P(None, "y", None),
            P("y", None),
            P(),
            P(),
        ),
        out_specs=P(None, TIME, None, "y", None),
        check_vma=False,
    )
```

```python
import math

import jax
import jax.numpy as jnp
import ml_dtypes
import numpy as np
from jax import lax
from jax.experimental import pallas as pl
from jax.experimental.pallas import tpu as pltpu
from jax.sharding import Mesh
from jax.sharding import PartitionSpec as P

NB = 125
SWEEPS = 8
STEPS = 64
LANES = 128
FREQS = STEPS // 2
CHUNK = 16
WINDOW = 32
HALO = 8
ES_LANE = NB

circ_alpha = 0.01
damping = 0.7

TIME = ("z", "x", "core")
PLANE = ("core", "y", "x")


def tables():
    n = np.arange(STEPS)
    log_alpha = math.log(circ_alpha)
    grow = np.exp(n * (log_alpha / STEPS))
    forward = np.zeros((STEPS, STEPS))
    backward = np.zeros((STEPS, STEPS))
    shifts = np.zeros((FREQS, 4))
    root = math.exp(log_alpha / STEPS)
    forward[0] = 1.0
    forward[1] = (-1.0) ** n
    backward[:, 0] = 1.0
    backward[:, 1] = (-1.0) ** n
    shifts[0] = (1.0 - root, 1.0 + root, 0.0, 0.0)
    for k in range(1, FREQS):
        angle = 2.0 * math.pi * ((k * n) % STEPS) / STEPS
        forward[2 * k] = np.cos(angle)
        forward[2 * k + 1] = -np.sin(angle)
        backward[:, 2 * k] = 2.0 * np.cos(angle)
        backward[:, 2 * k + 1] = -2.0 * np.sin(angle)
        theta = 2.0 * math.pi * k / STEPS
        shifts[k, :3] = (1.0 - root * math.cos(theta), 1.0 - root * math.cos(theta), root * math.sin(theta))
    forward = forward * grow[None, :]
    backward = backward / grow[:, None] / STEPS
    carry = 0.5 * forward.sum(1) + forward[:, 0]
    last = backward[STEPS - 1]
    return tuple(a.astype(np.float32) for a in (forward, backward, shifts, carry, last))


def in_parts(table):
    high = table.astype(ml_dtypes.bfloat16)
    rest = table - high.astype(np.float32)
    middle = rest.astype(ml_dtypes.bfloat16)
    low = (rest - middle.astype(np.float32)).astype(ml_dtypes.bfloat16)
    return np.concatenate((high, high, middle, high, middle, low), axis=1)


FORWARD, BACKWARD, SHIFTS, CARRY, LAST = tables()
BY_PART = np.concatenate((np.arange(0, STEPS, 2), np.arange(1, STEPS, 2)))
FORWARD = in_parts(FORWARD[BY_PART])
BACKWARD = in_parts(BACKWARD[:, BY_PART])
SLOTS = np.concatenate((SHIFTS[:, :3], LAST.reshape(FREQS, 2), CARRY.reshape(FREQS, 2), SHIFTS[:, :1]), axis=1)
SLOTS = np.repeat(SLOTS[:, :, None], LANES, axis=2)

VMEM = pl.BlockSpec(memory_space=pltpu.VMEM)
HBM = pl.BlockSpec(memory_space=pltpu.HBM)
ANY = pl.BlockSpec(memory_space=pl.ANY)
PARAMS = pltpu.CompilerParams(vmem_limit_bytes=32 * 1024 * 1024)


def split(value):
    high = value.astype(jnp.bfloat16)
    return high, (value - high.astype(jnp.float32)).astype(jnp.bfloat16)


def transform(table, parts):
    whole = jnp.concatenate(parts, axis=1)
    high = whole.astype(jnp.bfloat16)
    middle, low = split(whole - high.astype(jnp.float32))
    stack = jnp.concatenate((high, middle, high, low, middle, high), axis=0)
    return jnp.dot(table[...], stack, preferred_element_type=jnp.float32)


def pack_kernel(
    forcing, init, scale, vol, faces, out, ops, lows, diag, value, state, elems, volume, sides, rows, flip, sems
):
    copies = [
        pltpu.make_async_copy(ref, into, sems.at[i])
        for i, (ref, into) in enumerate(
            ((vol, volume), (faces, sides), (forcing, value), (init, state), (scale, elems))
        )
    ]
    for copy in copies:
        copy.start()
    step = lax.axis_index("z") * 8 + lax.axis_index("x") * 2 + lax.axis_index("core")
    weight = jnp.where(step == 0, 1.5, 0.5).astype(jnp.float32)
    flip[...] = jnp.zeros((LANES, LANES), jnp.float32)
    rows[NB:, :] = jnp.zeros((LANES - NB, LANES), jnp.float32)
    for copy in copies[:2]:
        copy.wait()
    row = lax.broadcasted_iota(jnp.int32, (LANES, LANES), 0)
    col = lax.broadcasted_iota(jnp.int32, (LANES, LANES), 1)
    for op in range(5):
        flip[:NB, :NB] = volume[0] if op == 0 else sides[:, op - 1, :]
        square = flip[...]
        if op == 0:
            on = jnp.where(row == col, square, 0.0)
            diag[...] = jnp.broadcast_to(jnp.sum(on, axis=0, keepdims=True), (8, LANES))
            square = square - on
        square = square.T
        high, low = split(square)
        if op == 0:
            here, rest = 4 * LANES, ops.at[:LANES, 5 * LANES :]
        else:
            here = (op - 1) * LANES
            rest = lows.at[:, here : here + LANES]
        ops[:LANES, here : here + LANES] = high
        ops[LANES:, here : here + LANES] = high
        rest[...] = low
    ops[LANES:, 5 * LANES :] = jnp.zeros((LANES, LANES), jnp.bfloat16)
    for copy in copies[2:]:
        copy.wait()
    for s in (1, 0):
        for r in range(2):
            if s == 0:
                rows[:NB, :] = value[s * NB : (s + 1) * NB, r, :] + weight * state[0, :, r, :]
                rows[ES_LANE : ES_LANE + 1, :] = elems[0, r : r + 1, :]
            else:
                rows[:NB, :] = value[s * NB : (s + 1) * NB, r, :]
            flip[...] = rows[...].T
            for c in range(2):
                out[pl.ds(s * 8 + c * 2 + r, STEPS, stride=12), :] = flip[pl.ds(c, STEPS, stride=2), :]
    blank = jnp.zeros((4, LANES), jnp.float32)
    for m in range(STEPS):
        source = m - 4 if m % 8 < 4 else m + 4
        at = m * 12 + 4
        if 0 <= source < STEPS:
            out[at : at + 4, :] = out[source * 12 : source * 12 + 4, :]
        else:
            out[at : at + 4, :] = blank


def forward_kernel(table, got, out):
    lane = lax.broadcasted_iota(jnp.int32, (STEPS, LANES), 1)
    parts = [got[pl.ds(p, STEPS, stride=12), :] for p in range(12)]
    waves = transform(table, parts)
    for p in range(12):
        wave = waves[:, p * LANES : (p + 1) * LANES]
        if p < 8:
            wave = jnp.where(lane == ES_LANE, jnp.broadcast_to(parts[p][:1, :], wave.shape), wave)
        for c in range(2):
            at = c * 8 + p if p < 8 else 16 + c * 4 + p - 8
            out[pl.ds(at, FREQS, stride=24), :] = wave[c * FREQS : (c + 1) * FREQS]


def slot():
    return lax.axis_index("core") * 16 + lax.axis_index("y") * 4 + lax.axis_index("x")


def seat(xc, yd):
    return xc % 2 * 16 + yd * 4 + xc // 2


def invert(slots, diag, scale, inverse):
    mine = slots[slot()]
    shape = (WINDOW, 8, LANES)
    place = lax.axis_index("z") * CHUNK - HALO + lax.broadcasted_iota(jnp.int32, shape, 0)
    inside = jnp.logical_and(place >= 0, place < 8 * CHUNK)
    scaled = scale[...] * diag[...][None]
    im = mine[2:3][None]
    re0 = mine[0:1][None] + scaled
    re1 = mine[1:2][None] + scaled
    mod0 = jnp.where(inside, damping / (re0 * re0 + im * im), 0.0)
    mod1 = jnp.where(inside, damping / (re1 * re1 + im * im), 0.0)
    inverse[0] = re0 * mod0
    inverse[1] = re1 * mod1
    inverse[2] = im * mod0


def start(inverse, field, source, at):
    lane = lax.broadcasted_iota(jnp.int32, field.shape[1:], 2)
    g0 = jnp.where(lane < NB, field[0], 0.0)
    g1 = jnp.where(lane < NB, field[1], 0.0)
    source[0, at] = inverse[0, at] * g0 + inverse[2, at] * g1
    source[1, at] = inverse[1, at] * g1 - inverse[2, at] * g0


def couple(ops, lows, scale, field):
    wide = field.shape[0]
    inner = (wide - 2, 8, LANES)
    high, low = split(field.reshape(wide * 8, LANES))
    both = jnp.concatenate((high, low), axis=1)

    def product(left, right):
        return jnp.dot(left, right, preferred_element_type=jnp.float32)

    def columns(sums, i):
        return sums[:, i * LANES : (i + 1) * LANES].reshape(-1, 8, LANES)

    own = product(both[8:-8], ops[:, 4 * LANES :])
    along = product(both, ops[:, : 2 * LANES]) + product(high, lows[:, : 2 * LANES])
    across = product(both[8:-8], ops[:, 2 * LANES : 4 * LANES]) + product(high[8:-8], lows[:, 2 * LANES :])
    return (
        scale * (columns(own, 0) + columns(own, 1))
        + columns(along, 0)[:-2]
        + columns(along, 1)[2:]
        + pltpu.roll(columns(across, 0), 1, 1)
        + pltpu.roll(columns(across, 1), 7, 1)
    )


def damped(field, source, inverse, coupled):
    keep = 1.0 - damping
    return (
        keep * field[0] + source[0] - inverse[0] * coupled[0] - inverse[2] * coupled[1],
        keep * field[1] + source[1] - inverse[1] * coupled[1] + inverse[2] * coupled[0],
    )


def relax(ops, lows, scale, inverse, iterate, source):
    start(inverse, iterate[...], source, slice(0, WINDOW))
    iterate[...] = source[...]
    for sweep in range(1, SWEEPS):
        here = slice(sweep + 1, WINDOW - sweep - 1)
        coupled = [couple(ops, lows, scale[here], iterate[c, sweep : WINDOW - sweep]) for c in range(2)]
        fresh = damped(iterate[:, here], source[:, here], inverse[:, here], coupled)
        iterate[0, here] = fresh[0]
        iterate[1, here] = fresh[1]


def first_kernel(slots, ops, lows, diag, got, solved, state, scale, inverse, iterate, source):
    for xc in range(8):
        for yd in range(4):
            for c in range(2):
                for col in range(4):
                    w = HALO + 2 * xc + col
                    if col >= 2:
                        w = (2 * xc if xc < 4 else 16 + 2 * xc) + col - 2
                    at = c * 8 + col * 2
                    iterate[c, w, 2 * yd : 2 * yd + 2, :] = got[seat(xc, yd), at : at + 2, :]
    scale[...] = jnp.broadcast_to(iterate[0, :, :, ES_LANE : ES_LANE + 1], scale.shape)
    invert(slots, diag, scale, inverse)
    relax(ops, lows, scale, inverse, iterate, source)
    mine = slots[slot()]
    middle = iterate[:, HALO : HALO + CHUNK]
    solved[...] = middle
    state[...] = mine[3:4][None] * middle[0] + mine[4:5][None] * middle[1]


def between_kernel(got, solved, after, done, left, right):
    del after
    for c in range(2):
        for xc in range(8):
            side = left if xc < 4 else right
            for yd in range(4):
                for col in range(2):
                    rows = slice(2 * yd, 2 * yd + 2)
                    at = c * 4 + col * 2
                    done[seat(xc, yd), at : at + 2, :] = solved[c, 2 * xc + col, rows, :]
                    side[c, 2 * (xc % 4) + col, rows, :] = got[seat(xc, yd), 16 + at : 18 + at, :]


def by_side(one, two):
    even = lax.rem(lax.axis_index("z"), 2) == 0
    return jnp.where(even, two, one), jnp.where(even, one, two)


def carry_kernel(slots, left, right, state0, state1, state2, state3, far, near):
    state = (state0[...] + state1[...]) + (state2[...] + state3[...])
    mine = slots[slot()]
    for c in range(2):
        part = mine[5 + c : 6 + c][None] * state
        far[c], near[c] = by_side(right[c] + part[CHUNK // 2 :], left[c] + part[: CHUNK // 2])


def inner_kernel(ops, lows, scale, inverse, far, near, edges, iterate, source):
    middle = slice(HALO, HALO + CHUNK)
    for i, part in enumerate(by_side(near[...], far[...])):
        start(inverse, part, source, slice((i + 1) * HALO, (i + 2) * HALO))
    iterate[...] = source[:, middle]
    for sweep in range(SWEEPS):
        lo, hi = sweep, CHUNK - sweep
        if sweep:
            here = slice(HALO + lo, HALO + hi)
            coupled = [couple(ops, lows, scale[here], iterate[c, lo - 1 : hi + 1]) for c in range(2)]
            fresh = damped(iterate[:, lo:hi], source[:, here], inverse[:, here], coupled)
            iterate[0, lo:hi] = fresh[0]
            iterate[1, lo:hi] = fresh[1]
        edges[sweep, :, :2] = iterate[:, lo : lo + 2]
        edges[sweep, :, 2:] = iterate[:, hi - 2 : hi]


def outer_kernel(ops, lows, scale, inverse, far, near, beyond_far, beyond_near, edges, before, out, iterate, source):
    left, right = by_side(near[...], far[...])
    west, east = by_side(beyond_near[...], beyond_far[...])
    for i, part in enumerate((west, left, right, east)):
        start(inverse, part, source, slice(i * HALO, (i + 1) * HALO))
    out[:, :8, :] = before[...]
    reach = SWEEPS - 1
    iterate[:, :reach] = source[:, 1:HALO]
    iterate[:, reach + 4 :] = source[:, HALO + CHUNK : WINDOW - 1]
    for sweep in range(1, SWEEPS):
        iterate[:, reach : reach + 4] = edges[sweep - 1]
        one = slice(sweep + 1, HALO + sweep)
        two = slice(WINDOW - HALO - sweep, WINDOW - 1 - sweep)
        sides = [
            jnp.concatenate((ref[one], ref[HALO : HALO + 2], ref[two]), axis=0)
            for ref in [scale] + [inverse.at[i] for i in range(3)] + [source.at[i] for i in range(2)]
        ]
        coupled = [couple(ops, lows, sides[0], iterate[c]) for c in range(2)]
        fresh = damped(iterate[:, 1:-1], sides[4:], sides[1:4], coupled)
        for c in range(2):
            iterate[c, :reach] = fresh[c][:reach]
            iterate[c, reach + 4 :] = fresh[c][reach + 2 :]
    last = edges.at[SWEEPS - 1]
    for xc in range(8):
        for col in range(2):
            x = 2 * xc + col
            for c in range(2):
                if x < reach:
                    tile = iterate.at[c, x]
                elif x < reach + 2:
                    tile = last.at[c, x - reach]
                else:
                    tile = iterate.at[c, x + 2]
                at = 8 + c * 4 + col * 2
                for yd in range(4):
                    out[seat(xc, yd), at : at + 2, :] = tile[2 * yd : 2 * yd + 2, :]


def backward_kernel(table, got, out):
    parts = []
    for p in range(8):
        at = (p // 4) * 8 + p % 4
        halves = [got[pl.ds(at + 4 * c, FREQS, stride=16), :] for c in range(2)]
        parts.append(jnp.concatenate(halves, axis=0))
    slices = transform(table, parts)
    for p in range(8):
        out[pl.ds(p, STEPS, stride=8), :] = slices[:, p * LANES : (p + 1) * LANES]


def unpack_kernel(got, out, flip, held, sems):
    copies = []
    for s in range(2):
        for r in range(2):
            for c in range(2):
                flip[pl.ds(c, STEPS, stride=2), :] = got[pl.ds(s * 4 + c * 2 + r, STEPS, stride=8), :]
            held[s, 0, :, r, :] = flip[...].T[:NB, :]
        copies.append(pltpu.make_async_copy(held.at[s], out.at[s], sems.at[s]))
        copies[s].start()
    for copy in copies:
        copy.wait()


def call(kernel, outs, ins, scratch=(), specs=None, name=None, params=PARAMS, out=VMEM, cost=None):
    return pl.pallas_call(
        kernel,
        out_shape=outs,
        in_specs=specs or [VMEM] * len(ins),
        out_specs=jax.tree.map(lambda _: out, outs),
        scratch_shapes=scratch,
        compiler_params=params,
        cost_estimate=cost,
        name=name,
    )(*ins)


def f32(*shape):
    return jax.ShapeDtypeStruct(shape, jnp.float32)


def exchange(blocks, axes):
    return lax.all_to_all(blocks, axes, 0, 0, tiled=True)


def swapped(block, axis, bits):
    return lax.ppermute(block, axis, [(i, i ^ bits) for i in range(lax.axis_size(axis))])


def per_device(forcing, init_state, elem_scale, vol_op, face_ops):
    square = pltpu.VMEM((LANES, LANES), jnp.float32)
    window = (WINDOW, 8, LANES)
    inputs = (
        forcing.reshape(2 * NB, 2, LANES),
        init_state.reshape(1, NB, 2, LANES),
        elem_scale.reshape(1, 2, LANES),
        vol_op.reshape(1, NB, NB),
        jnp.transpose(face_ops, (1, 0, 2)),
    )
    packed, ops, lows, diag = call(
        pack_kernel,
        (
            pltpu.VMEM((STEPS * 12, LANES), jnp.float32),
            pltpu.VMEM((2 * LANES, 6 * LANES), jnp.bfloat16),
            pltpu.VMEM((LANES, 4 * LANES), jnp.bfloat16),
            pltpu.VMEM((8, LANES), jnp.float32),
        ),
        inputs,
        [pltpu.VMEM(value.shape, jnp.float32) for value in inputs]
        + [square, square, pltpu.SemaphoreType.DMA((len(inputs),))],
        [HBM] * len(inputs),
        name="pack",
        params=pltpu.CompilerParams(vmem_limit_bytes=60 * 1024 * 1024),
    )
    by_point = exchange(packed.reshape(STEPS, 3, 4, LANES), TIME).reshape(STEPS * 12, LANES)
    waves = call(forward_kernel, f32(FREQS * 24, LANES), (FORWARD, by_point), name="forward")
    got = exchange(waves.reshape(FREQS, 24, LANES), PLANE)
    both = pltpu.VMEM((2,) + window, jnp.float32)
    solved, state, scale, inverse = call(
        first_kernel,
        (f32(2, CHUNK, 8, LANES), f32(CHUNK, 8, LANES), f32(*window), f32(3, *window)),
        (SLOTS, ops, lows, diag, got),
        (both, both),
        name="first",
    )
    half = f32(2, CHUNK // 2, 8, LANES)
    state = state + swapped(state, "core", 1)
    done, left, right = call(
        between_kernel, (f32(FREQS, 8, LANES), half, half), (got, solved, state), (), [VMEM, VMEM, ANY], name="between"
    )
    near, far, across = (swapped(state, "y", bits) for bits in (1, 3, 2))
    state = ((state + near) + far) + across
    states = [state] + [swapped(state, "x", bits) for bits in (1, 3, 2)]
    far, near = call(carry_kernel, (half, half), (SLOTS, left, right, *states), name="carry")
    planes = lax.axis_size("z")
    other = [(z, (z + 1 if z % 2 else z - 1) % planes) for z in range(planes)]
    beyond_far = lax.ppermute(far, "z", other)
    beyond_near = swapped(near, "z", 1)
    edges = call(
        inner_kernel,
        f32(SWEEPS, 2, 4, 8, LANES),
        (ops, lows, scale, inverse, far, near),
        (pltpu.VMEM((2, CHUNK, 8, LANES), jnp.float32), both),
        name="inner",
        cost=pl.CostEstimate(flops=2_000_000_000, bytes_accessed=1_000_000, transcendentals=0),
    )
    done = call(
        outer_kernel,
        f32(FREQS, 16, LANES),
        (ops, lows, scale, inverse, far, near, beyond_far, beyond_near, edges, done),
        (pltpu.VMEM((2, 2 * SWEEPS + 2, 8, LANES), jnp.float32), both),
        name="outer",
    )
    got = exchange(done, PLANE).reshape(FREQS * 16, LANES)
    slices = call(backward_kernel, f32(STEPS * 8, LANES), (BACKWARD, got), name="backward")
    by_column = exchange(slices.reshape(STEPS, 8, LANES), TIME).reshape(STEPS * 8, LANES)
    result = f32(2, 1, NB, 2, LANES)
    return call(
        unpack_kernel,
        result,
        (by_column,),
        (square, pltpu.VMEM(result.shape, jnp.float32), pltpu.SemaphoreType.DMA((2,))),
        name="unpack",
        out=ANY,
    )


def solution(mesh):
    grid = Mesh(mesh.devices.reshape(8, 4, 2, 4), ("z", "x", "core", "y"))
    return jax.shard_map(
        per_device,
        mesh=grid,
        in_specs=(
            P(None, TIME, None, "y", None),
            P(None, "y", None),
            P("y", None),
            P(),
            P(),
        ),
        out_specs=P(None, TIME, None, "y", None),
        check_vma=False,
    )
```

```python
import math

import jax
import jax.numpy as jnp
import ml_dtypes
import numpy as np
from jax import lax
from jax.experimental import pallas as pl
from jax.experimental.pallas import tpu as pltpu
from jax.sharding import Mesh
from jax.sharding import PartitionSpec as P

NB = 125
SWEEPS = 8
STEPS = 64
LANES = 128
FREQS = STEPS // 2
CHUNK = 16
WINDOW = 32
HALO = 8
INNER = 4
ES_LANE = NB

circ_alpha = 0.01
damping = 0.7

TIME = ("z", "x", "core")
PLANE = ("core", "y", "x")


def tables():
    n = np.arange(STEPS)
    log_alpha = math.log(circ_alpha)
    grow = np.exp(n * (log_alpha / STEPS))
    forward = np.zeros((STEPS, STEPS))
    backward = np.zeros((STEPS, STEPS))
    shifts = np.zeros((FREQS, 4))
    root = math.exp(log_alpha / STEPS)
    forward[0] = 1.0
    forward[1] = (-1.0) ** n
    backward[:, 0] = 1.0
    backward[:, 1] = (-1.0) ** n
    shifts[0] = (1.0 - root, 1.0 + root, 0.0, 0.0)
    for k in range(1, FREQS):
        angle = 2.0 * math.pi * ((k * n) % STEPS) / STEPS
        forward[2 * k] = np.cos(angle)
        forward[2 * k + 1] = -np.sin(angle)
        backward[:, 2 * k] = 2.0 * np.cos(angle)
        backward[:, 2 * k + 1] = -2.0 * np.sin(angle)
        theta = 2.0 * math.pi * k / STEPS
        shifts[k, :3] = (1.0 - root * math.cos(theta), 1.0 - root * math.cos(theta), root * math.sin(theta))
    forward = forward * grow[None, :]
    backward = backward / grow[:, None] / STEPS
    carry = 0.5 * forward.sum(1) + forward[:, 0]
    last = backward[STEPS - 1]
    return tuple(a.astype(np.float32) for a in (forward, backward, shifts, carry, last))


def in_parts(table):
    high = table.astype(ml_dtypes.bfloat16)
    rest = table - high.astype(np.float32)
    middle = rest.astype(ml_dtypes.bfloat16)
    low = (rest - middle.astype(np.float32)).astype(ml_dtypes.bfloat16)
    return np.concatenate((high, high, middle, high, middle, low), axis=1)


FORWARD, BACKWARD, SHIFTS, CARRY, LAST = tables()
BY_PART = np.concatenate((np.arange(0, STEPS, 2), np.arange(1, STEPS, 2)))
FORWARD = in_parts(FORWARD[BY_PART])
BACKWARD = in_parts(BACKWARD[:, BY_PART])
SLOTS = np.concatenate((SHIFTS[:, :3], LAST.reshape(FREQS, 2), CARRY.reshape(FREQS, 2), SHIFTS[:, :1]), axis=1)
SLOTS = np.repeat(SLOTS[:, :, None], LANES, axis=2)

VMEM = pl.BlockSpec(memory_space=pltpu.VMEM)
HBM = pl.BlockSpec(memory_space=pltpu.HBM)
ANY = pl.BlockSpec(memory_space=pl.ANY)
PARAMS = pltpu.CompilerParams(vmem_limit_bytes=32 * 1024 * 1024)


def split(value):
    high = value.astype(jnp.bfloat16)
    return high, (value - high.astype(jnp.float32)).astype(jnp.bfloat16)


def transform(table, parts):
    whole = jnp.concatenate(parts, axis=1)
    high = whole.astype(jnp.bfloat16)
    middle, low = split(whole - high.astype(jnp.float32))
    stack = jnp.concatenate((high, middle, high, low, middle, high), axis=0)
    return jnp.dot(table[...], stack, preferred_element_type=jnp.float32)


def pack_kernel(
    forcing, init, scale, vol, faces, out, ops, lows, diag, value, state, elems, volume, sides, rows, flip, sems
):
    copies = [
        pltpu.make_async_copy(ref, into, sems.at[i])
        for i, (ref, into) in enumerate(
            ((vol, volume), (faces, sides), (forcing, value), (init, state), (scale, elems))
        )
    ]
    for copy in copies:
        copy.start()
    step = lax.axis_index("z") * 8 + lax.axis_index("x") * 2 + lax.axis_index("core")
    weight = jnp.where(step == 0, 1.5, 0.5).astype(jnp.float32)
    flip[...] = jnp.zeros((LANES, LANES), jnp.float32)
    rows[NB:, :] = jnp.zeros((LANES - NB, LANES), jnp.float32)
    for copy in copies[:2]:
        copy.wait()
    row = lax.broadcasted_iota(jnp.int32, (LANES, LANES), 0)
    col = lax.broadcasted_iota(jnp.int32, (LANES, LANES), 1)
    for op in range(5):
        flip[:NB, :NB] = volume[0] if op == 0 else sides[:, op - 1, :]
        square = flip[...]
        if op == 0:
            on = jnp.where(row == col, square, 0.0)
            diag[...] = jnp.broadcast_to(jnp.sum(on, axis=0, keepdims=True), (8, LANES))
            square = square - on
        square = square.T
        high, low = split(square)
        if op == 0:
            here, rest = 4 * LANES, ops.at[:LANES, 5 * LANES :]
        else:
            here = (op - 1) * LANES
            rest = lows.at[:, here : here + LANES]
        ops[:LANES, here : here + LANES] = high
        ops[LANES:, here : here + LANES] = high
        rest[...] = low
    ops[LANES:, 5 * LANES :] = jnp.zeros((LANES, LANES), jnp.bfloat16)
    for copy in copies[2:]:
        copy.wait()
    for s in (1, 0):
        for r in range(2):
            if s == 0:
                rows[:NB, :] = value[s * NB : (s + 1) * NB, r, :] + weight * state[0, :, r, :]
                rows[ES_LANE : ES_LANE + 1, :] = elems[0, r : r + 1, :]
            else:
                rows[:NB, :] = value[s * NB : (s + 1) * NB, r, :]
            flip[...] = rows[...].T
            for c in range(2):
                out[pl.ds(s * 8 + c * 2 + r, STEPS, stride=12), :] = flip[pl.ds(c, STEPS, stride=2), :]
    blank = jnp.zeros((4, LANES), jnp.float32)
    for m in range(STEPS):
        source = m - 4 if m % 8 < 4 else m + 4
        at = m * 12 + 4
        if 0 <= source < STEPS:
            out[at : at + 4, :] = out[source * 12 : source * 12 + 4, :]
        else:
            out[at : at + 4, :] = blank


def forward_kernel(table, got, out):
    lane = lax.broadcasted_iota(jnp.int32, (STEPS, LANES), 1)
    parts = [got[pl.ds(p, STEPS, stride=12), :] for p in range(12)]
    waves = transform(table, parts)
    for p in range(12):
        wave = waves[:, p * LANES : (p + 1) * LANES]
        if p < 8:
            wave = jnp.where(lane == ES_LANE, jnp.broadcast_to(parts[p][:1, :], wave.shape), wave)
        for c in range(2):
            at = c * 8 + p if p < 8 else 16 + c * 4 + p - 8
            out[pl.ds(at, FREQS, stride=24), :] = wave[c * FREQS : (c + 1) * FREQS]


def slot():
    return lax.axis_index("core") * 16 + lax.axis_index("y") * 4 + lax.axis_index("x")


def seat(xc, yd):
    return xc % 2 * 16 + yd * 4 + xc // 2


def invert(slots, diag, scale, inverse):
    mine = slots[slot()]
    shape = (WINDOW, 8, LANES)
    place = lax.axis_index("z") * CHUNK - HALO + lax.broadcasted_iota(jnp.int32, shape, 0)
    inside = jnp.logical_and(place >= 0, place < 8 * CHUNK)
    scaled = scale[...] * diag[...][None]
    im = mine[2:3][None]
    re0 = mine[0:1][None] + scaled
    re1 = mine[1:2][None] + scaled
    mod0 = jnp.where(inside, damping / (re0 * re0 + im * im), 0.0)
    mod1 = jnp.where(inside, damping / (re1 * re1 + im * im), 0.0)
    inverse[0] = re0 * mod0
    inverse[1] = re1 * mod1
    inverse[2] = im * mod0


def start(inverse, field, source, at):
    lane = lax.broadcasted_iota(jnp.int32, field.shape[1:], 2)
    g0 = jnp.where(lane < NB, field[0], 0.0)
    g1 = jnp.where(lane < NB, field[1], 0.0)
    source[0, at] = inverse[0, at] * g0 + inverse[2, at] * g1
    source[1, at] = inverse[1, at] * g1 - inverse[2, at] * g0


def couple(ops, lows, scale, field):
    wide = field.shape[0]
    inner = (wide - 2, 8, LANES)
    high, low = split(field.reshape(wide * 8, LANES))
    both = jnp.concatenate((high, low), axis=1)

    def product(left, right):
        return jnp.dot(left, right, preferred_element_type=jnp.float32)

    def columns(sums, i):
        return sums[:, i * LANES : (i + 1) * LANES].reshape(-1, 8, LANES)

    own = product(both[8:-8], ops[:, 4 * LANES :])
    along = product(both, ops[:, : 2 * LANES]) + product(high, lows[:, : 2 * LANES])
    across = product(both[8:-8], ops[:, 2 * LANES : 4 * LANES]) + product(high[8:-8], lows[:, 2 * LANES :])
    return (
        scale * (columns(own, 0) + columns(own, 1))
        + columns(along, 0)[:-2]
        + columns(along, 1)[2:]
        + pltpu.roll(columns(across, 0), 1, 1)
        + pltpu.roll(columns(across, 1), 7, 1)
    )


def damped(field, source, inverse, coupled):
    keep = 1.0 - damping
    return (
        keep * field[0] + source[0] - inverse[0] * coupled[0] - inverse[2] * coupled[1],
        keep * field[1] + source[1] - inverse[1] * coupled[1] + inverse[2] * coupled[0],
    )


def relax(ops, lows, scale, inverse, iterate, source, done):
    for sweep in range(done, SWEEPS):
        here = slice(sweep + 1, WINDOW - sweep - 1)
        coupled = [couple(ops, lows, scale[here], iterate[c, sweep : WINDOW - sweep]) for c in range(2)]
        fresh = damped(iterate[:, here], source[:, here], inverse[:, here], coupled)
        iterate[0, here] = fresh[0]
        iterate[1, here] = fresh[1]


def first_kernel(slots, ops, lows, diag, got, solved, state, scale, inverse, iterate, source):
    for xc in range(8):
        for yd in range(4):
            for c in range(2):
                for col in range(4):
                    w = HALO + 2 * xc + col
                    if col >= 2:
                        w = (2 * xc if xc < 4 else 16 + 2 * xc) + col - 2
                    at = c * 8 + col * 2
                    iterate[c, w, 2 * yd : 2 * yd + 2, :] = got[seat(xc, yd), at : at + 2, :]
    scale[...] = jnp.broadcast_to(iterate[0, :, :, ES_LANE : ES_LANE + 1], scale.shape)
    invert(slots, diag, scale, inverse)
    start(inverse, iterate[...], source, slice(0, WINDOW))
    iterate[...] = source[...]
    relax(ops, lows, scale, inverse, iterate, source, 1)
    mine = slots[slot()]
    middle = iterate[:, HALO : HALO + CHUNK]
    solved[...] = middle
    state[...] = mine[3:4][None] * middle[0] + mine[4:5][None] * middle[1]


def between_kernel(got, solved, after, done, left, right):
    del after
    for c in range(2):
        for xc in range(8):
            side = left if xc < 4 else right
            for yd in range(4):
                for col in range(2):
                    rows = slice(2 * yd, 2 * yd + 2)
                    at = c * 4 + col * 2
                    done[seat(xc, yd), at : at + 2, :] = solved[c, 2 * xc + col, rows, :]
                    side[c, 2 * (xc % 4) + col, rows, :] = got[seat(xc, yd), 16 + at : 18 + at, :]


def by_side(one, two):
    even = lax.rem(lax.axis_index("z"), 2) == 0
    return jnp.where(even, two, one), jnp.where(even, one, two)


def carry_kernel(slots, left, right, state0, state1, state2, state3, far, near):
    state = (state0[...] + state1[...]) + (state2[...] + state3[...])
    mine = slots[slot()]
    for c in range(2):
        part = mine[5 + c : 6 + c][None] * state
        far[c], near[c] = by_side(right[c] + part[CHUNK // 2 :], left[c] + part[: CHUNK // 2])


def inner_kernel(ops, lows, scale, inverse, far, near, edges, core, iterate, source):
    middle = slice(HALO, HALO + CHUNK)
    for i, part in enumerate(by_side(near[...], far[...])):
        start(inverse, part, source, slice((i + 1) * HALO, (i + 2) * HALO))
    iterate[...] = source[:, middle]
    for sweep in range(INNER + 1):
        lo, hi = sweep, CHUNK - sweep
        if sweep:
            here = slice(HALO + lo, HALO + hi)
            coupled = [couple(ops, lows, scale[here], iterate[c, lo - 1 : hi + 1]) for c in range(2)]
            fresh = damped(iterate[:, lo:hi], source[:, here], inverse[:, here], coupled)
            iterate[0, lo:hi] = fresh[0]
            iterate[1, lo:hi] = fresh[1]
        if sweep < INNER:
            edges[sweep, :, :2] = iterate[:, lo : lo + 2]
            edges[sweep, :, 2:] = iterate[:, hi - 2 : hi]
    core[...] = iterate[:, INNER : CHUNK - INNER]


def outer_kernel(
    ops, lows, scale, inverse, far, near, beyond_far, beyond_near, edges, core, before, out, sides, iterate, source
):
    left, right = by_side(near[...], far[...])
    west, east = by_side(beyond_near[...], beyond_far[...])
    for i, part in enumerate((west, left, right, east)):
        start(inverse, part, source, slice(i * HALO, (i + 1) * HALO))
    out[:, :8, :] = before[...]
    reach = HALO - 1
    sides[:, :reach] = source[:, 1:HALO]
    sides[:, reach + 4 :] = source[:, HALO + CHUNK : WINDOW - 1]
    for sweep in range(1, INNER + 1):
        sides[:, reach : reach + 4] = edges[sweep - 1]
        one = slice(sweep + 1, HALO + sweep)
        two = slice(WINDOW - HALO - sweep, WINDOW - 1 - sweep)
        given = [
            jnp.concatenate((ref[one], ref[HALO : HALO + 2], ref[two]), axis=0)
            for ref in [scale] + [inverse.at[i] for i in range(3)] + [source.at[i] for i in range(2)]
        ]
        coupled = [couple(ops, lows, given[0], sides[c]) for c in range(2)]
        fresh = damped(sides[:, 1:-1], given[4:], given[1:4], coupled)
        for c in range(2):
            sides[c, :reach] = fresh[c][:reach]
            sides[c, reach + 4 :] = fresh[c][reach + 2 :]
    iterate[:, INNER + 1 : HALO + INNER] = sides[:, :reach]
    iterate[:, HALO + INNER : WINDOW - HALO - INNER] = core[...]
    iterate[:, WINDOW - HALO - INNER : WINDOW - 1 - INNER] = sides[:, reach + 4 :]
    relax(ops, lows, scale, inverse, iterate, source, INNER + 1)
    for xc in range(8):
        for yd in range(4):
            for c in range(2):
                for col in range(2):
                    at = 8 + c * 4 + col * 2
                    out[seat(xc, yd), at : at + 2, :] = iterate[c, HALO + 2 * xc + col, 2 * yd : 2 * yd + 2, :]


def backward_kernel(table, got, out):
    parts = []
    for p in range(8):
        at = (p // 4) * 8 + p % 4
        halves = [got[pl.ds(at + 4 * c, FREQS, stride=16), :] for c in range(2)]
        parts.append(jnp.concatenate(halves, axis=0))
    slices = transform(table, parts)
    for p in range(8):
        out[pl.ds(p, STEPS, stride=8), :] = slices[:, p * LANES : (p + 1) * LANES]


def unpack_kernel(got, out, flip, held, sems):
    copies = []
    for s in range(2):
        for r in range(2):
            for c in range(2):
                flip[pl.ds(c, STEPS, stride=2), :] = got[pl.ds(s * 4 + c * 2 + r, STEPS, stride=8), :]
            held[s, 0, :, r, :] = flip[...].T[:NB, :]
        copies.append(pltpu.make_async_copy(held.at[s], out.at[s], sems.at[s]))
        copies[s].start()
    for copy in copies:
        copy.wait()


def call(kernel, outs, ins, scratch=(), specs=None, name=None, params=PARAMS, out=VMEM, cost=None):
    return pl.pallas_call(
        kernel,
        out_shape=outs,
        in_specs=specs or [VMEM] * len(ins),
        out_specs=jax.tree.map(lambda _: out, outs),
        scratch_shapes=scratch,
        compiler_params=params,
        cost_estimate=cost,
        name=name,
    )(*ins)


def f32(*shape):
    return jax.ShapeDtypeStruct(shape, jnp.float32)


def exchange(blocks, axes):
    return lax.all_to_all(blocks, axes, 0, 0, tiled=True)


def swapped(block, axis, bits):
    return lax.ppermute(block, axis, [(i, i ^ bits) for i in range(lax.axis_size(axis))])


def per_device(forcing, init_state, elem_scale, vol_op, face_ops):
    square = pltpu.VMEM((LANES, LANES), jnp.float32)
    window = (WINDOW, 8, LANES)
    inputs = (
        forcing.reshape(2 * NB, 2, LANES),
        init_state.reshape(1, NB, 2, LANES),
        elem_scale.reshape(1, 2, LANES),
        vol_op.reshape(1, NB, NB),
        jnp.transpose(face_ops, (1, 0, 2)),
    )
    packed, ops, lows, diag = call(
        pack_kernel,
        (
            pltpu.VMEM((STEPS * 12, LANES), jnp.float32),
            pltpu.VMEM((2 * LANES, 6 * LANES), jnp.bfloat16),
            pltpu.VMEM((LANES, 4 * LANES), jnp.bfloat16),
            pltpu.VMEM((8, LANES), jnp.float32),
        ),
        inputs,
        [pltpu.VMEM(value.shape, jnp.float32) for value in inputs]
        + [square, square, pltpu.SemaphoreType.DMA((len(inputs),))],
        [HBM] * len(inputs),
        name="pack",
        params=pltpu.CompilerParams(vmem_limit_bytes=60 * 1024 * 1024),
    )
    by_point = exchange(packed.reshape(STEPS, 3, 4, LANES), TIME).reshape(STEPS * 12, LANES)
    waves = call(forward_kernel, f32(FREQS * 24, LANES), (FORWARD, by_point), name="forward")
    got = exchange(waves.reshape(FREQS, 24, LANES), PLANE)
    both = pltpu.VMEM((2,) + window, jnp.float32)
    solved, state, scale, inverse = call(
        first_kernel,
        (f32(2, CHUNK, 8, LANES), f32(CHUNK, 8, LANES), f32(*window), f32(3, *window)),
        (SLOTS, ops, lows, diag, got),
        (both, both),
        name="first",
    )
    half = f32(2, CHUNK // 2, 8, LANES)
    state = state + swapped(state, "core", 1)
    done, left, right = call(
        between_kernel, (f32(FREQS, 8, LANES), half, half), (got, solved, state), (), [VMEM, VMEM, ANY], name="between"
    )
    near, far, across = (swapped(state, "y", bits) for bits in (1, 3, 2))
    state = ((state + near) + far) + across
    states = [state] + [swapped(state, "x", bits) for bits in (1, 3, 2)]
    far, near = call(carry_kernel, (half, half), (SLOTS, left, right, *states), name="carry")
    planes = lax.axis_size("z")
    other = [(z, (z + 1 if z % 2 else z - 1) % planes) for z in range(planes)]
    beyond_far = lax.ppermute(far, "z", other)
    beyond_near = swapped(near, "z", 1)
    edges, core = call(
        inner_kernel,
        (f32(INNER, 2, 4, 8, LANES), f32(2, CHUNK - 2 * INNER, 8, LANES)),
        (ops, lows, scale, inverse, far, near),
        (pltpu.VMEM((2, CHUNK, 8, LANES), jnp.float32), both),
        name="inner",
        cost=pl.CostEstimate(flops=2_000_000_000, bytes_accessed=1_000_000, transcendentals=0),
    )
    done = call(
        outer_kernel,
        f32(FREQS, 16, LANES),
        (ops, lows, scale, inverse, far, near, beyond_far, beyond_near, edges, core, done),
        (pltpu.VMEM((2, 2 * HALO + 2, 8, LANES), jnp.float32), both, both),
        name="outer",
    )
    got = exchange(done, PLANE).reshape(FREQS * 16, LANES)
    slices = call(backward_kernel, f32(STEPS * 8, LANES), (BACKWARD, got), name="backward")
    by_column = exchange(slices.reshape(STEPS, 8, LANES), TIME).reshape(STEPS * 8, LANES)
    result = f32(2, 1, NB, 2, LANES)
    return call(
        unpack_kernel,
        result,
        (by_column,),
        (square, pltpu.VMEM(result.shape, jnp.float32), pltpu.SemaphoreType.DMA((2,))),
        name="unpack",
        out=ANY,
    )


def solution(mesh):
    grid = Mesh(mesh.devices.reshape(8, 4, 2, 4), ("z", "x", "core", "y"))
    return jax.shard_map(
        per_device,
        mesh=grid,
        in_specs=(
            P(None, TIME, None, "y", None),
            P(None, "y", None),
            P("y", None),
            P(),
            P(),
        ),
        out_specs=P(None, TIME, None, "y", None),
        check_vma=False,
    )
```

```python
import math

import jax
import jax.numpy as jnp
import ml_dtypes
import numpy as np
from jax import lax
from jax.experimental import pallas as pl
from jax.experimental.pallas import tpu as pltpu
from jax.sharding import Mesh
from jax.sharding import PartitionSpec as P

NB = 125
SWEEPS = 8
STEPS = 64
LANES = 128
FREQS = STEPS // 2
CHUNK = 16
WINDOW = 32
HALO = 8
INNER = 4
ES_LANE = NB

circ_alpha = 0.01
damping = 0.7

TIME = ("z", "x", "core")
PLANE = ("core", "y", "x")


def tables():
    n = np.arange(STEPS)
    log_alpha = math.log(circ_alpha)
    grow = np.exp(n * (log_alpha / STEPS))
    forward = np.zeros((STEPS, STEPS))
    backward = np.zeros((STEPS, STEPS))
    shifts = np.zeros((FREQS, 4))
    root = math.exp(log_alpha / STEPS)
    forward[0] = 1.0
    forward[1] = (-1.0) ** n
    backward[:, 0] = 1.0
    backward[:, 1] = (-1.0) ** n
    shifts[0] = (1.0 - root, 1.0 + root, 0.0, 0.0)
    for k in range(1, FREQS):
        angle = 2.0 * math.pi * ((k * n) % STEPS) / STEPS
        forward[2 * k] = np.cos(angle)
        forward[2 * k + 1] = -np.sin(angle)
        backward[:, 2 * k] = 2.0 * np.cos(angle)
        backward[:, 2 * k + 1] = -2.0 * np.sin(angle)
        theta = 2.0 * math.pi * k / STEPS
        shifts[k, :3] = (1.0 - root * math.cos(theta), 1.0 - root * math.cos(theta), root * math.sin(theta))
    forward = forward * grow[None, :]
    backward = backward / grow[:, None] / STEPS
    carry = 0.5 * forward.sum(1) + forward[:, 0]
    last = backward[STEPS - 1]
    return tuple(a.astype(np.float32) for a in (forward, backward, shifts, carry, last))


def in_parts(table):
    high = table.astype(ml_dtypes.bfloat16)
    rest = table - high.astype(np.float32)
    middle = rest.astype(ml_dtypes.bfloat16)
    low = (rest - middle.astype(np.float32)).astype(ml_dtypes.bfloat16)
    return np.concatenate((high, high, middle, high, middle, low), axis=1)


FORWARD, BACKWARD, SHIFTS, CARRY, LAST = tables()
BY_PART = np.concatenate((np.arange(0, STEPS, 2), np.arange(1, STEPS, 2)))
FORWARD = in_parts(FORWARD[BY_PART])
BACKWARD = in_parts(BACKWARD[:, BY_PART])
SLOTS = np.concatenate((SHIFTS[:, :3], LAST.reshape(FREQS, 2), CARRY.reshape(FREQS, 2), SHIFTS[:, :1]), axis=1)
SLOTS = np.repeat(SLOTS[:, :, None], LANES, axis=2)

VMEM = pl.BlockSpec(memory_space=pltpu.VMEM)
HBM = pl.BlockSpec(memory_space=pltpu.HBM)
ANY = pl.BlockSpec(memory_space=pl.ANY)
PARAMS = pltpu.CompilerParams(vmem_limit_bytes=32 * 1024 * 1024)


def split(value):
    high = value.astype(jnp.bfloat16)
    return high, (value - high.astype(jnp.float32)).astype(jnp.bfloat16)


def transform(table, parts):
    whole = jnp.concatenate(parts, axis=1)
    high = whole.astype(jnp.bfloat16)
    middle, low = split(whole - high.astype(jnp.float32))
    stack = jnp.concatenate((high, middle, high, low, middle, high), axis=0)
    return jnp.dot(table[...], stack, preferred_element_type=jnp.float32)


def pack_kernel(
    forcing, init, scale, vol, faces, out, ops, lows, diag, value, state, elems, volume, sides, rows, flip, sems
):
    copies = [
        pltpu.make_async_copy(ref, into, sems.at[i])
        for i, (ref, into) in enumerate(
            ((vol, volume), (faces, sides), (forcing, value), (init, state), (scale, elems))
        )
    ]
    for copy in copies:
        copy.start()
    step = lax.axis_index("z") * 8 + lax.axis_index("x") * 2 + lax.axis_index("core")
    weight = jnp.where(step == 0, 1.5, 0.5).astype(jnp.float32)
    flip[...] = jnp.zeros((LANES, LANES), jnp.float32)
    rows[NB:, :] = jnp.zeros((LANES - NB, LANES), jnp.float32)
    for copy in copies[:2]:
        copy.wait()
    row = lax.broadcasted_iota(jnp.int32, (LANES, LANES), 0)
    col = lax.broadcasted_iota(jnp.int32, (LANES, LANES), 1)
    for op in range(5):
        flip[:NB, :NB] = volume[0] if op == 0 else sides[:, op - 1, :]
        square = flip[...]
        if op == 0:
            on = jnp.where(row == col, square, 0.0)
            diag[...] = jnp.broadcast_to(jnp.sum(on, axis=0, keepdims=True), (8, LANES))
            square = square - on
        square = square.T
        high, low = split(square)
        if op == 0:
            here, rest = 4 * LANES, ops.at[:LANES, 5 * LANES :]
        else:
            here = (op - 1) * LANES
            rest = lows.at[:, here : here + LANES]
        ops[:LANES, here : here + LANES] = high
        ops[LANES:, here : here + LANES] = high
        rest[...] = low
    ops[LANES:, 5 * LANES :] = jnp.zeros((LANES, LANES), jnp.bfloat16)
    for copy in copies[2:]:
        copy.wait()
    for s in (1, 0):
        for r in range(2):
            if s == 0:
                rows[:NB, :] = value[s * NB : (s + 1) * NB, r, :] + weight * state[0, :, r, :]
                rows[ES_LANE : ES_LANE + 1, :] = elems[0, r : r + 1, :]
            else:
                rows[:NB, :] = value[s * NB : (s + 1) * NB, r, :]
            flip[...] = rows[...].T
            for c in range(2):
                out[pl.ds(s * 8 + c * 2 + r, STEPS, stride=12), :] = flip[pl.ds(c, STEPS, stride=2), :]
    blank = jnp.zeros((4, LANES), jnp.float32)
    for m in range(STEPS):
        source = m - 4 if m % 8 < 4 else m + 4
        at = m * 12 + 4
        if 0 <= source < STEPS:
            out[at : at + 4, :] = out[source * 12 : source * 12 + 4, :]
        else:
            out[at : at + 4, :] = blank


def forward_kernel(table, got, out):
    lane = lax.broadcasted_iota(jnp.int32, (STEPS, LANES), 1)
    parts = [got[pl.ds(p, STEPS, stride=12), :] for p in range(12)]
    waves = transform(table, parts)
    for p in range(12):
        wave = waves[:, p * LANES : (p + 1) * LANES]
        if p < 8:
            wave = jnp.where(lane == ES_LANE, jnp.broadcast_to(parts[p][:1, :], wave.shape), wave)
        for c in range(2):
            at = c * 8 + p if p < 8 else 16 + c * 4 + p - 8
            out[pl.ds(at, FREQS, stride=24), :] = wave[c * FREQS : (c + 1) * FREQS]


def slot():
    return lax.axis_index("core") * 16 + lax.axis_index("y") * 4 + lax.axis_index("x")


def seat(xc, yd):
    return xc % 2 * 16 + yd * 4 + xc // 2


def invert(slots, diag, scale, inverse):
    mine = slots[slot()]
    shape = (WINDOW, 8, LANES)
    place = lax.axis_index("z") * CHUNK - HALO + lax.broadcasted_iota(jnp.int32, shape, 0)
    inside = jnp.logical_and(place >= 0, place < 8 * CHUNK)
    scaled = scale[...] * diag[...][None]
    im = mine[2:3][None]
    re0 = mine[0:1][None] + scaled
    re1 = mine[1:2][None] + scaled
    mod0 = jnp.where(inside, damping / (re0 * re0 + im * im), 0.0)
    mod1 = jnp.where(inside, damping / (re1 * re1 + im * im), 0.0)
    inverse[0] = re0 * mod0
    inverse[1] = re1 * mod1
    inverse[2] = im * mod0


def start(inverse, field, source, at):
    lane = lax.broadcasted_iota(jnp.int32, field.shape[1:], 2)
    g0 = jnp.where(lane < NB, field[0], 0.0)
    g1 = jnp.where(lane < NB, field[1], 0.0)
    source[0, at] = inverse[0, at] * g0 + inverse[2, at] * g1
    source[1, at] = inverse[1, at] * g1 - inverse[2, at] * g0


def couple(ops, lows, scale, field):
    wide = field.shape[0]
    inner = (wide - 2, 8, LANES)
    high, low = split(field.reshape(wide * 8, LANES))
    both = jnp.concatenate((high, low), axis=1)

    def product(left, right):
        return jnp.dot(left, right, preferred_element_type=jnp.float32)

    def columns(sums, i):
        return sums[:, i * LANES : (i + 1) * LANES].reshape(-1, 8, LANES)

    own = product(both[8:-8], ops[:, 4 * LANES :])
    along = product(both, ops[:, : 2 * LANES]) + product(high, lows[:, : 2 * LANES])
    across = product(both[8:-8], ops[:, 2 * LANES : 4 * LANES]) + product(high[8:-8], lows[:, 2 * LANES :])
    return (
        scale * (columns(own, 0) + columns(own, 1))
        + columns(along, 0)[:-2]
        + columns(along, 1)[2:]
        + pltpu.roll(columns(across, 0), 1, 1)
        + pltpu.roll(columns(across, 1), 7, 1)
    )


def damped(field, source, inverse, coupled):
    keep = 1.0 - damping
    return (
        keep * field[0] + source[0] - inverse[0] * coupled[0] - inverse[2] * coupled[1],
        keep * field[1] + source[1] - inverse[1] * coupled[1] + inverse[2] * coupled[0],
    )


def relax(ops, lows, scale, inverse, iterate, source, done):
    for sweep in range(done, SWEEPS):
        here = slice(sweep + 1, WINDOW - sweep - 1)
        coupled = [couple(ops, lows, scale[here], iterate[c, sweep : WINDOW - sweep]) for c in range(2)]
        fresh = damped(iterate[:, here], source[:, here], inverse[:, here], coupled)
        iterate[0, here] = fresh[0]
        iterate[1, here] = fresh[1]


def first_kernel(slots, ops, lows, diag, got, solved, state, scale, inverse, iterate, source):
    for xc in range(8):
        for yd in range(4):
            for c in range(2):
                for col in range(4):
                    w = HALO + 2 * xc + col
                    if col >= 2:
                        w = (2 * xc if xc < 4 else 16 + 2 * xc) + col - 2
                    at = c * 8 + col * 2
                    iterate[c, w, 2 * yd : 2 * yd + 2, :] = got[seat(xc, yd), at : at + 2, :]
    scale[...] = jnp.broadcast_to(iterate[0, :, :, ES_LANE : ES_LANE + 1], scale.shape)
    invert(slots, diag, scale, inverse)
    start(inverse, iterate[...], source, slice(0, WINDOW))
    iterate[...] = source[...]
    relax(ops, lows, scale, inverse, iterate, source, 1)
    mine = slots[slot()]
    middle = iterate[:, HALO : HALO + CHUNK]
    solved[...] = middle
    state[...] = mine[3:4][None] * middle[0] + mine[4:5][None] * middle[1]


def between_kernel(got, solved, after, done, left, right):
    del after
    for c in range(2):
        for xc in range(8):
            side = left if xc < 4 else right
            for yd in range(4):
                for col in range(2):
                    rows = slice(2 * yd, 2 * yd + 2)
                    at = c * 4 + col * 2
                    done[seat(xc, yd), at : at + 2, :] = solved[c, 2 * xc + col, rows, :]
                    side[c, 2 * (xc % 4) + col, rows, :] = got[seat(xc, yd), 16 + at : 18 + at, :]


def by_side(one, two):
    even = lax.rem(lax.axis_index("z") + lax.axis_index("core"), 2) == 0
    return jnp.where(even, two, one), jnp.where(even, one, two)


def carry_kernel(slots, left, right, state0, state1, state2, state3, far, near):
    state = (state0[...] + state1[...]) + (state2[...] + state3[...])
    mine = slots[slot()]
    for c in range(2):
        part = mine[5 + c : 6 + c][None] * state
        far[c], near[c] = by_side(right[c] + part[CHUNK // 2 :], left[c] + part[: CHUNK // 2])


def inner_kernel(ops, lows, scale, inverse, far, near, edges, core, iterate, source):
    middle = slice(HALO, HALO + CHUNK)
    for i, part in enumerate(by_side(near[...], far[...])):
        start(inverse, part, source, slice((i + 1) * HALO, (i + 2) * HALO))
    iterate[...] = source[:, middle]
    for sweep in range(INNER + 1):
        lo, hi = sweep, CHUNK - sweep
        if sweep:
            here = slice(HALO + lo, HALO + hi)
            coupled = [couple(ops, lows, scale[here], iterate[c, lo - 1 : hi + 1]) for c in range(2)]
            fresh = damped(iterate[:, lo:hi], source[:, here], inverse[:, here], coupled)
            iterate[0, lo:hi] = fresh[0]
            iterate[1, lo:hi] = fresh[1]
        if sweep < INNER:
            edges[sweep, :, :2] = iterate[:, lo : lo + 2]
            edges[sweep, :, 2:] = iterate[:, hi - 2 : hi]
    core[...] = iterate[:, INNER : CHUNK - INNER]


def outer_kernel(
    ops, lows, scale, inverse, far, near, beyond_far, beyond_near, edges, core, before, out, sides, iterate, source
):
    left, right = by_side(near[...], far[...])
    west, east = by_side(beyond_near[...], beyond_far[...])
    for i, part in enumerate((west, left, right, east)):
        start(inverse, part, source, slice(i * HALO, (i + 1) * HALO))
    out[:, :8, :] = before[...]
    reach = HALO - 1
    sides[:, :reach] = source[:, 1:HALO]
    sides[:, reach + 4 :] = source[:, HALO + CHUNK : WINDOW - 1]
    for sweep in range(1, INNER + 1):
        sides[:, reach : reach + 4] = edges[sweep - 1]
        one = slice(sweep + 1, HALO + sweep)
        two = slice(WINDOW - HALO - sweep, WINDOW - 1 - sweep)
        given = [
            jnp.concatenate((ref[one], ref[HALO : HALO + 2], ref[two]), axis=0)
            for ref in [scale] + [inverse.at[i] for i in range(3)] + [source.at[i] for i in range(2)]
        ]
        coupled = [couple(ops, lows, given[0], sides[c]) for c in range(2)]
        fresh = damped(sides[:, 1:-1], given[4:], given[1:4], coupled)
        for c in range(2):
            sides[c, :reach] = fresh[c][:reach]
            sides[c, reach + 4 :] = fresh[c][reach + 2 :]
    iterate[:, INNER + 1 : HALO + INNER] = sides[:, :reach]
    iterate[:, HALO + INNER : WINDOW - HALO - INNER] = core[...]
    iterate[:, WINDOW - HALO - INNER : WINDOW - 1 - INNER] = sides[:, reach + 4 :]
    relax(ops, lows, scale, inverse, iterate, source, INNER + 1)
    for xc in range(8):
        for yd in range(4):
            for c in range(2):
                for col in range(2):
                    at = 8 + c * 4 + col * 2
                    out[seat(xc, yd), at : at + 2, :] = iterate[c, HALO + 2 * xc + col, 2 * yd : 2 * yd + 2, :]


def backward_kernel(table, got, out):
    parts = []
    for p in range(8):
        at = (p // 4) * 8 + p % 4
        halves = [got[pl.ds(at + 4 * c, FREQS, stride=16), :] for c in range(2)]
        parts.append(jnp.concatenate(halves, axis=0))
    slices = transform(table, parts)
    for p in range(8):
        out[pl.ds(p, STEPS, stride=8), :] = slices[:, p * LANES : (p + 1) * LANES]


def unpack_kernel(got, out, flip, held, sems):
    copies = []
    for s in range(2):
        for r in range(2):
            for c in range(2):
                flip[pl.ds(c, STEPS, stride=2), :] = got[pl.ds(s * 4 + c * 2 + r, STEPS, stride=8), :]
            held[s, 0, :, r, :] = flip[...].T[:NB, :]
        copies.append(pltpu.make_async_copy(held.at[s], out.at[s], sems.at[s]))
        copies[s].start()
    for copy in copies:
        copy.wait()


def call(kernel, outs, ins, scratch=(), specs=None, name=None, params=PARAMS, out=VMEM, cost=None):
    return pl.pallas_call(
        kernel,
        out_shape=outs,
        in_specs=specs or [VMEM] * len(ins),
        out_specs=jax.tree.map(lambda _: out, outs),
        scratch_shapes=scratch,
        compiler_params=params,
        cost_estimate=cost,
        name=name,
    )(*ins)


def f32(*shape):
    return jax.ShapeDtypeStruct(shape, jnp.float32)


def exchange(blocks, axes):
    return lax.all_to_all(blocks, axes, 0, 0, tiled=True)


def routed(block, axis, partners):
    count = lax.axis_size(axis)
    axes = ("core", axis) if axis == "y" else (axis, "core")

    def at(core, place):
        return core * count + place if axis == "y" else place * 2 + core

    pairs = [(at(core, i), at(core, partners[core](i))) for core in range(2) for i in range(count)]
    return lax.ppermute(block, axes, pairs)


def crossed(block, axis):
    near, other, across = (lambda i: i ^ 1), (lambda i: i ^ 3), (lambda i: i ^ 2)
    return [routed(block, axis, pair) for pair in ((near, other), (other, near), (across, across))]


def per_device(forcing, init_state, elem_scale, vol_op, face_ops):
    square = pltpu.VMEM((LANES, LANES), jnp.float32)
    window = (WINDOW, 8, LANES)
    inputs = (
        forcing.reshape(2 * NB, 2, LANES),
        init_state.reshape(1, NB, 2, LANES),
        elem_scale.reshape(1, 2, LANES),
        vol_op.reshape(1, NB, NB),
        jnp.transpose(face_ops, (1, 0, 2)),
    )
    packed, ops, lows, diag = call(
        pack_kernel,
        (
            pltpu.VMEM((STEPS * 12, LANES), jnp.float32),
            pltpu.VMEM((2 * LANES, 6 * LANES), jnp.bfloat16),
            pltpu.VMEM((LANES, 4 * LANES), jnp.bfloat16),
            pltpu.VMEM((8, LANES), jnp.float32),
        ),
        inputs,
        [pltpu.VMEM(value.shape, jnp.float32) for value in inputs]
        + [square, square, pltpu.SemaphoreType.DMA((len(inputs),))],
        [HBM] * len(inputs),
        name="pack",
        params=pltpu.CompilerParams(vmem_limit_bytes=60 * 1024 * 1024),
    )
    by_point = exchange(packed.reshape(STEPS, 3, 4, LANES), TIME).reshape(STEPS * 12, LANES)
    waves = call(forward_kernel, f32(FREQS * 24, LANES), (FORWARD, by_point), name="forward")
    got = exchange(waves.reshape(FREQS, 24, LANES), PLANE)
    both = pltpu.VMEM((2,) + window, jnp.float32)
    solved, state, scale, inverse = call(
        first_kernel,
        (f32(2, CHUNK, 8, LANES), f32(CHUNK, 8, LANES), f32(*window), f32(3, *window)),
        (SLOTS, ops, lows, diag, got),
        (both, both),
        name="first",
    )
    half = f32(2, CHUNK // 2, 8, LANES)
    state = state + lax.ppermute(state, "core", [(0, 1), (1, 0)])
    done, left, right = call(
        between_kernel, (f32(FREQS, 8, LANES), half, half), (got, solved, state), (), [VMEM, VMEM, ANY], name="between"
    )
    one, two, three = crossed(state, "y")
    state = ((state + one) + two) + three
    states = [state] + crossed(state, "x")
    far, near = call(carry_kernel, (half, half), (SLOTS, left, right, *states), name="carry")
    planes = lax.axis_size("z")

    def paired(z):
        return z ^ 1

    def other(z):
        return (z + 1 if z % 2 else z - 1) % planes

    beyond_far = routed(far, "z", (other, paired))
    beyond_near = routed(near, "z", (paired, other))
    edges, core = call(
        inner_kernel,
        (f32(INNER, 2, 4, 8, LANES), f32(2, CHUNK - 2 * INNER, 8, LANES)),
        (ops, lows, scale, inverse, far, near),
        (pltpu.VMEM((2, CHUNK, 8, LANES), jnp.float32), both),
        name="inner",
        cost=pl.CostEstimate(flops=2_000_000_000, bytes_accessed=1_000_000, transcendentals=0),
    )
    done = call(
        outer_kernel,
        f32(FREQS, 16, LANES),
        (ops, lows, scale, inverse, far, near, beyond_far, beyond_near, edges, core, done),
        (pltpu.VMEM((2, 2 * HALO + 2, 8, LANES), jnp.float32), both, both),
        name="outer",
    )
    got = exchange(done, PLANE).reshape(FREQS * 16, LANES)
    slices = call(backward_kernel, f32(STEPS * 8, LANES), (BACKWARD, got), name="backward")
    by_column = exchange(slices.reshape(STEPS, 8, LANES), TIME).reshape(STEPS * 8, LANES)
    result = f32(2, 1, NB, 2, LANES)
    return call(
        unpack_kernel,
        result,
        (by_column,),
        (square, pltpu.VMEM(result.shape, jnp.float32), pltpu.SemaphoreType.DMA((2,))),
        name="unpack",
        out=ANY,
    )


def solution(mesh):
    grid = Mesh(mesh.devices.reshape(8, 4, 2, 4), ("z", "x", "core", "y"))
    return jax.shard_map(
        per_device,
        mesh=grid,
        in_specs=(
            P(None, TIME, None, "y", None),
            P(None, "y", None),
            P("y", None),
            P(),
            P(),
        ),
        out_specs=P(None, TIME, None, "y", None),
        check_vma=False,
    )
```

```python
import math

import jax
import jax.numpy as jnp
import ml_dtypes
import numpy as np
from jax import lax
from jax.experimental import pallas as pl
from jax.experimental.pallas import tpu as pltpu
from jax.sharding import Mesh
from jax.sharding import PartitionSpec as P

NB = 125
SWEEPS = 8
STEPS = 64
LANES = 128
FREQS = STEPS // 2
CHUNK = 16
WINDOW = 32
HALO = 8
ES_LANE = NB

circ_alpha = 0.01
damping = 0.7

TIME = ("z", "x", "core")
PLANE = ("core", "y", "x")


def tables():
    n = np.arange(STEPS)
    log_alpha = math.log(circ_alpha)
    grow = np.exp(n * (log_alpha / STEPS))
    forward = np.zeros((STEPS, STEPS))
    backward = np.zeros((STEPS, STEPS))
    shifts = np.zeros((FREQS, 4))
    root = math.exp(log_alpha / STEPS)
    forward[0] = 1.0
    forward[1] = (-1.0) ** n
    backward[:, 0] = 1.0
    backward[:, 1] = (-1.0) ** n
    shifts[0] = (1.0 - root, 1.0 + root, 0.0, 0.0)
    for k in range(1, FREQS):
        angle = 2.0 * math.pi * ((k * n) % STEPS) / STEPS
        forward[2 * k] = np.cos(angle)
        forward[2 * k + 1] = -np.sin(angle)
        backward[:, 2 * k] = 2.0 * np.cos(angle)
        backward[:, 2 * k + 1] = -2.0 * np.sin(angle)
        theta = 2.0 * math.pi * k / STEPS
        shifts[k, :3] = (1.0 - root * math.cos(theta), 1.0 - root * math.cos(theta), root * math.sin(theta))
    forward = forward * grow[None, :]
    backward = backward / grow[:, None] / STEPS
    carry = 0.5 * forward.sum(1) + forward[:, 0]
    last = backward[STEPS - 1]
    return tuple(a.astype(np.float32) for a in (forward, backward, shifts, carry, last))


def in_parts(table):
    high = table.astype(ml_dtypes.bfloat16)
    rest = table - high.astype(np.float32)
    middle = rest.astype(ml_dtypes.bfloat16)
    low = (rest - middle.astype(np.float32)).astype(ml_dtypes.bfloat16)
    return np.concatenate((high, high, middle, high, middle, low), axis=1)


FORWARD, BACKWARD, SHIFTS, CARRY, LAST = tables()
BY_PART = np.concatenate((np.arange(0, STEPS, 2), np.arange(1, STEPS, 2)))
FORWARD = in_parts(FORWARD[BY_PART])
BACKWARD = in_parts(BACKWARD[:, BY_PART])
SLOTS = np.concatenate((SHIFTS[:, :3], LAST.reshape(FREQS, 2), CARRY.reshape(FREQS, 2), SHIFTS[:, :1]), axis=1)
SLOTS = np.repeat(SLOTS[:, :, None], LANES, axis=2)

VMEM = pl.BlockSpec(memory_space=pltpu.VMEM)
HBM = pl.BlockSpec(memory_space=pltpu.HBM)
ANY = pl.BlockSpec(memory_space=pl.ANY)
PARAMS = pltpu.CompilerParams(vmem_limit_bytes=32 * 1024 * 1024)


def split(value):
    high = value.astype(jnp.bfloat16)
    return high, (value - high.astype(jnp.float32)).astype(jnp.bfloat16)


def transform(table, parts):
    whole = jnp.concatenate(parts, axis=1)
    high = whole.astype(jnp.bfloat16)
    middle, low = split(whole - high.astype(jnp.float32))
    stack = jnp.concatenate((high, middle, high, low, middle, high), axis=0)
    return jnp.dot(table[...], stack, preferred_element_type=jnp.float32)


def pack_kernel(
    forcing, init, scale, vol, faces, out, ops, lows, diag, value, state, elems, volume, sides, rows, flip, sems
):
    copies = [
        pltpu.make_async_copy(ref, into, sems.at[i])
        for i, (ref, into) in enumerate(
            ((vol, volume), (faces, sides), (forcing, value), (init, state), (scale, elems))
        )
    ]
    for copy in copies:
        copy.start()
    step = lax.axis_index("z") * 8 + lax.axis_index("x") * 2 + lax.axis_index("core")
    weight = jnp.where(step == 0, 1.5, 0.5).astype(jnp.float32)
    flip[...] = jnp.zeros((LANES, LANES), jnp.float32)
    rows[NB:, :] = jnp.zeros((LANES - NB, LANES), jnp.float32)
    for copy in copies[:2]:
        copy.wait()
    row = lax.broadcasted_iota(jnp.int32, (LANES, LANES), 0)
    col = lax.broadcasted_iota(jnp.int32, (LANES, LANES), 1)
    for op in range(5):
        flip[:NB, :NB] = volume[0] if op == 0 else sides[:, op - 1, :]
        square = flip[...]
        if op == 0:
            on = jnp.where(row == col, square, 0.0)
            diag[...] = jnp.broadcast_to(jnp.sum(on, axis=0, keepdims=True), (8, LANES))
            square = square - on
        square = square.T
        high, low = split(square)
        if op == 0:
            here, rest = 4 * LANES, ops.at[:LANES, 5 * LANES :]
        else:
            here = (op - 1) * LANES
            rest = lows.at[:, here : here + LANES]
        ops[:LANES, here : here + LANES] = high
        ops[LANES:, here : here + LANES] = high
        rest[...] = low
    ops[LANES:, 5 * LANES :] = jnp.zeros((LANES, LANES), jnp.bfloat16)
    for copy in copies[2:]:
        copy.wait()
    for s in (1, 0):
        for r in range(2):
            if s == 0:
                rows[:NB, :] = value[s * NB : (s + 1) * NB, r, :] + weight * state[0, :, r, :]
                rows[ES_LANE : ES_LANE + 1, :] = elems[0, r : r + 1, :]
            else:
                rows[:NB, :] = value[s * NB : (s + 1) * NB, r, :]
            flip[...] = rows[...].T
            for c in range(2):
                out[pl.ds(s * 8 + c * 2 + r, STEPS, stride=12), :] = flip[pl.ds(c, STEPS, stride=2), :]
    blank = jnp.zeros((4, LANES), jnp.float32)
    for m in range(STEPS):
        source = m - 4 if m % 8 < 4 else m + 4
        at = m * 12 + 4
        if 0 <= source < STEPS:
            out[at : at + 4, :] = out[source * 12 : source * 12 + 4, :]
        else:
            out[at : at + 4, :] = blank


def forward_kernel(table, got, out):
    lane = lax.broadcasted_iota(jnp.int32, (STEPS, LANES), 1)
    parts = [got[pl.ds(p, STEPS, stride=12), :] for p in range(12)]
    waves = transform(table, parts)
    for p in range(12):
        wave = waves[:, p * LANES : (p + 1) * LANES]
        if p < 8:
            wave = jnp.where(lane == ES_LANE, jnp.broadcast_to(parts[p][:1, :], wave.shape), wave)
        for c in range(2):
            at = c * 8 + p if p < 8 else 16 + c * 4 + p - 8
            out[pl.ds(at, FREQS, stride=24), :] = wave[c * FREQS : (c + 1) * FREQS]


def slot():
    return lax.axis_index("core") * 16 + lax.axis_index("y") * 4 + lax.axis_index("x")


def seat(xc, yd):
    return xc % 2 * 16 + yd * 4 + xc // 2


def invert(slots, diag, scale, inverse):
    mine = slots[slot()]
    shape = (WINDOW, 8, LANES)
    place = lax.axis_index("z") * CHUNK - HALO + lax.broadcasted_iota(jnp.int32, shape, 0)
    inside = jnp.logical_and(place >= 0, place < 8 * CHUNK)
    scaled = scale[...] * diag[...][None]
    im = mine[2:3][None]
    re0 = mine[0:1][None] + scaled
    re1 = mine[1:2][None] + scaled
    mod0 = jnp.where(inside, damping / (re0 * re0 + im * im), 0.0)
    mod1 = jnp.where(inside, damping / (re1 * re1 + im * im), 0.0)
    inverse[0] = re0 * mod0
    inverse[1] = re1 * mod1
    inverse[2] = im * mod0


def start(inverse, field, source, at):
    lane = lax.broadcasted_iota(jnp.int32, field.shape[1:], 2)
    g0 = jnp.where(lane < NB, field[0], 0.0)
    g1 = jnp.where(lane < NB, field[1], 0.0)
    source[0, at] = inverse[0, at] * g0 + inverse[2, at] * g1
    source[1, at] = inverse[1, at] * g1 - inverse[2, at] * g0


def couple(ops, lows, scale, field):
    wide = field.shape[0]
    inner = (wide - 2, 8, LANES)
    high, low = split(field.reshape(wide * 8, LANES))
    both = jnp.concatenate((high, low), axis=1)

    def product(left, right):
        return jnp.dot(left, right, preferred_element_type=jnp.float32)

    def columns(sums, i):
        return sums[:, i * LANES : (i + 1) * LANES].reshape(-1, 8, LANES)

    own = product(both[8:-8], ops[:, 4 * LANES :])
    along = product(both, ops[:, : 2 * LANES]) + product(high, lows[:, : 2 * LANES])
    across = product(both[8:-8], ops[:, 2 * LANES : 4 * LANES]) + product(high[8:-8], lows[:, 2 * LANES :])
    return (
        scale * (columns(own, 0) + columns(own, 1))
        + columns(along, 0)[:-2]
        + columns(along, 1)[2:]
        + pltpu.roll(columns(across, 0), 1, 1)
        + pltpu.roll(columns(across, 1), 7, 1)
    )


def damped(field, source, inverse, coupled):
    keep = 1.0 - damping
    return (
        keep * field[0] + source[0] - inverse[0] * coupled[0] - inverse[2] * coupled[1],
        keep * field[1] + source[1] - inverse[1] * coupled[1] + inverse[2] * coupled[0],
    )


def relax(ops, lows, scale, inverse, iterate, source):
    start(inverse, iterate[...], source, slice(0, WINDOW))
    iterate[...] = source[...]
    for sweep in range(1, SWEEPS):
        here = slice(sweep + 1, WINDOW - sweep - 1)
        coupled = [couple(ops, lows, scale[here], iterate[c, sweep : WINDOW - sweep]) for c in range(2)]
        fresh = damped(iterate[:, here], source[:, here], inverse[:, here], coupled)
        iterate[0, here] = fresh[0]
        iterate[1, here] = fresh[1]


def first_kernel(slots, ops, lows, diag, got, solved, state, scale, inverse, iterate, source):
    for xc in range(8):
        for yd in range(4):
            for c in range(2):
                for col in range(4):
                    w = HALO + 2 * xc + col
                    if col >= 2:
                        w = (2 * xc if xc < 4 else 16 + 2 * xc) + col - 2
                    at = c * 8 + col * 2
                    iterate[c, w, 2 * yd : 2 * yd + 2, :] = got[seat(xc, yd), at : at + 2, :]
    scale[...] = jnp.broadcast_to(iterate[0, :, :, ES_LANE : ES_LANE + 1], scale.shape)
    invert(slots, diag, scale, inverse)
    relax(ops, lows, scale, inverse, iterate, source)
    mine = slots[slot()]
    middle = iterate[:, HALO : HALO + CHUNK]
    solved[...] = middle
    state[...] = mine[3:4][None] * middle[0] + mine[4:5][None] * middle[1]


def between_kernel(got, solved, after, done, far, near, left, right):
    del after
    for c in range(2):
        for xc in range(8):
            side = left if xc < 4 else right
            for yd in range(4):
                for col in range(2):
                    rows = slice(2 * yd, 2 * yd + 2)
                    at = c * 4 + col * 2
                    done[seat(xc, yd), at : at + 2, :] = solved[c, 2 * xc + col, rows, :]
                    side[c, 2 * (xc % 4) + col, rows, :] = got[seat(xc, yd), 16 + at : 18 + at, :]
    far[...], near[...] = by_side(right[...], left[...])


def by_side(one, two):
    even = lax.rem(lax.axis_index("z"), 2) == 0
    return jnp.where(even, two, one), jnp.where(even, one, two)


def carry_kernel(slots, wave_far, wave_near, state0, state1, state2, state3, far, near, state_far, state_near):
    state = (state0[...] + state1[...]) + (state2[...] + state3[...])
    mine = slots[slot()]
    state_far[...], state_near[...] = by_side(state[CHUNK // 2 :], state[: CHUNK // 2])
    for c in range(2):
        far[c] = wave_far[c] + mine[5 + c : 6 + c][None] * state_far[...]
        near[c] = wave_near[c] + mine[5 + c : 6 + c][None] * state_near[...]


def inner_kernel(ops, lows, scale, inverse, far, near, edges, iterate, source):
    middle = slice(HALO, HALO + CHUNK)
    for i, part in enumerate(by_side(near[...], far[...])):
        start(inverse, part, source, slice((i + 1) * HALO, (i + 2) * HALO))
    iterate[...] = source[:, middle]
    for sweep in range(SWEEPS):
        lo, hi = sweep, CHUNK - sweep
        if sweep:
            here = slice(HALO + lo, HALO + hi)
            coupled = [couple(ops, lows, scale[here], iterate[c, lo - 1 : hi + 1]) for c in range(2)]
            fresh = damped(iterate[:, lo:hi], source[:, here], inverse[:, here], coupled)
            iterate[0, lo:hi] = fresh[0]
            iterate[1, lo:hi] = fresh[1]
        edges[sweep, :, :2] = iterate[:, lo : lo + 2]
        edges[sweep, :, 2:] = iterate[:, hi - 2 : hi]


def outer_kernel(
    slots, ops, lows, scale, inverse, far, near, wave_far, state_far, wave_near, state_near, edges, before,
    out, iterate, source,
):
    mine = slots[slot()]

    def sides(wave, state):
        return jnp.stack([wave[c] + mine[5 + c : 6 + c][None] * state[...] for c in range(2)])

    left, right = by_side(near[...], far[...])
    west, east = by_side(sides(wave_near, state_near), sides(wave_far, state_far))
    for i, part in enumerate((west, left, right, east)):
        start(inverse, part, source, slice(i * HALO, (i + 1) * HALO))
    out[:, :8, :] = before[...]
    reach = SWEEPS - 1
    iterate[:, :reach] = source[:, 1:HALO]
    iterate[:, reach + 4 :] = source[:, HALO + CHUNK : WINDOW - 1]
    for sweep in range(1, SWEEPS):
        iterate[:, reach : reach + 4] = edges[sweep - 1]
        one = slice(sweep + 1, HALO + sweep)
        two = slice(WINDOW - HALO - sweep, WINDOW - 1 - sweep)
        sides = [
            jnp.concatenate((ref[one], ref[HALO : HALO + 2], ref[two]), axis=0)
            for ref in [scale] + [inverse.at[i] for i in range(3)] + [source.at[i] for i in range(2)]
        ]
        coupled = [couple(ops, lows, sides[0], iterate[c]) for c in range(2)]
        fresh = damped(iterate[:, 1:-1], sides[4:], sides[1:4], coupled)
        for c in range(2):
            iterate[c, :reach] = fresh[c][:reach]
            iterate[c, reach + 4 :] = fresh[c][reach + 2 :]
    last = edges.at[SWEEPS - 1]
    for xc in range(8):
        for col in range(2):
            x = 2 * xc + col
            for c in range(2):
                if x < reach:
                    tile = iterate.at[c, x]
                elif x < reach + 2:
                    tile = last.at[c, x - reach]
                else:
                    tile = iterate.at[c, x + 2]
                at = 8 + c * 4 + col * 2
                for yd in range(4):
                    out[seat(xc, yd), at : at + 2, :] = tile[2 * yd : 2 * yd + 2, :]


def backward_kernel(table, got, out):
    parts = []
    for p in range(8):
        at = (p // 4) * 8 + p % 4
        halves = [got[pl.ds(at + 4 * c, FREQS, stride=16), :] for c in range(2)]
        parts.append(jnp.concatenate(halves, axis=0))
    slices = transform(table, parts)
    for p in range(8):
        out[pl.ds(p, STEPS, stride=8), :] = slices[:, p * LANES : (p + 1) * LANES]


def unpack_kernel(got, out, flip, held, sems):
    copies = []
    for s in range(2):
        for r in range(2):
            for c in range(2):
                flip[pl.ds(c, STEPS, stride=2), :] = got[pl.ds(s * 4 + c * 2 + r, STEPS, stride=8), :]
            held[s, 0, :, r, :] = flip[...].T[:NB, :]
        copies.append(pltpu.make_async_copy(held.at[s], out.at[s], sems.at[s]))
        copies[s].start()
    for copy in copies:
        copy.wait()


def call(kernel, outs, ins, scratch=(), specs=None, name=None, params=PARAMS, out=VMEM, cost=None):
    return pl.pallas_call(
        kernel,
        out_shape=outs,
        in_specs=specs or [VMEM] * len(ins),
        out_specs=jax.tree.map(lambda _: out, outs),
        scratch_shapes=scratch,
        compiler_params=params,
        cost_estimate=cost,
        name=name,
    )(*ins)


def f32(*shape):
    return jax.ShapeDtypeStruct(shape, jnp.float32)


def exchange(blocks, axes):
    return lax.all_to_all(blocks, axes, 0, 0, tiled=True)


def swapped(block, axis, bits):
    return lax.ppermute(block, axis, [(i, i ^ bits) for i in range(lax.axis_size(axis))])


def per_device(forcing, init_state, elem_scale, vol_op, face_ops):
    square = pltpu.VMEM((LANES, LANES), jnp.float32)
    window = (WINDOW, 8, LANES)
    inputs = (
        forcing.reshape(2 * NB, 2, LANES),
        init_state.reshape(1, NB, 2, LANES),
        elem_scale.reshape(1, 2, LANES),
        vol_op.reshape(1, NB, NB),
        jnp.transpose(face_ops, (1, 0, 2)),
    )
    packed, ops, lows, diag = call(
        pack_kernel,
        (
            pltpu.VMEM((STEPS * 12, LANES), jnp.float32),
            pltpu.VMEM((2 * LANES, 6 * LANES), jnp.bfloat16),
            pltpu.VMEM((LANES, 4 * LANES), jnp.bfloat16),
            pltpu.VMEM((8, LANES), jnp.float32),
        ),
        inputs,
        [pltpu.VMEM(value.shape, jnp.float32) for value in inputs]
        + [square, square, pltpu.SemaphoreType.DMA((len(inputs),))],
        [HBM] * len(inputs),
        name="pack",
        params=pltpu.CompilerParams(vmem_limit_bytes=60 * 1024 * 1024),
    )
    by_point = exchange(packed.reshape(STEPS, 3, 4, LANES), TIME).reshape(STEPS * 12, LANES)
    waves = call(forward_kernel, f32(FREQS * 24, LANES), (FORWARD, by_point), name="forward")
    got = exchange(waves.reshape(FREQS, 24, LANES), PLANE)
    both = pltpu.VMEM((2,) + window, jnp.float32)
    solved, state, scale, inverse = call(
        first_kernel,
        (f32(2, CHUNK, 8, LANES), f32(CHUNK, 8, LANES), f32(*window), f32(3, *window)),
        (SLOTS, ops, lows, diag, got),
        (both, both),
        name="first",
    )
    half = f32(2, CHUNK // 2, 8, LANES)
    state = state + swapped(state, "core", 1)
    planes = lax.axis_size("z")
    other = [(z, (z + 1 if z % 2 else z - 1) % planes) for z in range(planes)]
    done, wave_far, wave_near = call(
        between_kernel,
        (f32(FREQS, 8, LANES), half, half),
        (got, solved, state),
        (pltpu.VMEM(half.shape, jnp.float32), pltpu.VMEM(half.shape, jnp.float32)),
        [VMEM, VMEM, ANY],
        name="between",
    )
    beyond_wave_far = lax.ppermute(wave_far, "z", other)
    beyond_wave_near = swapped(wave_near, "z", 1)
    one, three, two = (swapped(state, "y", bits) for bits in (1, 3, 2))
    state = ((state + one) + three) + two
    states = [state] + [swapped(state, "x", bits) for bits in (1, 3, 2)]
    part = f32(CHUNK // 2, 8, LANES)
    far, near, state_far, state_near = call(
        carry_kernel, (half, half, part, part), (SLOTS, wave_far, wave_near, *states), name="carry"
    )
    beyond_far = lax.ppermute(state_far, "z", other)
    beyond_near = swapped(state_near, "z", 1)
    edges = call(
        inner_kernel,
        f32(SWEEPS, 2, 4, 8, LANES),
        (ops, lows, scale, inverse, far, near),
        (pltpu.VMEM((2, CHUNK, 8, LANES), jnp.float32), both),
        name="inner",
        cost=pl.CostEstimate(flops=2_000_000_000, bytes_accessed=1_000_000, transcendentals=0),
    )
    done = call(
        outer_kernel,
        f32(FREQS, 16, LANES),
        (SLOTS, ops, lows, scale, inverse, far, near, beyond_wave_far, beyond_far, beyond_wave_near, beyond_near, edges, done),
        (pltpu.VMEM((2, 2 * SWEEPS + 2, 8, LANES), jnp.float32), both),
        name="outer",
    )
    got = exchange(done, PLANE).reshape(FREQS * 16, LANES)
    slices = call(backward_kernel, f32(STEPS * 8, LANES), (BACKWARD, got), name="backward")
    by_column = exchange(slices.reshape(STEPS, 8, LANES), TIME).reshape(STEPS * 8, LANES)
    result = f32(2, 1, NB, 2, LANES)
    return call(
        unpack_kernel,
        result,
        (by_column,),
        (square, pltpu.VMEM(result.shape, jnp.float32), pltpu.SemaphoreType.DMA((2,))),
        name="unpack",
        out=ANY,
    )


def solution(mesh):
    grid = Mesh(mesh.devices.reshape(8, 4, 2, 4), ("z", "x", "core", "y"))
    return jax.shard_map(
        per_device,
        mesh=grid,
        in_specs=(
            P(None, TIME, None, "y", None),
            P(None, "y", None),
            P("y", None),
            P(),
            P(),
        ),
        out_specs=P(None, TIME, None, "y", None),
        check_vma=False,
    )
```

```python
import math

import jax
import jax.numpy as jnp
import ml_dtypes
import numpy as np
from jax import lax
from jax.experimental import pallas as pl
from jax.experimental.pallas import tpu as pltpu
from jax.sharding import Mesh
from jax.sharding import PartitionSpec as P

NB = 125
SWEEPS = 8
STEPS = 64
LANES = 128
FREQS = STEPS // 2
CHUNK = 16
WINDOW = 32
HALO = 8
INNER = 4
ES_LANE = NB

circ_alpha = 0.01
damping = 0.7

TIME = ("z", "x", "core")
PLANE = ("core", "y", "x")


def tables():
    n = np.arange(STEPS)
    log_alpha = math.log(circ_alpha)
    grow = np.exp(n * (log_alpha / STEPS))
    forward = np.zeros((STEPS, STEPS))
    backward = np.zeros((STEPS, STEPS))
    shifts = np.zeros((FREQS, 4))
    root = math.exp(log_alpha / STEPS)
    forward[0] = 1.0
    forward[1] = (-1.0) ** n
    backward[:, 0] = 1.0
    backward[:, 1] = (-1.0) ** n
    shifts[0] = (1.0 - root, 1.0 + root, 0.0, 0.0)
    for k in range(1, FREQS):
        angle = 2.0 * math.pi * ((k * n) % STEPS) / STEPS
        forward[2 * k] = np.cos(angle)
        forward[2 * k + 1] = -np.sin(angle)
        backward[:, 2 * k] = 2.0 * np.cos(angle)
        backward[:, 2 * k + 1] = -2.0 * np.sin(angle)
        theta = 2.0 * math.pi * k / STEPS
        shifts[k, :3] = (1.0 - root * math.cos(theta), 1.0 - root * math.cos(theta), root * math.sin(theta))
    forward = forward * grow[None, :]
    backward = backward / grow[:, None] / STEPS
    carry = 0.5 * forward.sum(1) + forward[:, 0]
    last = backward[STEPS - 1]
    return tuple(a.astype(np.float32) for a in (forward, backward, shifts, carry, last))


def in_parts(table):
    high = table.astype(ml_dtypes.bfloat16)
    rest = table - high.astype(np.float32)
    middle = rest.astype(ml_dtypes.bfloat16)
    low = (rest - middle.astype(np.float32)).astype(ml_dtypes.bfloat16)
    return np.concatenate((high, high, middle, high, middle, low), axis=1)


FORWARD, BACKWARD, SHIFTS, CARRY, LAST = tables()
BY_PART = np.concatenate((np.arange(0, STEPS, 2), np.arange(1, STEPS, 2)))
FORWARD = in_parts(FORWARD[BY_PART])
BACKWARD = in_parts(BACKWARD[:, BY_PART])
SLOTS = np.concatenate((SHIFTS[:, :3], LAST.reshape(FREQS, 2), CARRY.reshape(FREQS, 2), SHIFTS[:, :1]), axis=1)
SLOTS = np.repeat(SLOTS[:, :, None], LANES, axis=2)

VMEM = pl.BlockSpec(memory_space=pltpu.VMEM)
HBM = pl.BlockSpec(memory_space=pltpu.HBM)
ANY = pl.BlockSpec(memory_space=pl.ANY)
PARAMS = pltpu.CompilerParams(vmem_limit_bytes=32 * 1024 * 1024)


def split(value):
    high = value.astype(jnp.bfloat16)
    return high, (value - high.astype(jnp.float32)).astype(jnp.bfloat16)


def transform(table, parts):
    whole = jnp.concatenate(parts, axis=1)
    high = whole.astype(jnp.bfloat16)
    middle, low = split(whole - high.astype(jnp.float32))
    stack = jnp.concatenate((high, middle, high, low, middle, high), axis=0)
    return jnp.dot(table[...], stack, preferred_element_type=jnp.float32)


def pack_kernel(
    forcing, init, scale, vol, faces, out, ops, lows, diag, value, state, elems, volume, sides, rows, flip, sems
):
    copies = [
        pltpu.make_async_copy(ref, into, sems.at[i])
        for i, (ref, into) in enumerate(
            ((vol, volume), (faces, sides), (forcing, value), (init, state), (scale, elems))
        )
    ]
    for copy in copies:
        copy.start()
    step = lax.axis_index("z") * 8 + lax.axis_index("x") * 2 + lax.axis_index("core")
    weight = jnp.where(step == 0, 1.5, 0.5).astype(jnp.float32)
    flip[...] = jnp.zeros((LANES, LANES), jnp.float32)
    rows[NB:, :] = jnp.zeros((LANES - NB, LANES), jnp.float32)
    for copy in copies[:2]:
        copy.wait()
    row = lax.broadcasted_iota(jnp.int32, (LANES, LANES), 0)
    col = lax.broadcasted_iota(jnp.int32, (LANES, LANES), 1)
    for op in range(5):
        flip[:NB, :NB] = volume[0] if op == 0 else sides[:, op - 1, :]
        square = flip[...]
        if op == 0:
            on = jnp.where(row == col, square, 0.0)
            diag[...] = jnp.broadcast_to(jnp.sum(on, axis=0, keepdims=True), (8, LANES))
            square = square - on
        square = square.T
        high, low = split(square)
        if op == 0:
            here, rest = 4 * LANES, ops.at[:LANES, 5 * LANES :]
        else:
            here = (op - 1) * LANES
            rest = lows.at[:, here : here + LANES]
        ops[:LANES, here : here + LANES] = high
        ops[LANES:, here : here + LANES] = high
        rest[...] = low
    ops[LANES:, 5 * LANES :] = jnp.zeros((LANES, LANES), jnp.bfloat16)
    for copy in copies[2:]:
        copy.wait()
    for s in (1, 0):
        for r in range(2):
            if s == 0:
                rows[:NB, :] = value[s * NB : (s + 1) * NB, r, :] + weight * state[0, :, r, :]
                rows[ES_LANE : ES_LANE + 1, :] = elems[0, r : r + 1, :]
            else:
                rows[:NB, :] = value[s * NB : (s + 1) * NB, r, :]
            flip[...] = rows[...].T
            for c in range(2):
                out[pl.ds(s * 8 + c * 2 + r, STEPS, stride=12), :] = flip[pl.ds(c, STEPS, stride=2), :]
    blank = jnp.zeros((4, LANES), jnp.float32)
    for m in range(STEPS):
        source = m - 4 if m % 8 < 4 else m + 4
        at = m * 12 + 4
        if 0 <= source < STEPS:
            out[at : at + 4, :] = out[source * 12 : source * 12 + 4, :]
        else:
            out[at : at + 4, :] = blank


def forward_kernel(table, got, out):
    lane = lax.broadcasted_iota(jnp.int32, (STEPS, LANES), 1)
    parts = [got[pl.ds(p, STEPS, stride=12), :] for p in range(12)]
    waves = transform(table, parts)
    for p in range(12):
        wave = waves[:, p * LANES : (p + 1) * LANES]
        if p < 8:
            wave = jnp.where(lane == ES_LANE, jnp.broadcast_to(parts[p][:1, :], wave.shape), wave)
        for c in range(2):
            at = c * 8 + p if p < 8 else 16 + c * 4 + p - 8
            out[pl.ds(at, FREQS, stride=24), :] = wave[c * FREQS : (c + 1) * FREQS]


def slot():
    return lax.axis_index("core") * 16 + lax.axis_index("y") * 4 + lax.axis_index("x")


def seat(xc, yd):
    return xc % 2 * 16 + yd * 4 + xc // 2


def invert(slots, diag, scale, inverse):
    mine = slots[slot()]
    shape = (WINDOW, 8, LANES)
    place = lax.axis_index("z") * CHUNK - HALO + lax.broadcasted_iota(jnp.int32, shape, 0)
    inside = jnp.logical_and(place >= 0, place < 8 * CHUNK)
    scaled = scale[...] * diag[...][None]
    im = mine[2:3][None]
    re0 = mine[0:1][None] + scaled
    re1 = mine[1:2][None] + scaled
    mod0 = jnp.where(inside, damping / (re0 * re0 + im * im), 0.0)
    mod1 = jnp.where(inside, damping / (re1 * re1 + im * im), 0.0)
    inverse[0] = re0 * mod0
    inverse[1] = re1 * mod1
    inverse[2] = im * mod0


def start(inverse, field, source, at):
    lane = lax.broadcasted_iota(jnp.int32, field.shape[1:], 2)
    g0 = jnp.where(lane < NB, field[0], 0.0)
    g1 = jnp.where(lane < NB, field[1], 0.0)
    source[0, at] = inverse[0, at] * g0 + inverse[2, at] * g1
    source[1, at] = inverse[1, at] * g1 - inverse[2, at] * g0


def couple(ops, lows, scale, field):
    wide = field.shape[0]
    inner = (wide - 2, 8, LANES)
    high, low = split(field.reshape(wide * 8, LANES))
    both = jnp.concatenate((high, low), axis=1)

    def product(left, right):
        return jnp.dot(left, right, preferred_element_type=jnp.float32)

    def columns(sums, i):
        return sums[:, i * LANES : (i + 1) * LANES].reshape(-1, 8, LANES)

    own = product(both[8:-8], ops[:, 4 * LANES :])
    along = product(both, ops[:, : 2 * LANES]) + product(high, lows[:, : 2 * LANES])
    across = product(both[8:-8], ops[:, 2 * LANES : 4 * LANES]) + product(high[8:-8], lows[:, 2 * LANES :])
    return (
        scale * (columns(own, 0) + columns(own, 1))
        + columns(along, 0)[:-2]
        + columns(along, 1)[2:]
        + pltpu.roll(columns(across, 0), 1, 1)
        + pltpu.roll(columns(across, 1), 7, 1)
    )


def damped(field, source, inverse, coupled):
    keep = 1.0 - damping
    return (
        keep * field[0] + source[0] - inverse[0] * coupled[0] - inverse[2] * coupled[1],
        keep * field[1] + source[1] - inverse[1] * coupled[1] + inverse[2] * coupled[0],
    )


def relax(ops, lows, scale, inverse, iterate, source, done):
    for sweep in range(done, SWEEPS):
        here = slice(sweep + 1, WINDOW - sweep - 1)
        coupled = [couple(ops, lows, scale[here], iterate[c, sweep : WINDOW - sweep]) for c in range(2)]
        fresh = damped(iterate[:, here], source[:, here], inverse[:, here], coupled)
        iterate[0, here] = fresh[0]
        iterate[1, here] = fresh[1]


def first_kernel(slots, ops, lows, diag, got, solved, state, scale, inverse, iterate, source):
    for xc in range(8):
        for yd in range(4):
            for c in range(2):
                for col in range(4):
                    w = HALO + 2 * xc + col
                    if col >= 2:
                        w = (2 * xc if xc < 4 else 16 + 2 * xc) + col - 2
                    at = c * 8 + col * 2
                    iterate[c, w, 2 * yd : 2 * yd + 2, :] = got[seat(xc, yd), at : at + 2, :]
    scale[...] = jnp.broadcast_to(iterate[0, :, :, ES_LANE : ES_LANE + 1], scale.shape)
    invert(slots, diag, scale, inverse)
    start(inverse, iterate[...], source, slice(0, WINDOW))
    iterate[...] = source[...]
    relax(ops, lows, scale, inverse, iterate, source, 1)
    mine = slots[slot()]
    middle = iterate[:, HALO : HALO + CHUNK]
    solved[...] = middle
    state[...] = mine[3:4][None] * middle[0] + mine[4:5][None] * middle[1]


def between_kernel(got, solved, after, done, far, near, left, right):
    del after
    for c in range(2):
        for xc in range(8):
            side = left if xc < 4 else right
            for yd in range(4):
                for col in range(2):
                    rows = slice(2 * yd, 2 * yd + 2)
                    at = c * 4 + col * 2
                    done[seat(xc, yd), at : at + 2, :] = solved[c, 2 * xc + col, rows, :]
                    side[c, 2 * (xc % 4) + col, rows, :] = got[seat(xc, yd), 16 + at : 18 + at, :]
    far[...], near[...] = by_side(right[...], left[...])


def by_side(one, two):
    even = lax.rem(lax.axis_index("z"), 2) == 0
    return jnp.where(even, two, one), jnp.where(even, one, two)


def carry_kernel(slots, wave_far, wave_near, state0, state1, state2, state3, far, near, state_far, state_near):
    state = (state0[...] + state1[...]) + (state2[...] + state3[...])
    mine = slots[slot()]
    state_far[...], state_near[...] = by_side(state[CHUNK // 2 :], state[: CHUNK // 2])
    for c in range(2):
        far[c] = wave_far[c] + mine[5 + c : 6 + c][None] * state_far[...]
        near[c] = wave_near[c] + mine[5 + c : 6 + c][None] * state_near[...]


def inner_kernel(ops, lows, scale, inverse, far, near, edges, core, iterate, source):
    middle = slice(HALO, HALO + CHUNK)
    for i, part in enumerate(by_side(near[...], far[...])):
        start(inverse, part, source, slice((i + 1) * HALO, (i + 2) * HALO))
    iterate[...] = source[:, middle]
    for sweep in range(INNER + 1):
        lo, hi = sweep, CHUNK - sweep
        if sweep:
            here = slice(HALO + lo, HALO + hi)
            coupled = [couple(ops, lows, scale[here], iterate[c, lo - 1 : hi + 1]) for c in range(2)]
            fresh = damped(iterate[:, lo:hi], source[:, here], inverse[:, here], coupled)
            iterate[0, lo:hi] = fresh[0]
            iterate[1, lo:hi] = fresh[1]
        if sweep < INNER:
            edges[sweep, :, :2] = iterate[:, lo : lo + 2]
            edges[sweep, :, 2:] = iterate[:, hi - 2 : hi]
    core[...] = iterate[:, INNER : CHUNK - INNER]


def outer_kernel(
    slots, ops, lows, scale, inverse, far, near, wave_far, state_far, wave_near, state_near, edges, core, before,
    out, sides, iterate, source,
):
    mine = slots[slot()]

    def halo(wave, state):
        return jnp.stack([wave[c] + mine[5 + c : 6 + c][None] * state[...] for c in range(2)])

    left, right = by_side(near[...], far[...])
    west, east = by_side(halo(wave_near, state_near), halo(wave_far, state_far))
    for i, part in enumerate((west, left, right, east)):
        start(inverse, part, source, slice(i * HALO, (i + 1) * HALO))
    out[:, :8, :] = before[...]
    reach = HALO - 1
    sides[:, :reach] = source[:, 1:HALO]
    sides[:, reach + 4 :] = source[:, HALO + CHUNK : WINDOW - 1]
    for sweep in range(1, INNER + 1):
        sides[:, reach : reach + 4] = edges[sweep - 1]
        one = slice(sweep + 1, HALO + sweep)
        two = slice(WINDOW - HALO - sweep, WINDOW - 1 - sweep)
        given = [
            jnp.concatenate((ref[one], ref[HALO : HALO + 2], ref[two]), axis=0)
            for ref in [scale] + [inverse.at[i] for i in range(3)] + [source.at[i] for i in range(2)]
        ]
        coupled = [couple(ops, lows, given[0], sides[c]) for c in range(2)]
        fresh = damped(sides[:, 1:-1], given[4:], given[1:4], coupled)
        for c in range(2):
            sides[c, :reach] = fresh[c][:reach]
            sides[c, reach + 4 :] = fresh[c][reach + 2 :]
    iterate[:, INNER + 1 : HALO + INNER] = sides[:, :reach]
    iterate[:, HALO + INNER : WINDOW - HALO - INNER] = core[...]
    iterate[:, WINDOW - HALO - INNER : WINDOW - 1 - INNER] = sides[:, reach + 4 :]
    relax(ops, lows, scale, inverse, iterate, source, INNER + 1)
    for xc in range(8):
        for yd in range(4):
            for c in range(2):
                for col in range(2):
                    at = 8 + c * 4 + col * 2
                    out[seat(xc, yd), at : at + 2, :] = iterate[c, HALO + 2 * xc + col, 2 * yd : 2 * yd + 2, :]


def backward_kernel(table, got, out):
    parts = []
    for p in range(8):
        at = (p // 4) * 8 + p % 4
        halves = [got[pl.ds(at + 4 * c, FREQS, stride=16), :] for c in range(2)]
        parts.append(jnp.concatenate(halves, axis=0))
    slices = transform(table, parts)
    for p in range(8):
        out[pl.ds(p, STEPS, stride=8), :] = slices[:, p * LANES : (p + 1) * LANES]


def unpack_kernel(got, out, flip, held, sems):
    copies = []
    for s in range(2):
        for r in range(2):
            for c in range(2):
                flip[pl.ds(c, STEPS, stride=2), :] = got[pl.ds(s * 4 + c * 2 + r, STEPS, stride=8), :]
            held[s, 0, :, r, :] = flip[...].T[:NB, :]
        copies.append(pltpu.make_async_copy(held.at[s], out.at[s], sems.at[s]))
        copies[s].start()
    for copy in copies:
        copy.wait()


def call(kernel, outs, ins, scratch=(), specs=None, name=None, params=PARAMS, out=VMEM, cost=None):
    return pl.pallas_call(
        kernel,
        out_shape=outs,
        in_specs=specs or [VMEM] * len(ins),
        out_specs=jax.tree.map(lambda _: out, outs),
        scratch_shapes=scratch,
        compiler_params=params,
        cost_estimate=cost,
        name=name,
    )(*ins)


def f32(*shape):
    return jax.ShapeDtypeStruct(shape, jnp.float32)


def exchange(blocks, axes):
    return lax.all_to_all(blocks, axes, 0, 0, tiled=True)


def swapped(block, axis, bits):
    return lax.ppermute(block, axis, [(i, i ^ bits) for i in range(lax.axis_size(axis))])


def per_device(forcing, init_state, elem_scale, vol_op, face_ops):
    square = pltpu.VMEM((LANES, LANES), jnp.float32)
    window = (WINDOW, 8, LANES)
    inputs = (
        forcing.reshape(2 * NB, 2, LANES),
        init_state.reshape(1, NB, 2, LANES),
        elem_scale.reshape(1, 2, LANES),
        vol_op.reshape(1, NB, NB),
        jnp.transpose(face_ops, (1, 0, 2)),
    )
    packed, ops, lows, diag = call(
        pack_kernel,
        (
            pltpu.VMEM((STEPS * 12, LANES), jnp.float32),
            pltpu.VMEM((2 * LANES, 6 * LANES), jnp.bfloat16),
            pltpu.VMEM((LANES, 4 * LANES), jnp.bfloat16),
            pltpu.VMEM((8, LANES), jnp.float32),
        ),
        inputs,
        [pltpu.VMEM(value.shape, jnp.float32) for value in inputs]
        + [square, square, pltpu.SemaphoreType.DMA((len(inputs),))],
        [HBM] * len(inputs),
        name="pack",
        params=pltpu.CompilerParams(vmem_limit_bytes=60 * 1024 * 1024),
    )
    by_point = exchange(packed.reshape(STEPS, 3, 4, LANES), TIME).reshape(STEPS * 12, LANES)
    waves = call(forward_kernel, f32(FREQS * 24, LANES), (FORWARD, by_point), name="forward")
    got = exchange(waves.reshape(FREQS, 24, LANES), PLANE)
    both = pltpu.VMEM((2,) + window, jnp.float32)
    solved, state, scale, inverse = call(
        first_kernel,
        (f32(2, CHUNK, 8, LANES), f32(CHUNK, 8, LANES), f32(*window), f32(3, *window)),
        (SLOTS, ops, lows, diag, got),
        (both, both),
        name="first",
    )
    half = f32(2, CHUNK // 2, 8, LANES)
    state = state + swapped(state, "core", 1)
    planes = lax.axis_size("z")
    other = [(z, (z + 1 if z % 2 else z - 1) % planes) for z in range(planes)]
    done, wave_far, wave_near = call(
        between_kernel,
        (f32(FREQS, 8, LANES), half, half),
        (got, solved, state),
        (pltpu.VMEM(half.shape, jnp.float32), pltpu.VMEM(half.shape, jnp.float32)),
        [VMEM, VMEM, ANY],
        name="between",
    )
    beyond_wave_far = lax.ppermute(wave_far, "z", other)
    beyond_wave_near = swapped(wave_near, "z", 1)
    one, three, two = (swapped(state, "y", bits) for bits in (1, 3, 2))
    state = ((state + one) + three) + two
    states = [state] + [swapped(state, "x", bits) for bits in (1, 3, 2)]
    part = f32(CHUNK // 2, 8, LANES)
    far, near, state_far, state_near = call(
        carry_kernel, (half, half, part, part), (SLOTS, wave_far, wave_near, *states), name="carry"
    )
    beyond_far = lax.ppermute(state_far, "z", other)
    beyond_near = swapped(state_near, "z", 1)
    edges, core = call(
        inner_kernel,
        (f32(INNER, 2, 4, 8, LANES), f32(2, CHUNK - 2 * INNER, 8, LANES)),
        (ops, lows, scale, inverse, far, near),
        (pltpu.VMEM((2, CHUNK, 8, LANES), jnp.float32), both),
        name="inner",
        cost=pl.CostEstimate(flops=2_000_000_000, bytes_accessed=1_000_000, transcendentals=0),
    )
    done = call(
        outer_kernel,
        f32(FREQS, 16, LANES),
        (SLOTS, ops, lows, scale, inverse, far, near, beyond_wave_far, beyond_far, beyond_wave_near, beyond_near, edges, core, done),
        (pltpu.VMEM((2, 2 * HALO + 2, 8, LANES), jnp.float32), both, both),
        name="outer",
    )
    got = exchange(done, PLANE).reshape(FREQS * 16, LANES)
    slices = call(backward_kernel, f32(STEPS * 8, LANES), (BACKWARD, got), name="backward")
    by_column = exchange(slices.reshape(STEPS, 8, LANES), TIME).reshape(STEPS * 8, LANES)
    result = f32(2, 1, NB, 2, LANES)
    return call(
        unpack_kernel,
        result,
        (by_column,),
        (square, pltpu.VMEM(result.shape, jnp.float32), pltpu.SemaphoreType.DMA((2,))),
        name="unpack",
        out=ANY,
    )


def solution(mesh):
    grid = Mesh(mesh.devices.reshape(8, 4, 2, 4), ("z", "x", "core", "y"))
    return jax.shard_map(
        per_device,
        mesh=grid,
        in_specs=(
            P(None, TIME, None, "y", None),
            P(None, "y", None),
            P("y", None),
            P(),
            P(),
        ),
        out_specs=P(None, TIME, None, "y", None),
        check_vma=False,
    )
```

```python
import math

import jax
import jax.numpy as jnp
import ml_dtypes
import numpy as np
from jax import lax
from jax.experimental import pallas as pl
from jax.experimental.pallas import tpu as pltpu
from jax.sharding import Mesh
from jax.sharding import PartitionSpec as P

NB = 125
SWEEPS = 8
STEPS = 64
LANES = 128
FREQS = STEPS // 2
CHUNK = 16
WINDOW = 32
HALO = 8
INNER = 4
ES_LANE = NB

circ_alpha = 0.01
damping = 0.7

TIME = ("z", "x", "core")
PLANE = ("core", "y", "x")


def tables():
    n = np.arange(STEPS)
    log_alpha = math.log(circ_alpha)
    grow = np.exp(n * (log_alpha / STEPS))
    forward = np.zeros((STEPS, STEPS))
    backward = np.zeros((STEPS, STEPS))
    shifts = np.zeros((FREQS, 4))
    root = math.exp(log_alpha / STEPS)
    forward[0] = 1.0
    forward[1] = (-1.0) ** n
    backward[:, 0] = 1.0
    backward[:, 1] = (-1.0) ** n
    shifts[0] = (1.0 - root, 1.0 + root, 0.0, 0.0)
    for k in range(1, FREQS):
        angle = 2.0 * math.pi * ((k * n) % STEPS) / STEPS
        forward[2 * k] = np.cos(angle)
        forward[2 * k + 1] = -np.sin(angle)
        backward[:, 2 * k] = 2.0 * np.cos(angle)
        backward[:, 2 * k + 1] = -2.0 * np.sin(angle)
        theta = 2.0 * math.pi * k / STEPS
        shifts[k, :3] = (1.0 - root * math.cos(theta), 1.0 - root * math.cos(theta), root * math.sin(theta))
    forward = forward * grow[None, :]
    backward = backward / grow[:, None] / STEPS
    carry = 0.5 * forward.sum(1) + forward[:, 0]
    last = backward[STEPS - 1]
    return tuple(a.astype(np.float32) for a in (forward, backward, shifts, carry, last))


def in_parts(table):
    high = table.astype(ml_dtypes.bfloat16)
    rest = table - high.astype(np.float32)
    middle = rest.astype(ml_dtypes.bfloat16)
    low = (rest - middle.astype(np.float32)).astype(ml_dtypes.bfloat16)
    return np.concatenate((high, high, middle, high, middle, low), axis=1)


FORWARD, BACKWARD, SHIFTS, CARRY, LAST = tables()
BY_PART = np.concatenate((np.arange(0, STEPS, 2), np.arange(1, STEPS, 2)))
FORWARD = in_parts(FORWARD[BY_PART])
BACKWARD = in_parts(BACKWARD[:, BY_PART])
SLOTS = np.concatenate((SHIFTS[:, :3], LAST.reshape(FREQS, 2), CARRY.reshape(FREQS, 2), SHIFTS[:, :1]), axis=1)
SLOTS = np.repeat(SLOTS[:, :, None], LANES, axis=2)

VMEM = pl.BlockSpec(memory_space=pltpu.VMEM)
HBM = pl.BlockSpec(memory_space=pltpu.HBM)
ANY = pl.BlockSpec(memory_space=pl.ANY)
PARAMS = pltpu.CompilerParams(vmem_limit_bytes=32 * 1024 * 1024)


def split(value):
    high = value.astype(jnp.bfloat16)
    return high, (value - high.astype(jnp.float32)).astype(jnp.bfloat16)


def transform(table, parts):
    whole = jnp.concatenate(parts, axis=1)
    high = whole.astype(jnp.bfloat16)
    middle, low = split(whole - high.astype(jnp.float32))
    stack = jnp.concatenate((high, middle, high, low, middle, high), axis=0)
    return jnp.dot(table[...], stack, preferred_element_type=jnp.float32)


def pack_kernel(
    forcing, init, scale, vol, faces, out, ops, lows, diag, value, state, elems, volume, sides, rows, flip, sems
):
    copies = [
        pltpu.make_async_copy(ref, into, sems.at[i])
        for i, (ref, into) in enumerate(
            ((vol, volume), (faces, sides), (forcing, value), (init, state), (scale, elems))
        )
    ]
    for copy in copies:
        copy.start()
    step = lax.axis_index("z") * 8 + lax.axis_index("x") * 2 + lax.axis_index("core")
    weight = jnp.where(step == 0, 1.5, 0.5).astype(jnp.float32)
    flip[...] = jnp.zeros((LANES, LANES), jnp.float32)
    rows[NB:, :] = jnp.zeros((LANES - NB, LANES), jnp.float32)
    for copy in copies[:2]:
        copy.wait()
    row = lax.broadcasted_iota(jnp.int32, (LANES, LANES), 0)
    col = lax.broadcasted_iota(jnp.int32, (LANES, LANES), 1)
    for op in range(5):
        flip[:NB, :NB] = volume[0] if op == 0 else sides[:, op - 1, :]
        square = flip[...]
        if op == 0:
            on = jnp.where(row == col, square, 0.0)
            diag[...] = jnp.broadcast_to(jnp.sum(on, axis=0, keepdims=True), (8, LANES))
            square = square - on
        square = square.T
        high, low = split(square)
        if op == 0:
            here, rest = 4 * LANES, ops.at[:LANES, 5 * LANES :]
        else:
            here = (op - 1) * LANES
            rest = lows.at[:, here : here + LANES]
        ops[:LANES, here : here + LANES] = high
        ops[LANES:, here : here + LANES] = high
        rest[...] = low
    ops[LANES:, 5 * LANES :] = jnp.zeros((LANES, LANES), jnp.bfloat16)
    for copy in copies[2:]:
        copy.wait()
    for s in (1, 0):
        for r in range(2):
            if s == 0:
                rows[:NB, :] = value[s * NB : (s + 1) * NB, r, :] + weight * state[0, :, r, :]
                rows[ES_LANE : ES_LANE + 1, :] = elems[0, r : r + 1, :]
            else:
                rows[:NB, :] = value[s * NB : (s + 1) * NB, r, :]
            flip[...] = rows[...].T
            for c in range(2):
                out[pl.ds(s * 8 + c * 2 + r, STEPS, stride=12), :] = flip[pl.ds(c, STEPS, stride=2), :]
    blank = jnp.zeros((4, LANES), jnp.float32)
    for m in range(STEPS):
        source = m - 4 if m % 8 < 4 else m + 4
        at = m * 12 + 4
        if 0 <= source < STEPS:
            out[at : at + 4, :] = out[source * 12 : source * 12 + 4, :]
        else:
            out[at : at + 4, :] = blank


def forward_kernel(table, got, out):
    lane = lax.broadcasted_iota(jnp.int32, (STEPS, LANES), 1)
    parts = [got[pl.ds(p, STEPS, stride=12), :] for p in range(12)]
    waves = transform(table, parts)
    for p in range(12):
        wave = waves[:, p * LANES : (p + 1) * LANES]
        if p < 8:
            wave = jnp.where(lane == ES_LANE, jnp.broadcast_to(parts[p][:1, :], wave.shape), wave)
        for c in range(2):
            at = c * 8 + p if p < 8 else 16 + c * 4 + p - 8
            out[pl.ds(at, FREQS, stride=24), :] = wave[c * FREQS : (c + 1) * FREQS]


def slot():
    return lax.axis_index("core") * 16 + lax.axis_index("y") * 4 + lax.axis_index("x")


def seat(xc, yd):
    return xc % 2 * 16 + yd * 4 + xc // 2


def invert(slots, diag, scale, inverse):
    mine = slots[slot()]
    shape = (WINDOW, 8, LANES)
    place = lax.axis_index("z") * CHUNK - HALO + lax.broadcasted_iota(jnp.int32, shape, 0)
    inside = jnp.logical_and(place >= 0, place < 8 * CHUNK)
    scaled = scale[...] * diag[...][None]
    im = mine[2:3][None]
    re0 = mine[0:1][None] + scaled
    re1 = mine[1:2][None] + scaled
    mod0 = jnp.where(inside, damping / (re0 * re0 + im * im), 0.0)
    mod1 = jnp.where(inside, damping / (re1 * re1 + im * im), 0.0)
    inverse[0] = re0 * mod0
    inverse[1] = re1 * mod1
    inverse[2] = im * mod0


def start(inverse, field, source, at):
    lane = lax.broadcasted_iota(jnp.int32, field.shape[1:], 2)
    g0 = jnp.where(lane < NB, field[0], 0.0)
    g1 = jnp.where(lane < NB, field[1], 0.0)
    source[0, at] = inverse[0, at] * g0 + inverse[2, at] * g1
    source[1, at] = inverse[1, at] * g1 - inverse[2, at] * g0


def couple(ops, lows, scale, field):
    wide = field.shape[0]
    inner = (wide - 2, 8, LANES)
    high, low = split(field.reshape(wide * 8, LANES))
    both = jnp.concatenate((high, low), axis=1)

    def product(left, right):
        return jnp.dot(left, right, preferred_element_type=jnp.float32)

    def columns(sums, i):
        return sums[:, i * LANES : (i + 1) * LANES].reshape(-1, 8, LANES)

    own = product(both[8:-8], ops[:, 4 * LANES :])
    along = product(both, ops[:, : 2 * LANES]) + product(high, lows[:, : 2 * LANES])
    across = product(both[8:-8], ops[:, 2 * LANES : 4 * LANES]) + product(high[8:-8], lows[:, 2 * LANES :])
    return (
        scale * (columns(own, 0) + columns(own, 1))
        + columns(along, 0)[:-2]
        + columns(along, 1)[2:]
        + pltpu.roll(columns(across, 0), 1, 1)
        + pltpu.roll(columns(across, 1), 7, 1)
    )


def damped(field, source, inverse, coupled):
    keep = 1.0 - damping
    return (
        keep * field[0] + source[0] - inverse[0] * coupled[0] - inverse[2] * coupled[1],
        keep * field[1] + source[1] - inverse[1] * coupled[1] + inverse[2] * coupled[0],
    )


def relax(ops, lows, scale, inverse, iterate, source, done):
    for sweep in range(done, SWEEPS):
        here = slice(sweep + 1, WINDOW - sweep - 1)
        coupled = [couple(ops, lows, scale[here], iterate[c, sweep : WINDOW - sweep]) for c in range(2)]
        fresh = damped(iterate[:, here], source[:, here], inverse[:, here], coupled)
        iterate[0, here] = fresh[0]
        iterate[1, here] = fresh[1]


def first_kernel(slots, ops, lows, diag, got, solved, state, scale, inverse, iterate, source):
    for xc in range(8):
        for yd in range(4):
            for c in range(2):
                for col in range(4):
                    w = HALO + 2 * xc + col
                    if col >= 2:
                        w = (2 * xc if xc < 4 else 16 + 2 * xc) + col - 2
                    at = c * 8 + col * 2
                    iterate[c, w, 2 * yd : 2 * yd + 2, :] = got[seat(xc, yd), at : at + 2, :]
    scale[...] = jnp.broadcast_to(iterate[0, :, :, ES_LANE : ES_LANE + 1], scale.shape)
    invert(slots, diag, scale, inverse)
    start(inverse, iterate[...], source, slice(0, WINDOW))
    iterate[...] = source[...]
    relax(ops, lows, scale, inverse, iterate, source, 1)
    mine = slots[slot()]
    middle = iterate[:, HALO : HALO + CHUNK]
    solved[...] = middle
    state[...] = mine[3:4][None] * middle[0] + mine[4:5][None] * middle[1]


def between_kernel(got, solved, after, done, far, near, left, right):
    del after
    for c in range(2):
        for xc in range(8):
            side = left if xc < 4 else right
            for yd in range(4):
                for col in range(2):
                    rows = slice(2 * yd, 2 * yd + 2)
                    at = c * 4 + col * 2
                    done[seat(xc, yd), at : at + 2, :] = solved[c, 2 * xc + col, rows, :]
                    side[c, 2 * (xc % 4) + col, rows, :] = got[seat(xc, yd), 16 + at : 18 + at, :]
    far[...], near[...] = by_side(right[...], left[...])


def by_side(one, two):
    even = lax.rem(lax.axis_index("z"), 2) == 0
    return jnp.where(even, two, one), jnp.where(even, one, two)


def carry_kernel(
    slots, wave_far, wave_near, state0, state1, state2, state3, early, far, near, state_far, state_near
):
    del early
    state = (state0[...] + state1[...]) + (state2[...] + state3[...])
    mine = slots[slot()]
    state_far[...], state_near[...] = by_side(state[CHUNK // 2 :], state[: CHUNK // 2])
    for c in range(2):
        far[c] = wave_far[c] + mine[5 + c : 6 + c][None] * state_far[...]
        near[c] = wave_near[c] + mine[5 + c : 6 + c][None] * state_near[...]


def inner_kernel(ops, lows, scale, inverse, far, near, edges, core, iterate, source):
    middle = slice(HALO, HALO + CHUNK)
    for i, part in enumerate(by_side(near[...], far[...])):
        start(inverse, part, source, slice((i + 1) * HALO, (i + 2) * HALO))
    iterate[...] = source[:, middle]
    for sweep in range(INNER + 1):
        lo, hi = sweep, CHUNK - sweep
        if sweep:
            here = slice(HALO + lo, HALO + hi)
            coupled = [couple(ops, lows, scale[here], iterate[c, lo - 1 : hi + 1]) for c in range(2)]
            fresh = damped(iterate[:, lo:hi], source[:, here], inverse[:, here], coupled)
            iterate[0, lo:hi] = fresh[0]
            iterate[1, lo:hi] = fresh[1]
        if sweep < INNER:
            edges[sweep, :, :2] = iterate[:, lo : lo + 2]
            edges[sweep, :, 2:] = iterate[:, hi - 2 : hi]
    core[...] = iterate[:, INNER : CHUNK - INNER]


def outer_kernel(
    slots, ops, lows, scale, inverse, far, near, wave_far, state_far, wave_near, state_near, edges, core, before,
    out, sides, iterate, source,
):
    mine = slots[slot()]

    def halo(wave, state):
        return jnp.stack([wave[c] + mine[5 + c : 6 + c][None] * state[...] for c in range(2)])

    left, right = by_side(near[...], far[...])
    west, east = by_side(halo(wave_near, state_near), halo(wave_far, state_far))
    for i, part in enumerate((west, left, right, east)):
        start(inverse, part, source, slice(i * HALO, (i + 1) * HALO))
    out[:, :8, :] = before[...]
    reach = HALO - 1
    sides[:, :reach] = source[:, 1:HALO]
    sides[:, reach + 4 :] = source[:, HALO + CHUNK : WINDOW - 1]
    for sweep in range(1, INNER + 1):
        sides[:, reach : reach + 4] = edges[sweep - 1]
        one = slice(sweep + 1, HALO + sweep)
        two = slice(WINDOW - HALO - sweep, WINDOW - 1 - sweep)
        given = [
            jnp.concatenate((ref[one], ref[HALO : HALO + 2], ref[two]), axis=0)
            for ref in [scale] + [inverse.at[i] for i in range(3)] + [source.at[i] for i in range(2)]
        ]
        coupled = [couple(ops, lows, given[0], sides[c]) for c in range(2)]
        fresh = damped(sides[:, 1:-1], given[4:], given[1:4], coupled)
        for c in range(2):
            sides[c, :reach] = fresh[c][:reach]
            sides[c, reach + 4 :] = fresh[c][reach + 2 :]
    iterate[:, INNER + 1 : HALO + INNER] = sides[:, :reach]
    iterate[:, HALO + INNER : WINDOW - HALO - INNER] = core[...]
    iterate[:, WINDOW - HALO - INNER : WINDOW - 1 - INNER] = sides[:, reach + 4 :]
    relax(ops, lows, scale, inverse, iterate, source, INNER + 1)
    for xc in range(8):
        for yd in range(4):
            for c in range(2):
                for col in range(2):
                    at = 8 + c * 4 + col * 2
                    out[seat(xc, yd), at : at + 2, :] = iterate[c, HALO + 2 * xc + col, 2 * yd : 2 * yd + 2, :]


def backward_kernel(table, got, out):
    parts = []
    for p in range(8):
        at = (p // 4) * 8 + p % 4
        halves = [got[pl.ds(at + 4 * c, FREQS, stride=16), :] for c in range(2)]
        parts.append(jnp.concatenate(halves, axis=0))
    slices = transform(table, parts)
    for p in range(8):
        out[pl.ds(p, STEPS, stride=8), :] = slices[:, p * LANES : (p + 1) * LANES]


def unpack_kernel(got, out, flip, held, sems):
    copies = []
    for s in range(2):
        for r in range(2):
            for c in range(2):
                flip[pl.ds(c, STEPS, stride=2), :] = got[pl.ds(s * 4 + c * 2 + r, STEPS, stride=8), :]
            held[s, 0, :, r, :] = flip[...].T[:NB, :]
        copies.append(pltpu.make_async_copy(held.at[s], out.at[s], sems.at[s]))
        copies[s].start()
    for copy in copies:
        copy.wait()


def call(kernel, outs, ins, scratch=(), specs=None, name=None, params=PARAMS, out=VMEM, cost=None):
    return pl.pallas_call(
        kernel,
        out_shape=outs,
        in_specs=specs or [VMEM] * len(ins),
        out_specs=jax.tree.map(lambda _: out, outs),
        scratch_shapes=scratch,
        compiler_params=params,
        cost_estimate=cost,
        name=name,
    )(*ins)


def f32(*shape):
    return jax.ShapeDtypeStruct(shape, jnp.float32)


def exchange(blocks, axes):
    return lax.all_to_all(blocks, axes, 0, 0, tiled=True)


def swapped(block, axis, bits):
    return lax.ppermute(block, axis, [(i, i ^ bits) for i in range(lax.axis_size(axis))])


def per_device(forcing, init_state, elem_scale, vol_op, face_ops):
    square = pltpu.VMEM((LANES, LANES), jnp.float32)
    window = (WINDOW, 8, LANES)
    inputs = (
        forcing.reshape(2 * NB, 2, LANES),
        init_state.reshape(1, NB, 2, LANES),
        elem_scale.reshape(1, 2, LANES),
        vol_op.reshape(1, NB, NB),
        jnp.transpose(face_ops, (1, 0, 2)),
    )
    packed, ops, lows, diag = call(
        pack_kernel,
        (
            pltpu.VMEM((STEPS * 12, LANES), jnp.float32),
            pltpu.VMEM((2 * LANES, 6 * LANES), jnp.bfloat16),
            pltpu.VMEM((LANES, 4 * LANES), jnp.bfloat16),
            pltpu.VMEM((8, LANES), jnp.float32),
        ),
        inputs,
        [pltpu.VMEM(value.shape, jnp.float32) for value in inputs]
        + [square, square, pltpu.SemaphoreType.DMA((len(inputs),))],
        [HBM] * len(inputs),
        name="pack",
        params=pltpu.CompilerParams(vmem_limit_bytes=60 * 1024 * 1024),
    )
    by_point = exchange(packed.reshape(STEPS, 3, 4, LANES), TIME).reshape(STEPS * 12, LANES)
    waves = call(forward_kernel, f32(FREQS * 24, LANES), (FORWARD, by_point), name="forward")
    got = exchange(waves.reshape(FREQS, 24, LANES), PLANE)
    both = pltpu.VMEM((2,) + window, jnp.float32)
    solved, state, scale, inverse = call(
        first_kernel,
        (f32(2, CHUNK, 8, LANES), f32(CHUNK, 8, LANES), f32(*window), f32(3, *window)),
        (SLOTS, ops, lows, diag, got),
        (both, both),
        name="first",
    )
    half = f32(2, CHUNK // 2, 8, LANES)
    state = state + swapped(state, "core", 1)
    planes = lax.axis_size("z")
    other = [(z, (z + 1 if z % 2 else z - 1) % planes) for z in range(planes)]
    done, wave_far, wave_near = call(
        between_kernel,
        (f32(FREQS, 8, LANES), half, half),
        (got, solved, state),
        (pltpu.VMEM(half.shape, jnp.float32), pltpu.VMEM(half.shape, jnp.float32)),
        [VMEM, VMEM, ANY],
        name="between",
    )
    beyond_wave_far = lax.ppermute(wave_far, "z", other)
    beyond_wave_near = swapped(wave_near, "z", 1)
    one, three, two = (swapped(state, "y", bits) for bits in (1, 3, 2))
    state = ((state + one) + three) + two
    states = [state] + [swapped(state, "x", bits) for bits in (1, 3, 2)]
    part = f32(CHUNK // 2, 8, LANES)
    far, near, state_far, state_near = call(
        carry_kernel,
        (half, half, part, part),
        (SLOTS, wave_far, wave_near, *states, beyond_wave_far),
        (),
        [VMEM] * 7 + [ANY],
        name="carry",
    )
    beyond_far = lax.ppermute(state_far, "z", other)
    beyond_near = swapped(state_near, "z", 1)
    edges, core = call(
        inner_kernel,
        (f32(INNER, 2, 4, 8, LANES), f32(2, CHUNK - 2 * INNER, 8, LANES)),
        (ops, lows, scale, inverse, far, near),
        (pltpu.VMEM((2, CHUNK, 8, LANES), jnp.float32), both),
        name="inner",
        cost=pl.CostEstimate(flops=2_000_000_000, bytes_accessed=1_000_000, transcendentals=0),
    )
    done = call(
        outer_kernel,
        f32(FREQS, 16, LANES),
        (SLOTS, ops, lows, scale, inverse, far, near, beyond_wave_far, beyond_far, beyond_wave_near, beyond_near, edges, core, done),
        (pltpu.VMEM((2, 2 * HALO + 2, 8, LANES), jnp.float32), both, both),
        name="outer",
    )
    got = exchange(done, PLANE).reshape(FREQS * 16, LANES)
    slices = call(backward_kernel, f32(STEPS * 8, LANES), (BACKWARD, got), name="backward")
    by_column = exchange(slices.reshape(STEPS, 8, LANES), TIME).reshape(STEPS * 8, LANES)
    result = f32(2, 1, NB, 2, LANES)
    return call(
        unpack_kernel,
        result,
        (by_column,),
        (square, pltpu.VMEM(result.shape, jnp.float32), pltpu.SemaphoreType.DMA((2,))),
        name="unpack",
        out=ANY,
    )


def solution(mesh):
    grid = Mesh(mesh.devices.reshape(8, 4, 2, 4), ("z", "x", "core", "y"))
    return jax.shard_map(
        per_device,
        mesh=grid,
        in_specs=(
            P(None, TIME, None, "y", None),
            P(None, "y", None),
            P("y", None),
            P(),
            P(),
        ),
        out_specs=P(None, TIME, None, "y", None),
        check_vma=False,
    )
```

```python
import math

import jax
import jax.numpy as jnp
import ml_dtypes
import numpy as np
from jax import lax
from jax.experimental import pallas as pl
from jax.experimental.pallas import tpu as pltpu
from jax.sharding import Mesh
from jax.sharding import PartitionSpec as P

NB = 125
SWEEPS = 8
STEPS = 64
LANES = 128
FREQS = STEPS // 2
CHUNK = 16
WINDOW = 32
HALO = 8
INNER = 3
ES_LANE = NB

circ_alpha = 0.01
damping = 0.7

TIME = ("z", "x", "core")
PLANE = ("core", "y", "x")


def tables():
    n = np.arange(STEPS)
    log_alpha = math.log(circ_alpha)
    grow = np.exp(n * (log_alpha / STEPS))
    forward = np.zeros((STEPS, STEPS))
    backward = np.zeros((STEPS, STEPS))
    shifts = np.zeros((FREQS, 4))
    root = math.exp(log_alpha / STEPS)
    forward[0] = 1.0
    forward[1] = (-1.0) ** n
    backward[:, 0] = 1.0
    backward[:, 1] = (-1.0) ** n
    shifts[0] = (1.0 - root, 1.0 + root, 0.0, 0.0)
    for k in range(1, FREQS):
        angle = 2.0 * math.pi * ((k * n) % STEPS) / STEPS
        forward[2 * k] = np.cos(angle)
        forward[2 * k + 1] = -np.sin(angle)
        backward[:, 2 * k] = 2.0 * np.cos(angle)
        backward[:, 2 * k + 1] = -2.0 * np.sin(angle)
        theta = 2.0 * math.pi * k / STEPS
        shifts[k, :3] = (1.0 - root * math.cos(theta), 1.0 - root * math.cos(theta), root * math.sin(theta))
    forward = forward * grow[None, :]
    backward = backward / grow[:, None] / STEPS
    carry = 0.5 * forward.sum(1) + forward[:, 0]
    last = backward[STEPS - 1]
    return tuple(a.astype(np.float32) for a in (forward, backward, shifts, carry, last))


def in_parts(table):
    high = table.astype(ml_dtypes.bfloat16)
    rest = table - high.astype(np.float32)
    middle = rest.astype(ml_dtypes.bfloat16)
    low = (rest - middle.astype(np.float32)).astype(ml_dtypes.bfloat16)
    return np.concatenate((high, high, middle, high, middle, low), axis=1)


FORWARD, BACKWARD, SHIFTS, CARRY, LAST = tables()
BY_PART = np.concatenate((np.arange(0, STEPS, 2), np.arange(1, STEPS, 2)))
FORWARD = in_parts(FORWARD[BY_PART])
BACKWARD = in_parts(BACKWARD[:, BY_PART])
SLOTS = np.concatenate((SHIFTS[:, :3], LAST.reshape(FREQS, 2), CARRY.reshape(FREQS, 2), SHIFTS[:, :1]), axis=1)
SLOTS = np.repeat(SLOTS[:, :, None], LANES, axis=2)

VMEM = pl.BlockSpec(memory_space=pltpu.VMEM)
HBM = pl.BlockSpec(memory_space=pltpu.HBM)
ANY = pl.BlockSpec(memory_space=pl.ANY)
PARAMS = pltpu.CompilerParams(vmem_limit_bytes=32 * 1024 * 1024)


def split(value):
    high = value.astype(jnp.bfloat16)
    return high, (value - high.astype(jnp.float32)).astype(jnp.bfloat16)


def transform(table, parts):
    whole = jnp.concatenate(parts, axis=1)
    high = whole.astype(jnp.bfloat16)
    middle, low = split(whole - high.astype(jnp.float32))
    stack = jnp.concatenate((high, middle, high, low, middle, high), axis=0)
    return jnp.dot(table[...], stack, preferred_element_type=jnp.float32)


def pack_kernel(
    forcing, init, scale, vol, faces, out, ops, lows, diag, value, state, elems, volume, sides, rows, flip, sems
):
    copies = [
        pltpu.make_async_copy(ref, into, sems.at[i])
        for i, (ref, into) in enumerate(
            ((vol, volume), (faces, sides), (forcing, value), (init, state), (scale, elems))
        )
    ]
    for copy in copies:
        copy.start()
    step = lax.axis_index("z") * 8 + lax.axis_index("x") * 2 + lax.axis_index("core")
    weight = jnp.where(step == 0, 1.5, 0.5).astype(jnp.float32)
    flip[...] = jnp.zeros((LANES, LANES), jnp.float32)
    rows[NB:, :] = jnp.zeros((LANES - NB, LANES), jnp.float32)
    for copy in copies[:2]:
        copy.wait()
    row = lax.broadcasted_iota(jnp.int32, (LANES, LANES), 0)
    col = lax.broadcasted_iota(jnp.int32, (LANES, LANES), 1)
    for op in range(5):
        flip[:NB, :NB] = volume[0] if op == 0 else sides[:, op - 1, :]
        square = flip[...]
        if op == 0:
            on = jnp.where(row == col, square, 0.0)
            diag[...] = jnp.broadcast_to(jnp.sum(on, axis=0, keepdims=True), (8, LANES))
            square = square - on
        square = square.T
        high, low = split(square)
        if op == 0:
            here, rest = 4 * LANES, ops.at[:LANES, 5 * LANES :]
        else:
            here = (op - 1) * LANES
            rest = lows.at[:, here : here + LANES]
        ops[:LANES, here : here + LANES] = high
        ops[LANES:, here : here + LANES] = high
        rest[...] = low
    ops[LANES:, 5 * LANES :] = jnp.zeros((LANES, LANES), jnp.bfloat16)
    for copy in copies[2:]:
        copy.wait()
    for s in (1, 0):
        for r in range(2):
            if s == 0:
                rows[:NB, :] = value[s * NB : (s + 1) * NB, r, :] + weight * state[0, :, r, :]
                rows[ES_LANE : ES_LANE + 1, :] = elems[0, r : r + 1, :]
            else:
                rows[:NB, :] = value[s * NB : (s + 1) * NB, r, :]
            flip[...] = rows[...].T
            for c in range(2):
                out[pl.ds(s * 8 + c * 2 + r, STEPS, stride=12), :] = flip[pl.ds(c, STEPS, stride=2), :]
    blank = jnp.zeros((4, LANES), jnp.float32)
    for m in range(STEPS):
        source = m - 4 if m % 8 < 4 else m + 4
        at = m * 12 + 4
        if 0 <= source < STEPS:
            out[at : at + 4, :] = out[source * 12 : source * 12 + 4, :]
        else:
            out[at : at + 4, :] = blank


def forward_kernel(table, got, out):
    lane = lax.broadcasted_iota(jnp.int32, (STEPS, LANES), 1)
    parts = [got[pl.ds(p, STEPS, stride=12), :] for p in range(12)]
    waves = transform(table, parts)
    for p in range(12):
        wave = waves[:, p * LANES : (p + 1) * LANES]
        if p < 8:
            wave = jnp.where(lane == ES_LANE, jnp.broadcast_to(parts[p][:1, :], wave.shape), wave)
        for c in range(2):
            at = c * 8 + p if p < 8 else 16 + c * 4 + p - 8
            out[pl.ds(at, FREQS, stride=24), :] = wave[c * FREQS : (c + 1) * FREQS]


def slot():
    return lax.axis_index("core") * 16 + lax.axis_index("y") * 4 + lax.axis_index("x")


def seat(xc, yd):
    return xc % 2 * 16 + yd * 4 + xc // 2


def invert(slots, diag, scale, inverse):
    mine = slots[slot()]
    shape = (WINDOW, 8, LANES)
    place = lax.axis_index("z") * CHUNK - HALO + lax.broadcasted_iota(jnp.int32, shape, 0)
    inside = jnp.logical_and(place >= 0, place < 8 * CHUNK)
    scaled = scale[...] * diag[...][None]
    im = mine[2:3][None]
    re0 = mine[0:1][None] + scaled
    re1 = mine[1:2][None] + scaled
    mod0 = jnp.where(inside, damping / (re0 * re0 + im * im), 0.0)
    mod1 = jnp.where(inside, damping / (re1 * re1 + im * im), 0.0)
    inverse[0] = re0 * mod0
    inverse[1] = re1 * mod1
    inverse[2] = im * mod0


def start(inverse, field, source, at):
    lane = lax.broadcasted_iota(jnp.int32, field.shape[1:], 2)
    g0 = jnp.where(lane < NB, field[0], 0.0)
    g1 = jnp.where(lane < NB, field[1], 0.0)
    source[0, at] = inverse[0, at] * g0 + inverse[2, at] * g1
    source[1, at] = inverse[1, at] * g1 - inverse[2, at] * g0


def couple(ops, lows, scale, field):
    wide = field.shape[0]
    inner = (wide - 2, 8, LANES)
    high, low = split(field.reshape(wide * 8, LANES))
    both = jnp.concatenate((high, low), axis=1)

    def product(left, right):
        return jnp.dot(left, right, preferred_element_type=jnp.float32)

    def columns(sums, i):
        return sums[:, i * LANES : (i + 1) * LANES].reshape(-1, 8, LANES)

    own = product(both[8:-8], ops[:, 4 * LANES :])
    along = product(both, ops[:, : 2 * LANES]) + product(high, lows[:, : 2 * LANES])
    across = product(both[8:-8], ops[:, 2 * LANES : 4 * LANES]) + product(high[8:-8], lows[:, 2 * LANES :])
    return (
        scale * (columns(own, 0) + columns(own, 1))
        + columns(along, 0)[:-2]
        + columns(along, 1)[2:]
        + pltpu.roll(columns(across, 0), 1, 1)
        + pltpu.roll(columns(across, 1), 7, 1)
    )


def damped(field, source, inverse, coupled):
    keep = 1.0 - damping
    return (
        keep * field[0] + source[0] - inverse[0] * coupled[0] - inverse[2] * coupled[1],
        keep * field[1] + source[1] - inverse[1] * coupled[1] + inverse[2] * coupled[0],
    )


def relax(ops, lows, scale, inverse, iterate, source, done):
    for sweep in range(done, SWEEPS):
        here = slice(sweep + 1, WINDOW - sweep - 1)
        coupled = [couple(ops, lows, scale[here], iterate[c, sweep : WINDOW - sweep]) for c in range(2)]
        fresh = damped(iterate[:, here], source[:, here], inverse[:, here], coupled)
        iterate[0, here] = fresh[0]
        iterate[1, here] = fresh[1]


def first_kernel(slots, ops, lows, diag, got, solved, state, scale, inverse, iterate, source):
    for xc in range(8):
        for yd in range(4):
            for c in range(2):
                for col in range(4):
                    w = HALO + 2 * xc + col
                    if col >= 2:
                        w = (2 * xc if xc < 4 else 16 + 2 * xc) + col - 2
                    at = c * 8 + col * 2
                    iterate[c, w, 2 * yd : 2 * yd + 2, :] = got[seat(xc, yd), at : at + 2, :]
    scale[...] = jnp.broadcast_to(iterate[0, :, :, ES_LANE : ES_LANE + 1], scale.shape)
    invert(slots, diag, scale, inverse)
    start(inverse, iterate[...], source, slice(0, WINDOW))
    iterate[...] = source[...]
    relax(ops, lows, scale, inverse, iterate, source, 1)
    mine = slots[slot()]
    middle = iterate[:, HALO : HALO + CHUNK]
    solved[...] = middle
    state[...] = mine[3:4][None] * middle[0] + mine[4:5][None] * middle[1]


def between_kernel(got, solved, after, done, far, near, left, right):
    del after
    for c in range(2):
        for xc in range(8):
            side = left if xc < 4 else right
            for yd in range(4):
                for col in range(2):
                    rows = slice(2 * yd, 2 * yd + 2)
                    at = c * 4 + col * 2
                    done[seat(xc, yd), at : at + 2, :] = solved[c, 2 * xc + col, rows, :]
                    side[c, 2 * (xc % 4) + col, rows, :] = got[seat(xc, yd), 16 + at : 18 + at, :]
    far[...], near[...] = by_side(right[...], left[...])


def by_side(one, two):
    even = lax.rem(lax.axis_index("z"), 2) == 0
    return jnp.where(even, two, one), jnp.where(even, one, two)


def carry_kernel(
    slots, wave_far, wave_near, state0, state1, state2, state3, early, far, near, state_far, state_near
):
    del early
    state = (state0[...] + state1[...]) + (state2[...] + state3[...])
    mine = slots[slot()]
    state_far[...], state_near[...] = by_side(state[CHUNK // 2 :], state[: CHUNK // 2])
    for c in range(2):
        far[c] = wave_far[c] + mine[5 + c : 6 + c][None] * state_far[...]
        near[c] = wave_near[c] + mine[5 + c : 6 + c][None] * state_near[...]


def inner_kernel(ops, lows, scale, inverse, far, near, edges, core, iterate, source):
    middle = slice(HALO, HALO + CHUNK)
    for i, part in enumerate(by_side(near[...], far[...])):
        start(inverse, part, source, slice((i + 1) * HALO, (i + 2) * HALO))
    iterate[...] = source[:, middle]
    for sweep in range(INNER + 1):
        lo, hi = sweep, CHUNK - sweep
        if sweep:
            here = slice(HALO + lo, HALO + hi)
            coupled = [couple(ops, lows, scale[here], iterate[c, lo - 1 : hi + 1]) for c in range(2)]
            fresh = damped(iterate[:, lo:hi], source[:, here], inverse[:, here], coupled)
            iterate[0, lo:hi] = fresh[0]
            iterate[1, lo:hi] = fresh[1]
        if sweep < INNER:
            edges[sweep, :, :2] = iterate[:, lo : lo + 2]
            edges[sweep, :, 2:] = iterate[:, hi - 2 : hi]
    core[...] = iterate[:, INNER : CHUNK - INNER]


def outer_kernel(
    slots, ops, lows, scale, inverse, far, near, wave_far, state_far, wave_near, state_near, edges, core, before,
    out, sides, iterate, source,
):
    mine = slots[slot()]

    def halo(wave, state):
        return jnp.stack([wave[c] + mine[5 + c : 6 + c][None] * state[...] for c in range(2)])

    left, right = by_side(near[...], far[...])
    west, east = by_side(halo(wave_near, state_near), halo(wave_far, state_far))
    for i, part in enumerate((west, left, right, east)):
        start(inverse, part, source, slice(i * HALO, (i + 1) * HALO))
    out[:, :8, :] = before[...]
    reach = HALO - 1
    sides[:, :reach] = source[:, 1:HALO]
    sides[:, reach + 4 :] = source[:, HALO + CHUNK : WINDOW - 1]
    for sweep in range(1, INNER + 1):
        sides[:, reach : reach + 4] = edges[sweep - 1]
        one = slice(sweep + 1, HALO + sweep)
        two = slice(WINDOW - HALO - sweep, WINDOW - 1 - sweep)
        given = [
            jnp.concatenate((ref[one], ref[HALO : HALO + 2], ref[two]), axis=0)
            for ref in [scale] + [inverse.at[i] for i in range(3)] + [source.at[i] for i in range(2)]
        ]
        coupled = [couple(ops, lows, given[0], sides[c]) for c in range(2)]
        fresh = damped(sides[:, 1:-1], given[4:], given[1:4], coupled)
        for c in range(2):
            sides[c, :reach] = fresh[c][:reach]
            sides[c, reach + 4 :] = fresh[c][reach + 2 :]
    iterate[:, INNER + 1 : HALO + INNER] = sides[:, :reach]
    iterate[:, HALO + INNER : WINDOW - HALO - INNER] = core[...]
    iterate[:, WINDOW - HALO - INNER : WINDOW - 1 - INNER] = sides[:, reach + 4 :]
    relax(ops, lows, scale, inverse, iterate, source, INNER + 1)
    for xc in range(8):
        for yd in range(4):
            for c in range(2):
                for col in range(2):
                    at = 8 + c * 4 + col * 2
                    out[seat(xc, yd), at : at + 2, :] = iterate[c, HALO + 2 * xc + col, 2 * yd : 2 * yd + 2, :]


def backward_kernel(table, got, out):
    parts = []
    for p in range(8):
        at = (p // 4) * 8 + p % 4
        halves = [got[pl.ds(at + 4 * c, FREQS, stride=16), :] for c in range(2)]
        parts.append(jnp.concatenate(halves, axis=0))
    slices = transform(table, parts)
    for p in range(8):
        out[pl.ds(p, STEPS, stride=8), :] = slices[:, p * LANES : (p + 1) * LANES]


def unpack_kernel(got, out, flip, held, sems):
    copies = []
    for s in range(2):
        for r in range(2):
            for c in range(2):
                flip[pl.ds(c, STEPS, stride=2), :] = got[pl.ds(s * 4 + c * 2 + r, STEPS, stride=8), :]
            held[s, 0, :, r, :] = flip[...].T[:NB, :]
        copies.append(pltpu.make_async_copy(held.at[s], out.at[s], sems.at[s]))
        copies[s].start()
    for copy in copies:
        copy.wait()


def call(kernel, outs, ins, scratch=(), specs=None, name=None, params=PARAMS, out=VMEM, cost=None):
    return pl.pallas_call(
        kernel,
        out_shape=outs,
        in_specs=specs or [VMEM] * len(ins),
        out_specs=jax.tree.map(lambda _: out, outs),
        scratch_shapes=scratch,
        compiler_params=params,
        cost_estimate=cost,
        name=name,
    )(*ins)


def f32(*shape):
    return jax.ShapeDtypeStruct(shape, jnp.float32)


def exchange(blocks, axes):
    return lax.all_to_all(blocks, axes, 0, 0, tiled=True)


def swapped(block, axis, bits):
    return lax.ppermute(block, axis, [(i, i ^ bits) for i in range(lax.axis_size(axis))])


def per_device(forcing, init_state, elem_scale, vol_op, face_ops):
    square = pltpu.VMEM((LANES, LANES), jnp.float32)
    window = (WINDOW, 8, LANES)
    inputs = (
        forcing.reshape(2 * NB, 2, LANES),
        init_state.reshape(1, NB, 2, LANES),
        elem_scale.reshape(1, 2, LANES),
        vol_op.reshape(1, NB, NB),
        jnp.transpose(face_ops, (1, 0, 2)),
    )
    packed, ops, lows, diag = call(
        pack_kernel,
        (
            pltpu.VMEM((STEPS * 12, LANES), jnp.float32),
            pltpu.VMEM((2 * LANES, 6 * LANES), jnp.bfloat16),
            pltpu.VMEM((LANES, 4 * LANES), jnp.bfloat16),
            pltpu.VMEM((8, LANES), jnp.float32),
        ),
        inputs,
        [pltpu.VMEM(value.shape, jnp.float32) for value in inputs]
        + [square, square, pltpu.SemaphoreType.DMA((len(inputs),))],
        [HBM] * len(inputs),
        name="pack",
        params=pltpu.CompilerParams(vmem_limit_bytes=60 * 1024 * 1024),
    )
    by_point = exchange(packed.reshape(STEPS, 3, 4, LANES), TIME).reshape(STEPS * 12, LANES)
    waves = call(forward_kernel, f32(FREQS * 24, LANES), (FORWARD, by_point), name="forward")
    got = exchange(waves.reshape(FREQS, 24, LANES), PLANE)
    both = pltpu.VMEM((2,) + window, jnp.float32)
    solved, state, scale, inverse = call(
        first_kernel,
        (f32(2, CHUNK, 8, LANES), f32(CHUNK, 8, LANES), f32(*window), f32(3, *window)),
        (SLOTS, ops, lows, diag, got),
        (both, both),
        name="first",
    )
    half = f32(2, CHUNK // 2, 8, LANES)
    state = state + swapped(state, "core", 1)
    planes = lax.axis_size("z")
    other = [(z, (z + 1 if z % 2 else z - 1) % planes) for z in range(planes)]
    done, wave_far, wave_near = call(
        between_kernel,
        (f32(FREQS, 8, LANES), half, half),
        (got, solved, state),
        (pltpu.VMEM(half.shape, jnp.float32), pltpu.VMEM(half.shape, jnp.float32)),
        [VMEM, VMEM, ANY],
        name="between",
    )
    beyond_wave_far = lax.ppermute(wave_far, "z", other)
    beyond_wave_near = swapped(wave_near, "z", 1)
    one, three, two = (swapped(state, "y", bits) for bits in (1, 3, 2))
    state = ((state + one) + three) + two
    states = [state] + [swapped(state, "x", bits) for bits in (1, 3, 2)]
    part = f32(CHUNK // 2, 8, LANES)
    far, near, state_far, state_near = call(
        carry_kernel,
        (half, half, part, part),
        (SLOTS, wave_far, wave_near, *states, beyond_wave_far),
        (),
        [VMEM] * 7 + [ANY],
        name="carry",
    )
    beyond_far = lax.ppermute(state_far, "z", other)
    beyond_near = swapped(state_near, "z", 1)
    edges, core = call(
        inner_kernel,
        (f32(INNER, 2, 4, 8, LANES), f32(2, CHUNK - 2 * INNER, 8, LANES)),
        (ops, lows, scale, inverse, far, near),
        (pltpu.VMEM((2, CHUNK, 8, LANES), jnp.float32), both),
        name="inner",
        cost=pl.CostEstimate(flops=2_000_000_000, bytes_accessed=1_000_000, transcendentals=0),
    )
    done = call(
        outer_kernel,
        f32(FREQS, 16, LANES),
        (SLOTS, ops, lows, scale, inverse, far, near, beyond_wave_far, beyond_far, beyond_wave_near, beyond_near, edges, core, done),
        (pltpu.VMEM((2, 2 * HALO + 2, 8, LANES), jnp.float32), both, both),
        name="outer",
    )
    got = exchange(done, PLANE).reshape(FREQS * 16, LANES)
    slices = call(backward_kernel, f32(STEPS * 8, LANES), (BACKWARD, got), name="backward")
    by_column = exchange(slices.reshape(STEPS, 8, LANES), TIME).reshape(STEPS * 8, LANES)
    result = f32(2, 1, NB, 2, LANES)
    return call(
        unpack_kernel,
        result,
        (by_column,),
        (square, pltpu.VMEM(result.shape, jnp.float32), pltpu.SemaphoreType.DMA((2,))),
        name="unpack",
        out=ANY,
    )


def solution(mesh):
    grid = Mesh(mesh.devices.reshape(8, 4, 2, 4), ("z", "x", "core", "y"))
    return jax.shard_map(
        per_device,
        mesh=grid,
        in_specs=(
            P(None, TIME, None, "y", None),
            P(None, "y", None),
            P("y", None),
            P(),
            P(),
        ),
        out_specs=P(None, TIME, None, "y", None),
        check_vma=False,
    )
```

```python
import math

import jax
import jax.numpy as jnp
import ml_dtypes
import numpy as np
from jax import lax
from jax.experimental import pallas as pl
from jax.experimental.pallas import tpu as pltpu
from jax.sharding import Mesh
from jax.sharding import PartitionSpec as P

NB = 125
SWEEPS = 8
STEPS = 64
LANES = 128
FREQS = STEPS // 2
CHUNK = 16
WINDOW = 32
HALO = 8
INNER = 4
ES_LANE = NB

circ_alpha = 0.01
damping = 0.7

TIME = ("z", "x", "core")
PLANE = ("core", "y", "x")


def tables():
    n = np.arange(STEPS)
    log_alpha = math.log(circ_alpha)
    grow = np.exp(n * (log_alpha / STEPS))
    forward = np.zeros((STEPS, STEPS))
    backward = np.zeros((STEPS, STEPS))
    shifts = np.zeros((FREQS, 4))
    root = math.exp(log_alpha / STEPS)
    forward[0] = 1.0
    forward[1] = (-1.0) ** n
    backward[:, 0] = 1.0
    backward[:, 1] = (-1.0) ** n
    shifts[0] = (1.0 - root, 1.0 + root, 0.0, 0.0)
    for k in range(1, FREQS):
        angle = 2.0 * math.pi * ((k * n) % STEPS) / STEPS
        forward[2 * k] = np.cos(angle)
        forward[2 * k + 1] = -np.sin(angle)
        backward[:, 2 * k] = 2.0 * np.cos(angle)
        backward[:, 2 * k + 1] = -2.0 * np.sin(angle)
        theta = 2.0 * math.pi * k / STEPS
        shifts[k, :3] = (1.0 - root * math.cos(theta), 1.0 - root * math.cos(theta), root * math.sin(theta))
    forward = forward * grow[None, :]
    backward = backward / grow[:, None] / STEPS
    carry = 0.5 * forward.sum(1) + forward[:, 0]
    last = backward[STEPS - 1]
    return tuple(a.astype(np.float32) for a in (forward, backward, shifts, carry, last))


def in_parts(table):
    high = table.astype(ml_dtypes.bfloat16)
    rest = table - high.astype(np.float32)
    middle = rest.astype(ml_dtypes.bfloat16)
    low = (rest - middle.astype(np.float32)).astype(ml_dtypes.bfloat16)
    return np.concatenate((high, high, middle, high, middle, low), axis=1)


FORWARD, BACKWARD, SHIFTS, CARRY, LAST = tables()
BY_PART = np.concatenate((np.arange(0, STEPS, 2), np.arange(1, STEPS, 2)))
FORWARD = in_parts(FORWARD[BY_PART])
BACKWARD = in_parts(BACKWARD[:, BY_PART])
SLOTS = np.concatenate((SHIFTS[:, :3], LAST.reshape(FREQS, 2), CARRY.reshape(FREQS, 2), SHIFTS[:, :1]), axis=1)
SLOTS = np.repeat(SLOTS[:, :, None], LANES, axis=2)

VMEM = pl.BlockSpec(memory_space=pltpu.VMEM)
HBM = pl.BlockSpec(memory_space=pltpu.HBM)
ANY = pl.BlockSpec(memory_space=pl.ANY)
PARAMS = pltpu.CompilerParams(vmem_limit_bytes=32 * 1024 * 1024)


def split(value):
    high = value.astype(jnp.bfloat16)
    return high, (value - high.astype(jnp.float32)).astype(jnp.bfloat16)


def transform(table, parts):
    whole = jnp.concatenate(parts, axis=1)
    high = whole.astype(jnp.bfloat16)
    middle, low = split(whole - high.astype(jnp.float32))
    stack = jnp.concatenate((high, middle, high, low, middle, high), axis=0)
    return jnp.dot(table[...], stack, preferred_element_type=jnp.float32)


def pack_kernel(
    forcing, init, scale, vol, faces, out, ops, lows, diag, value, state, elems, volume, sides, rows, flip, sems
):
    copies = [
        pltpu.make_async_copy(ref, into, sems.at[i])
        for i, (ref, into) in enumerate(
            ((vol, volume), (faces, sides), (forcing, value), (init, state), (scale, elems))
        )
    ]
    for copy in copies:
        copy.start()
    step = lax.axis_index("z") * 8 + lax.axis_index("x") * 2 + lax.axis_index("core")
    weight = jnp.where(step == 0, 1.5, 0.5).astype(jnp.float32)
    flip[...] = jnp.zeros((LANES, LANES), jnp.float32)
    rows[NB:, :] = jnp.zeros((LANES - NB, LANES), jnp.float32)
    for copy in copies[:2]:
        copy.wait()
    row = lax.broadcasted_iota(jnp.int32, (LANES, LANES), 0)
    col = lax.broadcasted_iota(jnp.int32, (LANES, LANES), 1)
    for op in range(5):
        flip[:NB, :NB] = volume[0] if op == 0 else sides[:, op - 1, :]
        square = flip[...]
        if op == 0:
            on = jnp.where(row == col, square, 0.0)
            diag[...] = jnp.broadcast_to(jnp.sum(on, axis=0, keepdims=True), (8, LANES))
            square = square - on
        square = square.T
        high, low = split(square)
        if op == 0:
            here, rest = 4 * LANES, ops.at[:LANES, 5 * LANES :]
        else:
            here = (op - 1) * LANES
            rest = lows.at[:, here : here + LANES]
        ops[:LANES, here : here + LANES] = high
        ops[LANES:, here : here + LANES] = high
        rest[...] = low
    ops[LANES:, 5 * LANES :] = jnp.zeros((LANES, LANES), jnp.bfloat16)
    for copy in copies[2:]:
        copy.wait()
    for s in (1, 0):
        for r in range(2):
            if s == 0:
                rows[:NB, :] = value[s * NB : (s + 1) * NB, r, :] + weight * state[0, :, r, :]
                rows[ES_LANE : ES_LANE + 1, :] = elems[0, r : r + 1, :]
            else:
                rows[:NB, :] = value[s * NB : (s + 1) * NB, r, :]
            flip[...] = rows[...].T
            for c in range(2):
                out[pl.ds(s * 8 + c * 2 + r, STEPS, stride=12), :] = flip[pl.ds(c, STEPS, stride=2), :]
    blank = jnp.zeros((4, LANES), jnp.float32)
    for m in range(STEPS):
        source = m - 4 if m % 8 < 4 else m + 4
        at = m * 12 + 4
        if 0 <= source < STEPS:
            out[at : at + 4, :] = out[source * 12 : source * 12 + 4, :]
        else:
            out[at : at + 4, :] = blank


def forward_kernel(table, got, out):
    lane = lax.broadcasted_iota(jnp.int32, (STEPS, LANES), 1)
    parts = [got[pl.ds(p, STEPS, stride=12), :] for p in range(12)]
    waves = transform(table, parts)
    for p in range(12):
        wave = waves[:, p * LANES : (p + 1) * LANES]
        if p < 8:
            wave = jnp.where(lane == ES_LANE, jnp.broadcast_to(parts[p][:1, :], wave.shape), wave)
        for c in range(2):
            at = c * 8 + p if p < 8 else 16 + c * 4 + p - 8
            out[pl.ds(at, FREQS, stride=24), :] = wave[c * FREQS : (c + 1) * FREQS]


def slot():
    return lax.axis_index("core") * 16 + lax.axis_index("y") * 4 + lax.axis_index("x")


def seat(xc, yd):
    return xc % 2 * 16 + yd * 4 + xc // 2


def invert(slots, diag, scale, inverse):
    mine = slots[slot()]
    shape = (WINDOW, 8, LANES)
    place = lax.axis_index("z") * CHUNK - HALO + lax.broadcasted_iota(jnp.int32, shape, 0)
    inside = jnp.logical_and(place >= 0, place < 8 * CHUNK)
    scaled = scale[...] * diag[...][None]
    im = mine[2:3][None]
    re0 = mine[0:1][None] + scaled
    re1 = mine[1:2][None] + scaled
    mod0 = jnp.where(inside, damping / (re0 * re0 + im * im), 0.0)
    mod1 = jnp.where(inside, damping / (re1 * re1 + im * im), 0.0)
    inverse[0] = re0 * mod0
    inverse[1] = re1 * mod1
    inverse[2] = im * mod0


def start(inverse, field, source, at):
    lane = lax.broadcasted_iota(jnp.int32, field.shape[1:], 2)
    g0 = jnp.where(lane < NB, field[0], 0.0)
    g1 = jnp.where(lane < NB, field[1], 0.0)
    source[0, at] = inverse[0, at] * g0 + inverse[2, at] * g1
    source[1, at] = inverse[1, at] * g1 - inverse[2, at] * g0


def couple(ops, lows, scale, field):
    wide = field.shape[0]
    inner = (wide - 2, 8, LANES)
    high, low = split(field.reshape(wide * 8, LANES))
    both = jnp.concatenate((high, low), axis=1)

    def product(left, right):
        return jnp.dot(left, right, preferred_element_type=jnp.float32)

    def columns(sums, i):
        return sums[:, i * LANES : (i + 1) * LANES].reshape(-1, 8, LANES)

    own = product(both[8:-8], ops[:, 4 * LANES :])
    along = product(both, ops[:, : 2 * LANES]) + product(high, lows[:, : 2 * LANES])
    across = product(both[8:-8], ops[:, 2 * LANES : 4 * LANES]) + product(high[8:-8], lows[:, 2 * LANES :])
    return (
        scale * (columns(own, 0) + columns(own, 1))
        + columns(along, 0)[:-2]
        + columns(along, 1)[2:]
        + pltpu.roll(columns(across, 0), 1, 1)
        + pltpu.roll(columns(across, 1), 7, 1)
    )


def damped(field, source, inverse, coupled):
    keep = 1.0 - damping
    return (
        keep * field[0] + source[0] - inverse[0] * coupled[0] - inverse[2] * coupled[1],
        keep * field[1] + source[1] - inverse[1] * coupled[1] + inverse[2] * coupled[0],
    )


def relax(ops, lows, scale, inverse, iterate, source, done):
    for sweep in range(done, SWEEPS):
        here = slice(sweep + 1, WINDOW - sweep - 1)
        coupled = [couple(ops, lows, scale[here], iterate[c, sweep : WINDOW - sweep]) for c in range(2)]
        fresh = damped(iterate[:, here], source[:, here], inverse[:, here], coupled)
        iterate[0, here] = fresh[0]
        iterate[1, here] = fresh[1]


def first_kernel(slots, ops, lows, diag, got, solved, state, scale, inverse, iterate, source):
    for xc in range(8):
        for yd in range(4):
            for c in range(2):
                for col in range(4):
                    w = HALO + 2 * xc + col
                    if col >= 2:
                        w = (2 * xc if xc < 4 else 16 + 2 * xc) + col - 2
                    at = c * 8 + col * 2
                    iterate[c, w, 2 * yd : 2 * yd + 2, :] = got[seat(xc, yd), at : at + 2, :]
    scale[...] = jnp.broadcast_to(iterate[0, :, :, ES_LANE : ES_LANE + 1], scale.shape)
    invert(slots, diag, scale, inverse)
    start(inverse, iterate[...], source, slice(0, WINDOW))
    iterate[...] = source[...]
    relax(ops, lows, scale, inverse, iterate, source, 1)
    mine = slots[slot()]
    middle = iterate[:, HALO : HALO + CHUNK]
    solved[...] = middle
    state[...] = mine[3:4][None] * middle[0] + mine[4:5][None] * middle[1]


def between_kernel(got, solved, after, done, far, near, left, right):
    del after
    for c in range(2):
        for xc in range(8):
            side = left if xc < 4 else right
            for yd in range(4):
                for col in range(2):
                    rows = slice(2 * yd, 2 * yd + 2)
                    at = c * 4 + col * 2
                    done[seat(xc, yd), at : at + 2, :] = solved[c, 2 * xc + col, rows, :]
                    side[c, 2 * (xc % 4) + col, rows, :] = got[seat(xc, yd), 16 + at : 18 + at, :]
    far[...], near[...] = by_side(right[...], left[...])


def by_side(one, two):
    even = lax.rem(lax.axis_index("z"), 2) == 0
    return jnp.where(even, two, one), jnp.where(even, one, two)


def carry_kernel(
    slots, wave_far, wave_near, state0, state1, state2, state3, early, far, near, state_far, state_near
):
    del early
    state = (state0[...] + state1[...]) + (state2[...] + state3[...])
    mine = slots[slot()]
    state_far[...], state_near[...] = by_side(state[CHUNK // 2 :], state[: CHUNK // 2])
    for c in range(2):
        far[c] = wave_far[c] + mine[5 + c : 6 + c][None] * state_far[...]
        near[c] = wave_near[c] + mine[5 + c : 6 + c][None] * state_near[...]


def inner_kernel(ops, lows, scale, inverse, far, near, edges, core, iterate, source):
    middle = slice(HALO, HALO + CHUNK)
    for i, part in enumerate(by_side(near[...], far[...])):
        start(inverse, part, source, slice((i + 1) * HALO, (i + 2) * HALO))
    iterate[...] = source[:, middle]
    for sweep in range(INNER + 1):
        lo, hi = sweep, CHUNK - sweep
        if sweep:
            here = slice(HALO + lo, HALO + hi)
            coupled = [couple(ops, lows, scale[here], iterate[c, lo - 1 : hi + 1]) for c in range(2)]
            fresh = damped(iterate[:, lo:hi], source[:, here], inverse[:, here], coupled)
            iterate[0, lo:hi] = fresh[0]
            iterate[1, lo:hi] = fresh[1]
        if sweep < INNER:
            edges[sweep, :, :2] = iterate[:, lo : lo + 2]
            edges[sweep, :, 2:] = iterate[:, hi - 2 : hi]
    core[...] = iterate[:, INNER : CHUNK - INNER]


def outer_kernel(
    slots, ops, lows, scale, inverse, far, near, wave_far, state_far, wave_near, state_near, edges, core, before,
    out, sides, iterate, source,
):
    mine = slots[slot()]

    def halo(wave, state):
        return jnp.stack([wave[c] + mine[5 + c : 6 + c][None] * state[...] for c in range(2)])

    left, right = by_side(near[...], far[...])
    west, east = by_side(halo(wave_near, state_near), halo(wave_far, state_far))
    for i, part in enumerate((west, left, right, east)):
        start(inverse, part, source, slice(i * HALO, (i + 1) * HALO))
    out[:, :8, :] = before[...]
    reach = HALO - 1
    sides[:, :reach] = source[:, 1:HALO]
    sides[:, reach + 4 :] = source[:, HALO + CHUNK : WINDOW - 1]
    for sweep in range(1, INNER + 1):
        sides[:, reach : reach + 4] = edges[sweep - 1]
        one = slice(sweep + 1, HALO + sweep)
        two = slice(WINDOW - HALO - sweep, WINDOW - 1 - sweep)
        given = [
            jnp.concatenate((ref[one], ref[HALO : HALO + 2], ref[two]), axis=0)
            for ref in [scale] + [inverse.at[i] for i in range(3)] + [source.at[i] for i in range(2)]
        ]
        coupled = [couple(ops, lows, given[0], sides[c]) for c in range(2)]
        fresh = damped(sides[:, 1:-1], given[4:], given[1:4], coupled)
        for c in range(2):
            sides[c, :reach] = fresh[c][:reach]
            sides[c, reach + 4 :] = fresh[c][reach + 2 :]
    iterate[:, INNER + 1 : HALO + INNER] = sides[:, :reach]
    iterate[:, HALO + INNER : WINDOW - HALO - INNER] = core[...]
    iterate[:, WINDOW - HALO - INNER : WINDOW - 1 - INNER] = sides[:, reach + 4 :]
    relax(ops, lows, scale, inverse, iterate, source, INNER + 1)
    for xc in range(8):
        for yd in range(4):
            for c in range(2):
                for col in range(2):
                    at = 8 + c * 4 + col * 2
                    out[seat(xc, yd), at : at + 2, :] = iterate[c, HALO + 2 * xc + col, 2 * yd : 2 * yd + 2, :]


def backward_kernel(table, got, out):
    parts = []
    for p in range(8):
        at = (p // 4) * 8 + p % 4
        halves = [got[pl.ds(at + 4 * c, FREQS, stride=16), :] for c in range(2)]
        parts.append(jnp.concatenate(halves, axis=0))
    slices = transform(table, parts)
    for p in range(8):
        out[pl.ds(p, STEPS, stride=8), :] = slices[:, p * LANES : (p + 1) * LANES]


def unpack_kernel(got, out, flip, held, sems):
    copies = []
    for s in range(2):
        for r in range(2):
            for c in range(2):
                flip[pl.ds(c, STEPS, stride=2), :] = got[pl.ds(s * 4 + c * 2 + r, STEPS, stride=8), :]
            held[s, 0, :, r, :] = flip[...].T[:NB, :]
        copies.append(pltpu.make_async_copy(held.at[s], out.at[s], sems.at[s]))
        copies[s].start()
    for copy in copies:
        copy.wait()


def call(kernel, outs, ins, scratch=(), specs=None, name=None, params=PARAMS, out=VMEM, cost=None):
    return pl.pallas_call(
        kernel,
        out_shape=outs,
        in_specs=specs or [VMEM] * len(ins),
        out_specs=jax.tree.map(lambda _: out, outs),
        scratch_shapes=scratch,
        compiler_params=params,
        cost_estimate=cost,
        name=name,
    )(*ins)


def f32(*shape):
    return jax.ShapeDtypeStruct(shape, jnp.float32)


def exchange(blocks, axes):
    return lax.all_to_all(blocks, axes, 0, 0, tiled=True)


def swapped(block, axis, bits):
    return lax.ppermute(block, axis, [(i, i ^ bits) for i in range(lax.axis_size(axis))])


def per_device(forcing, init_state, elem_scale, vol_op, face_ops):
    square = pltpu.VMEM((LANES, LANES), jnp.float32)
    window = (WINDOW, 8, LANES)
    inputs = (
        forcing.reshape(2 * NB, 2, LANES),
        init_state.reshape(1, NB, 2, LANES),
        elem_scale.reshape(1, 2, LANES),
        vol_op.reshape(1, NB, NB),
        jnp.transpose(face_ops, (1, 0, 2)),
    )
    packed, ops, lows, diag = call(
        pack_kernel,
        (
            pltpu.VMEM((STEPS * 12, LANES), jnp.float32),
            pltpu.VMEM((2 * LANES, 6 * LANES), jnp.bfloat16),
            pltpu.VMEM((LANES, 4 * LANES), jnp.bfloat16),
            pltpu.VMEM((8, LANES), jnp.float32),
        ),
        inputs,
        [pltpu.VMEM(value.shape, jnp.float32) for value in inputs]
        + [square, square, pltpu.SemaphoreType.DMA((len(inputs),))],
        [HBM] * len(inputs),
        name="pack",
        params=pltpu.CompilerParams(vmem_limit_bytes=60 * 1024 * 1024),
    )
    by_point = exchange(packed.reshape(STEPS, 3, 4, LANES), TIME).reshape(STEPS * 12, LANES)
    waves = call(forward_kernel, f32(FREQS * 24, LANES), (FORWARD, by_point), name="forward")
    got = exchange(waves.reshape(FREQS, 24, LANES), PLANE)
    both = pltpu.VMEM((2,) + window, jnp.float32)
    solved, state, scale, inverse = call(
        first_kernel,
        (f32(2, CHUNK, 8, LANES), f32(CHUNK, 8, LANES), f32(*window), f32(3, *window)),
        (SLOTS, ops, lows, diag, got),
        (both, both),
        name="first",
    )
    half = f32(2, CHUNK // 2, 8, LANES)
    state = state + swapped(state, "core", 1)
    planes = lax.axis_size("z")
    other = [(z, (z + 1 if z % 2 else z - 1) % planes) for z in range(planes)]
    done, wave_far, wave_near = call(
        between_kernel,
        (f32(FREQS, 8, LANES), half, half),
        (got, solved, state),
        (pltpu.VMEM(half.shape, jnp.float32), pltpu.VMEM(half.shape, jnp.float32)),
        [VMEM, VMEM, ANY],
        name="between",
    )
    beyond_wave_far = lax.ppermute(wave_far, "z", other)
    beyond_wave_near = swapped(wave_near, "z", 1)
    one, three, two = (swapped(state, "x", bits) for bits in (1, 3, 2))
    state = ((state + one) + three) + two
    states = [state] + [swapped(state, "y", bits) for bits in (1, 3, 2)]
    part = f32(CHUNK // 2, 8, LANES)
    far, near, state_far, state_near = call(
        carry_kernel,
        (half, half, part, part),
        (SLOTS, wave_far, wave_near, *states, beyond_wave_far),
        (),
        [VMEM] * 7 + [ANY],
        name="carry",
    )
    beyond_far = lax.ppermute(state_far, "z", other)
    beyond_near = swapped(state_near, "z", 1)
    edges, core = call(
        inner_kernel,
        (f32(INNER, 2, 4, 8, LANES), f32(2, CHUNK - 2 * INNER, 8, LANES)),
        (ops, lows, scale, inverse, far, near),
        (pltpu.VMEM((2, CHUNK, 8, LANES), jnp.float32), both),
        name="inner",
        cost=pl.CostEstimate(flops=2_000_000_000, bytes_accessed=1_000_000, transcendentals=0),
    )
    done = call(
        outer_kernel,
        f32(FREQS, 16, LANES),
        (SLOTS, ops, lows, scale, inverse, far, near, beyond_wave_far, beyond_far, beyond_wave_near, beyond_near, edges, core, done),
        (pltpu.VMEM((2, 2 * HALO + 2, 8, LANES), jnp.float32), both, both),
        name="outer",
    )
    got = exchange(done, PLANE).reshape(FREQS * 16, LANES)
    slices = call(backward_kernel, f32(STEPS * 8, LANES), (BACKWARD, got), name="backward")
    by_column = exchange(slices.reshape(STEPS, 8, LANES), TIME).reshape(STEPS * 8, LANES)
    result = f32(2, 1, NB, 2, LANES)
    return call(
        unpack_kernel,
        result,
        (by_column,),
        (square, pltpu.VMEM(result.shape, jnp.float32), pltpu.SemaphoreType.DMA((2,))),
        name="unpack",
        out=ANY,
    )


def solution(mesh):
    grid = Mesh(mesh.devices.reshape(8, 4, 2, 4), ("z", "x", "core", "y"))
    return jax.shard_map(
        per_device,
        mesh=grid,
        in_specs=(
            P(None, TIME, None, "y", None),
            P(None, "y", None),
            P("y", None),
            P(),
            P(),
        ),
        out_specs=P(None, TIME, None, "y", None),
        check_vma=False,
    )
```
